32 devices in a mesh: leaf: 8 (over z, y), rhs: 4 (over x, core).
Axes of the slice: x: 2, y: 2, z: 4, core: 2. Of those that a mesh axis runs over, the one named last changes fastest.
Arguments:
- leaf_rhs: float32 [2, 64, 4096], P(None, 'rhs', 'leaf'), may hold values from -6 to 6
- sep_rhs: float32 [2, 64, 3, 64], P(None, 'rhs', None, 'leaf'), may hold values from -6 to 6
- leaf_inv: bfloat16 [2, 512, 4096], P(None, 'rhs', 'leaf'), may hold values from -0.1875 to 0.1875
- leaf_low: bfloat16 [2, 512, 64], P(None, None, 'leaf'), may hold values from -0.1875 to 0.1875
- sep_inv: bfloat16 [2, 8, 896], P(None, None, 'leaf'), as said below
- sep_low: bfloat16 [2, 8, 384], P(None, None, 'leaf'), as said below
- leaf_live: int32 [8], P('leaf'), may hold values from 1 to 4
- targets: int32 [3, 8], replicated, may hold values from 0 to 7, as said below
Outputs:
- leaf_solution: float32 [2, 64, 4096], P(None, 'rhs', 'leaf')
- sep_solution: float32 [2, 64, 3, 64], P(None, 'rhs', None, 'leaf')
The draws below stay inside these ranges and needn't reach their ends.
Inputs may be any that keep to these rules, and one draw needn't show every extreme that they name: `targets`: in row l, the entries of each aligned group of 2 ** (l + 1) devices are a permutation of 0 to 2 ** (l + 1) - 1. Rows of a leaf front beyond 128 * leaf_live are padding and are ignored. `sep_inv`: entries are independent, of mean zero, with spread inversely proportional to the square root of the front's order. `sep_low`: entries are independent, of mean zero, with spread inversely proportional to the square root of the front's order.
All inputs are finite; a program needn't handle non-finite values.
Results may differ from the reference program's by a relative error of at most 0.025.
Values may be sent and summed in bfloat16 or wider, within the bound.
No kernel may reach another device: no remote copies, remote signals or barrier semaphores. Data moves between devices by JAX's collectives and lax.ppermute only.
A program may use at most 64 MiB of HBM per device.

```python
import jax
import jax.numpy as jnp
from jax import lax

PR = 8
LEAF = 512
NRHS = 64
LEVELS = 3
N_LEAF = 8


def front_order(column, depth):
    block_step = column // PR + 2
    front_size = jnp.ones_like(block_step)
    for exponent in range(1, depth + 1):
        front_size = jnp.where(block_step >= 2 ** exponent, 2 ** exponent, front_size)
    return front_size


def scaled_factor(key, slab):
    column = jnp.arange(N_LEAF * slab, dtype=jnp.int32) % slab
    front_size = front_order(column, LEVELS).astype(jnp.float32)
    spread_scale = 1.0 / jnp.sqrt(2.0 * PR * front_size)
    values = jax.random.normal(key, (2, PR, N_LEAF * slab), jnp.float32)
    return (values * spread_scale[None, None, :]).astype(jnp.bfloat16)


def draw_sep_inv(key, part):
    return scaled_factor(jax.random.fold_in(key, 11), PR * (2 * N_LEAF - 2))


def draw_sep_low(key, part):
    return scaled_factor(jax.random.fold_in(key, 23), PR * (N_LEAF - 2))


def draw_targets(key, part):
    rows_list = []
    for level_now in range(LEVELS):
        group_size = 2 ** (level_now + 1)
        keys_list = jax.random.split(jax.random.fold_in(key, level_now + 37), N_LEAF // group_size)
        shuffled = jax.vmap(lambda one_key: jax.random.permutation(one_key, group_size))(keys_list)
        rows_list.append(shuffled.reshape(N_LEAF).astype(jnp.int32))
    return jnp.stack(rows_list)


def with_ends(values, own_key, low, high):
    spot = [jax.random.randint(jax.random.fold_in(own_key, axis), (), 0, length) for axis, length in enumerate(values.shape)]
    longest = values.shape.index(max(values.shape))
    neighbour = spot[:longest] + [(spot[longest] + 1) % values.shape[longest]] + spot[longest + 1:]
    return values.at[tuple(spot)].set(low).at[tuple(neighbour)].set(high)


def levels(own_key, dims, cuts, least, largest):
    def one(position, shards_of):
        heights = jax.random.uniform(jax.random.fold_in(jax.random.fold_in(own_key, 6), position), (shards_of,), jnp.float32, least / len(cuts), largest / len(cuts))
        return jnp.repeat(jnp.exp(heights), dims[position] // shards_of).reshape((-1,) + (1,) * (len(dims) - position - 1))

    level = one(*cuts[0])
    for cut in cuts[1:]:
        level = level * one(*cut)
    return level


def centred(own_key, shape, spread, most, cuts=(), kind=jnp.bfloat16):
    values = jax.random.normal(own_key, shape, jnp.float32) * spread
    if len(cuts) > 0:
        values = levels(own_key, shape, cuts, -0.22, 0.18) * values
    return jnp.clip(values, min=-most, max=most).astype(kind)


def setup_inputs(seed: int = 0) -> dict:
    key_of = jax.random.split(jax.random.key(seed), 9)
    leaf_rhs = centred(key_of[0], (2, NRHS, N_LEAF * LEAF), 1.0, 6.0, ((1, 4), (2, 8)), jnp.float32)
    sep_rhs = centred(key_of[1], (2, NRHS, LEVELS, N_LEAF * PR), 1.0, 6.0, ((1, 4), (3, 8)), jnp.float32)
    leaf_inv = centred(key_of[2], (2, LEAF, N_LEAF * LEAF), (2 * LEAF) ** -0.5, 0.1875, ((1, 4), (2, 8)))
    leaf_low = centred(key_of[3], (2, LEAF, N_LEAF * PR), (2 * LEAF) ** -0.5, 0.1875, ((2, 8),))
    sep_inv = draw_sep_inv(jax.random.fold_in(key_of[8], 71), 0)
    sep_low = draw_sep_low(jax.random.fold_in(key_of[8], 71), 0)
    leaf_live = with_ends(jax.random.randint(key_of[6], (N_LEAF,), 1, LEAF // 128 + 1), jax.random.fold_in(key_of[6], 1), 1, (LEAF // 128 + 1) - 1).astype(jnp.int32)
    targets = draw_targets(jax.random.fold_in(key_of[8], 71), 0)
    return dict(leaf_rhs=leaf_rhs, sep_rhs=sep_rhs, leaf_inv=leaf_inv, leaf_low=leaf_low, sep_inv=sep_inv, sep_low=sep_low, leaf_live=leaf_live, targets=targets)


exact_mode = lax.Precision.HIGHEST


def complex_product(operand, factor, form):
    operand = operand.astype(jnp.float32)
    factor = factor.astype(jnp.float32)
    real_part = jnp.einsum(form, operand[0], factor[0], precision=exact_mode) - jnp.einsum(form, operand[1], factor[1], precision=exact_mode)
    imag_part = jnp.einsum(form, operand[0], factor[1], precision=exact_mode) + jnp.einsum(form, operand[1], factor[0], precision=exact_mode)
    return jnp.stack([real_part, imag_part])


def destination(targets, level_now):
    group_size = 2 ** (level_now + 1)
    source = jnp.arange(N_LEAF, dtype=jnp.int32)
    target_block = (source // group_size) * group_size + targets[level_now].astype(jnp.int32)
    return (target_block[:, None] == source[None, :]).astype(jnp.float32)


def rounded(values_in):
    return lax.optimization_barrier(values_in.astype(jnp.bfloat16)).astype(jnp.float32)


def reference(leaf_rhs, sep_rhs, leaf_inv, leaf_low, sep_inv, sep_low, leaf_live, targets):
    slab_inv = PR * (2 * N_LEAF - 2)
    slab_low = PR * (N_LEAF - 2)
    live_mask = (jnp.arange(LEAF)[None, :] < leaf_live[:, None] * 128).astype(jnp.float32)
    leaf_z = (leaf_rhs.reshape(2, NRHS, N_LEAF, LEAF) * live_mask[None, None]).astype(jnp.bfloat16)
    leaf_factor = leaf_inv.reshape(2, LEAF, N_LEAF, LEAF)
    leaf_panel = leaf_low.reshape(2, LEAF, N_LEAF, PR)
    leaf_w = complex_product(leaf_z, leaf_factor, 'rdi,idj->rdj') * live_mask[None, None]
    update = complex_product(leaf_z, leaf_panel, 'rdi,idp->rdp')
    inv_all = sep_inv.reshape(2, PR, N_LEAF, slab_inv)
    low_all = sep_low.reshape(2, PR, N_LEAF, slab_low)
    solved_w = []
    panels = []
    for level_now in range(1, LEVELS + 1):
        group_size = 2 ** level_now
        fronts = N_LEAF // group_size
        offset = PR * (group_size - 2)
        arriving = jnp.einsum('crjp,jn->crnp', update, destination(targets, level_now - 1), precision=exact_mode)
        level_z = (sep_rhs[:, :, level_now - 1].reshape(2, NRHS, N_LEAF, PR) - arriving).astype(jnp.bfloat16)
        front_z = level_z.reshape(2, NRHS, fronts, group_size, PR)
        inv_front = inv_all[..., offset: offset + PR * group_size].reshape(2, PR, fronts, group_size, PR * group_size)
        solved_w.append(complex_product(front_z, inv_front, 'rfmi,ifmj->rfj').reshape(2, NRHS, N_LEAF, PR))
        if level_now < LEVELS:
            low_front = low_all[..., offset: offset + PR * group_size].reshape(2, PR, fronts, group_size, PR * group_size)
            panels.append(low_front)
            update = complex_product(front_z, low_front, 'rfmi,ifmj->rfj').reshape(2, NRHS, N_LEAF, PR)
    solved_x = [solved_w[level_now] for level_now in range(LEVELS)]
    for level_now in range(LEVELS - 1, 0, -1):
        group_size = 2 ** level_now
        fronts = N_LEAF // group_size
        parent_x = rounded(solved_x[level_now])
        gathered = jnp.einsum('crnp,jn->crjp', parent_x, destination(targets, level_now), precision=exact_mode)
        front_g = gathered.reshape(2, NRHS, fronts, group_size * PR)
        solved_x[level_now - 1] = solved_w[level_now - 1] - complex_product(front_g, panels[level_now - 1], 'rfj,ifmj->rfmi').reshape(2, NRHS, N_LEAF, PR)
    parent_x = rounded(solved_x[0])
    gathered = jnp.einsum('crnp,jn->crjp', parent_x, destination(targets, 0), precision=exact_mode)
    leaf_x = (leaf_w - complex_product(gathered, leaf_panel, 'rdp,idp->rdi')) * live_mask[None, None]
    return leaf_x.reshape(2, NRHS, N_LEAF * LEAF), jnp.stack(solved_x, axis=2).reshape(2, NRHS, LEVELS, N_LEAF * PR)
```

```python
import functools

import jax
import jax.numpy as jnp
from jax import lax
from jax.experimental import pallas as pl
from jax.experimental.pallas import tpu as pltpu
from jax.sharding import PartitionSpec as P

exact_mode = lax.Precision.HIGHEST
VMEM = pltpu.MemorySpace.VMEM
SMEM = pltpu.MemorySpace.SMEM


def complex_dot(operand, factor):
    row_count = operand.shape[1]
    stacked = jnp.concatenate([operand[0], operand[1]], axis=0)
    real_acc = jnp.dot(stacked, factor[0], preferred_element_type=jnp.float32)
    imag_acc = jnp.dot(stacked, factor[1], preferred_element_type=jnp.float32)
    return jnp.stack(
        [real_acc[:row_count] - imag_acc[row_count:], imag_acc[:row_count] + real_acc[row_count:]]
    )


def complex_dot_back(operand, factor):
    row_count = operand.shape[1]
    stacked = jnp.concatenate([operand[0], operand[1]], axis=0)
    contract = (((1,), (1,)), ((), ()))
    real_acc = lax.dot_general(stacked, factor[0], contract, preferred_element_type=jnp.float32)
    imag_acc = lax.dot_general(stacked, factor[1], contract, preferred_element_type=jnp.float32)
    return jnp.stack(
        [real_acc[:row_count] - imag_acc[row_count:], imag_acc[:row_count] + real_acc[row_count:]]
    )


def to_blocks(values_in, group_size):
    return (
        values_in.reshape(2, values_in.shape[1], group_size, -1)
        .transpose(2, 0, 1, 3)
        .reshape(group_size, -1)
    )


def from_blocks(blocks, columns):
    group_size = blocks.shape[0]
    return blocks.reshape(group_size, 2, columns, -1).transpose(1, 2, 0, 3).reshape(2, columns, -1)


def selector(dest_index, total_slots):
    return (dest_index[:, None] == jnp.arange(total_slots, dtype=jnp.int32)[None, :]).astype(
        jnp.float32
    )


def exchange_sum(blocks, global_dest, devices):
    routed = jnp.dot(selector(global_dest, devices).T, blocks, precision=exact_mode)
    received = lax.all_to_all(
        routed.astype(jnp.bfloat16), "leaf", split_axis=0, concat_axis=0, tiled=True
    ).astype(routed.dtype)
    return jnp.sum(received, axis=0)


def collect(blocks, local_dest, level_bits, device, devices):
    group_start = device >> level_bits << level_bits
    return exchange_sum(blocks, group_start + local_dest, devices)


def spread(own_block, level_bits, device, devices):
    group_size = 2**level_bits
    group_start = device >> level_bits << level_bits
    slot_index = jnp.arange(devices, dtype=jnp.int32)[:, None]
    inside = (slot_index >= group_start) & (slot_index < group_start + group_size)
    routed = jnp.where(inside, own_block[None, :], jnp.zeros_like(own_block)[None, :])
    received = lax.all_to_all(routed, "leaf", split_axis=0, concat_axis=0, tiled=True)
    return lax.dynamic_slice_in_dim(received, group_start, group_size, 0)


def level_by_level(leaf_rhs, sep_rhs, leaf_w, leaf_low, sep_inv, sep_low, leaf_live, targets):
    devices = lax.axis_size("leaf")
    tree_depth = devices.bit_length() - 1
    device = lax.axis_index("leaf")
    leaf_rows = leaf_low.shape[1]
    sep_width = sep_inv.shape[1]
    columns = leaf_rhs.shape[1]
    live_mask = (jnp.arange(leaf_rows) < leaf_live[0] * 128).astype(jnp.float32)
    leaf_z = (leaf_rhs * live_mask).astype(jnp.bfloat16)
    first_dest = lax.dynamic_slice_in_dim(targets[0], device, 1)
    arriving = collect(complex_dot(leaf_z, leaf_low).reshape(1, -1), first_dest, 1, device, devices)
    solved_w = []
    for level_now in range(1, tree_depth + 1):
        group_size = 2**level_now
        offset = sep_width * (group_size - 2)
        level_z = (
            sep_rhs[:, :, level_now - 1, :] - arriving.reshape(2, columns, sep_width)
        ).astype(jnp.bfloat16)
        inv_rows = sep_inv[:, :, offset : offset + sep_width * group_size]
        own_w = collect(
            to_blocks(complex_dot(level_z, inv_rows), group_size),
            jnp.arange(group_size, dtype=jnp.int32),
            level_now,
            device,
            devices,
        )
        solved_w.append(own_w.reshape(2, columns, sep_width))
        if level_now < tree_depth:
            low_rows = sep_low[:, :, offset : offset + sep_width * group_size]
            group_start = device >> level_now << level_now
            dest_index = lax.dynamic_slice_in_dim(targets[level_now], group_start, group_size)
            arriving = collect(
                to_blocks(complex_dot(level_z, low_rows), group_size),
                dest_index,
                level_now + 1,
                device,
                devices,
            )
    solved_x = [solved_w[level_now] for level_now in range(tree_depth)]
    for level_now in range(tree_depth - 1, 0, -1):
        group_size = 2**level_now
        offset = sep_width * (group_size - 2)
        low_rows = sep_low[:, :, offset : offset + sep_width * group_size]
        parent_x = spread(
            solved_x[level_now].astype(jnp.bfloat16).reshape(-1), level_now + 1, device, devices
        )
        group_start = device >> level_now << level_now
        dest_index = lax.dynamic_slice_in_dim(targets[level_now], group_start, group_size)
        picked = jnp.dot(
            selector(dest_index, 2 * group_size).astype(jnp.bfloat16),
            parent_x,
            preferred_element_type=jnp.float32,
        ).astype(jnp.bfloat16)
        solved_x[level_now - 1] = solved_w[level_now - 1] - complex_dot_back(
            from_blocks(picked, columns), low_rows
        )
    parent_x = spread(solved_x[0].astype(jnp.bfloat16).reshape(-1), 1, device, devices)
    picked = jnp.dot(
        selector(first_dest, 2).astype(jnp.bfloat16), parent_x, preferred_element_type=jnp.float32
    ).astype(jnp.bfloat16)
    leaf_x = (
        leaf_w - complex_dot_back(picked.reshape(2, columns, sep_width), leaf_low)
    ) * live_mask
    return leaf_x, jnp.stack(solved_x, axis=2)


def masked_rows(leaf_rhs_ref, live_ref):
    rows = leaf_rhs_ref.shape[2]
    live = lax.broadcasted_iota(jnp.int32, (1, rows), 1) < live_ref[0] * 128
    stacked = jnp.concatenate([leaf_rhs_ref[0], leaf_rhs_ref[1]], axis=0)
    return jnp.where(live, stacked, 0.0).astype(jnp.bfloat16), live


def leaf_product_kernel(parts, live_ref, leaf_rhs_ref, *refs):
    inv_refs, out_ref, z_ref = refs[:parts], refs[parts], refs[parts + 1]
    columns = leaf_rhs_ref.shape[1]
    depth = inv_refs[0].shape[1]
    leaf_z, live = masked_rows(leaf_rhs_ref, live_ref)
    z_ref[...] = leaf_z
    mine = lax.axis_index("rhs")
    total = [None, None]
    for step in range(parts):
        owner = mine ^ step
        piece = z_ref[:, pl.ds(pl.multiple_of(owner * depth, 128), depth)]
        for part in range(2):
            term = jnp.dot(piece, inv_refs[step][part], preferred_element_type=jnp.float32)
            total[part] = term if step == 0 else total[part] + term
    real_acc, imag_acc = total
    out_ref[0] = jnp.where(live, real_acc[:columns] - imag_acc[columns:], 0.0)
    out_ref[1] = jnp.where(live, imag_acc[:columns] + real_acc[columns:], 0.0)


def xor_permute(values_in, axis, offset):
    count = lax.axis_size(axis)
    return lax.ppermute(values_in, axis, [(source, source ^ offset) for source in range(count)])


def leaf_product(leaf_rhs, leaf_inv, leaf_live):
    parts = lax.axis_size("rhs")
    pieces = {0: leaf_inv}
    offset = parts // 2
    while offset >= 1:
        for known in list(pieces):
            pieces[known ^ offset] = xor_permute(pieces[known], "rhs", offset)
        offset //= 2
    ordered = [pieces[step] for step in range(parts)]
    columns, rows = leaf_rhs.shape[1:]
    return pl.pallas_call(
        functools.partial(leaf_product_kernel, parts),
        out_shape=jax.ShapeDtypeStruct((2, columns, rows), jnp.float32),
        in_specs=[pl.BlockSpec(memory_space=SMEM)]
        + [pl.BlockSpec(memory_space=VMEM)] * (1 + parts),
        out_specs=pl.BlockSpec(memory_space=VMEM),
        scratch_shapes=[pltpu.VMEM((2 * columns, rows), jnp.bfloat16)],
        cost_estimate=pl.CostEstimate(
            flops=8 * columns * rows * rows, bytes_accessed=4 * rows * rows, transcendentals=0
        ),
    )(leaf_live, leaf_rhs, *ordered)


def pack_kernel(live_ref, leaf_rhs_ref, low_ref, rhs_ref, inv_ref, sep_low_ref, out_ref):
    columns = leaf_rhs_ref.shape[1]
    depth = rhs_ref.shape[1]
    leaf_z, _ = masked_rows(leaf_rhs_ref, live_ref)
    panel = jnp.concatenate([low_ref[0], low_ref[1]], axis=0)
    product = lax.dot_general(
        panel, leaf_z, (((1,), (1,)), ((), ())), preferred_element_type=jnp.float32
    )
    width = low_ref.shape[1]
    update = [
        product[:width, :columns] - product[width:, columns:],
        product[width:, :columns] + product[:width, columns:],
    ]
    used = (1 + depth) * columns + sep_low_ref.shape[2]
    halves = []
    for part in range(2):
        pieces = [update[part]] + [rhs_ref[part, level] for level in range(depth)]
        pieces.append(sep_low_ref[part].astype(jnp.float32))
        if used < 128:
            pieces.append(jnp.zeros((width, 128 - used), jnp.float32))
        pieces.append(inv_ref[part].astype(jnp.float32))
        if inv_ref.shape[2] < 128:
            pieces.append(jnp.zeros((width, 128 - inv_ref.shape[2]), jnp.float32))
        halves.append(jnp.concatenate(pieces, axis=1))
    out_ref[...] = jnp.concatenate(halves, axis=0).astype(jnp.bfloat16)


def tree_kernel(
    live_ref, targets_ref, gathered_ref, leaf_w_ref, low_ref, leaf_out_ref, sep_out_ref, panel_ref, turn_ref
):
    depth, devices = targets_ref.shape
    width = low_ref.shape[1]
    columns = leaf_w_ref.shape[1]
    slab = 2 * width
    size = devices * slab
    device = lax.axis_index("leaf")
    row = lax.broadcasted_iota(jnp.int32, (size, size), 0)
    lane = lax.broadcasted_iota(jnp.int32, (size, size), 1)
    lane_row = lax.broadcasted_iota(jnp.int32, (1, size), 1)
    row_part, lane_part = (row // width) % 2, (lane // width) % 2

    def owner(level, block):
        if level == 0:
            return jnp.int32(block)
        group = 2**level
        return block // group * group + targets_ref[level - 1, block]

    def rows_of(level):
        return jnp.concatenate(
            [
                gathered_ref[pl.ds(pl.multiple_of((owner(level, block) ^ device) * slab, slab), slab), :]
                for block in range(devices)
            ],
            axis=0,
        )

    raw = [rows_of(level) for level in range(depth + 1)]
    pick_row = lax.broadcasted_iota(jnp.int32, (columns, size), 0)
    pick_lane = lax.broadcasted_iota(jnp.int32, (columns, size), 1)
    back = (((1,), (1,)), ((), ()))

    def side(level):
        pick = jnp.where(pick_lane == pick_row + level * columns, 1.0, 0.0).astype(jnp.bfloat16)
        return lax.dot_general(pick, raw[level][:, :size], back, preferred_element_type=jnp.float32)

    def spread_lanes(source, first_lane, level, column_of):
        wanted = first_lane + column_of * width + lane_row % width
        pick = jnp.where(row == wanted, 1.0, 0.0).astype(jnp.bfloat16)
        plain = jnp.dot(source, pick, preferred_element_type=jnp.float32)
        swapped = plain.reshape(devices, 2, width, size)
        swapped = jnp.concatenate([swapped[:, 1:], swapped[:, :1]], axis=1).reshape(size, size)
        signed = jnp.where(row_part == 0, plain, -plain)
        full = jnp.where(lane_part == 0, signed, swapped)
        inside = row // (slab * 2**level) == lane // (slab * 2**level)
        return jnp.where(inside, full, 0.0).astype(jnp.bfloat16)

    low_start = (1 + depth) * columns
    inverse, lower = [None], [None]
    for level in range(1, depth + 1):
        offset = width * (2**level - 2)
        target_lane = jnp.zeros((1, size), jnp.int32)
        for block in range(devices):
            target_lane = jnp.where(lane_row // slab == block, targets_ref[level - 1, block], target_lane)
        inverse.append(spread_lanes(raw[level][:, size:], offset, level, target_lane))
        if level < depth:
            own_lane = (lane_row // slab) % 2**level
            lower.append(spread_lanes(raw[level][:, :size], low_start + offset, level, own_lane))

    arriving = side(0)
    partial = [None]
    for level in range(1, depth + 1):
        level_z = (side(level) - arriving).astype(jnp.bfloat16)
        partial.append(jnp.dot(level_z, inverse[level], preferred_element_type=jnp.float32))
        if level < depth:
            arriving = jnp.dot(level_z, lower[level], preferred_element_type=jnp.float32)

    sign = jnp.where((lane_row // width) % 2 == 0, 1.0, -1.0)
    solved = list(partial)
    for level in range(depth - 1, 0, -1):
        parent = (solved[level + 1] * sign).astype(jnp.bfloat16)
        product = lax.dot_general(parent, lower[level], back, preferred_element_type=jnp.float32)
        solved[level] = partial[level] - product * sign

    leaf_rows = low_ref.shape[2]
    panel_ref[...] = jnp.zeros_like(panel_ref)
    first = jnp.concatenate([low_ref[0], -low_ref[1]], axis=0)
    second = jnp.concatenate([low_ref[1], low_ref[0]], axis=0)
    panel_ref[pl.ds(pl.multiple_of(device * slab, slab), slab), :] = jnp.concatenate([first, second], axis=1)
    live = lax.broadcasted_iota(jnp.int32, (1, leaf_rows), 1) < live_ref[0] * 128
    product = jnp.dot(
        solved[1].astype(jnp.bfloat16), panel_ref[...], preferred_element_type=jnp.float32
    )
    for part in range(2):
        leaf_out_ref[part] = jnp.where(
            live, leaf_w_ref[part] - product[:, part * leaf_rows : (part + 1) * leaf_rows], 0.0
        )

    stacked = jnp.concatenate(
        solved[1:] + [jnp.zeros((size - depth * columns, size), jnp.float32)], axis=0
    )
    turn_ref[...] = stacked.T
    for level in range(1, depth + 1):
        place = jnp.int32(0)
        for block in range(devices):
            place = jnp.where(owner(level, block) == device, block, place)
        block_rows = turn_ref[pl.ds(pl.multiple_of(place * slab, slab), slab), :]
        for part in range(2):
            sep_out_ref[part, level - 1] = block_rows[
                part * width : (part + 1) * width, (level - 1) * columns : level * columns
            ]


def gathered_tree(leaf_rhs, sep_rhs, leaf_w, leaf_low, sep_inv, sep_low, leaf_live, targets):
    devices = lax.axis_size("leaf")
    columns, leaf_rows = leaf_rhs.shape[1:]
    width = sep_inv.shape[1]
    depth = sep_rhs.shape[2]
    slab = 2 * width
    size = devices * slab
    panel = leaf_low.transpose(0, 2, 1)
    tree_rhs = sep_rhs.transpose(0, 2, 3, 1)
    held = pl.pallas_call(
        pack_kernel,
        out_shape=jax.ShapeDtypeStruct((slab, 2 * size), jnp.bfloat16),
        in_specs=[pl.BlockSpec(memory_space=SMEM)] + [pl.BlockSpec(memory_space=VMEM)] * 5,
        out_specs=pl.BlockSpec(memory_space=VMEM),
    )(leaf_live, leaf_rhs, panel, tree_rhs, sep_inv, sep_low)
    offset = 1
    while offset < devices:
        held = jnp.concatenate([held, xor_permute(held, "leaf", offset)], axis=0)
        offset *= 2
    leaf_x, sep_x = pl.pallas_call(
        tree_kernel,
        out_shape=(
            jax.ShapeDtypeStruct((2, columns, leaf_rows), jnp.float32),
            jax.ShapeDtypeStruct((2, depth, width, columns), jnp.float32),
        ),
        in_specs=[pl.BlockSpec(memory_space=SMEM)] * 2 + [pl.BlockSpec(memory_space=VMEM)] * 3,
        out_specs=(pl.BlockSpec(memory_space=VMEM), pl.BlockSpec(memory_space=VMEM)),
        scratch_shapes=[
            pltpu.VMEM((size, 2 * leaf_rows), jnp.bfloat16),
            pltpu.VMEM((size, size), jnp.float32),
        ],
    )(leaf_live, targets, held, leaf_w, panel)
    return leaf_x, sep_x.transpose(0, 3, 1, 2)


def body(leaf_rhs, sep_rhs, leaf_inv, leaf_low, sep_inv, sep_low, leaf_live, targets):
    devices = lax.axis_size("leaf")
    columns = leaf_rhs.shape[1]
    width, depth = sep_inv.shape[1], sep_rhs.shape[2]
    leaf_w = leaf_product(leaf_rhs, leaf_inv, leaf_live)
    fits = (
        devices * 2 * width == 128
        and (1 + depth) * columns + sep_low.shape[2] <= 128
        and sep_inv.shape[2] <= 128
    )
    solve = gathered_tree if fits else level_by_level
    return solve(leaf_rhs, sep_rhs, leaf_w, leaf_low, sep_inv, sep_low, leaf_live, targets)


def solution(mesh):
    placed = (
        P(None, "rhs", "leaf"),
        P(None, "rhs", None, "leaf"),
        P(None, "rhs", "leaf"),
        P(None, None, "leaf"),
        P(None, None, "leaf"),
        P(None, None, "leaf"),
        P("leaf"),
        P(),
    )
    return jax.shard_map(
        body,
        mesh=mesh,
        in_specs=placed,
        out_specs=(P(None, "rhs", "leaf"), P(None, "rhs", None, "leaf")),
        check_vma=False,
    )
```

```python
import functools

import jax
import jax.numpy as jnp
from jax import lax
from jax.experimental import pallas as pl
from jax.experimental.pallas import tpu as pltpu
from jax.sharding import PartitionSpec as P

exact_mode = lax.Precision.HIGHEST
VMEM = pltpu.MemorySpace.VMEM
SMEM = pltpu.MemorySpace.SMEM


def complex_dot(operand, factor):
    row_count = operand.shape[1]
    stacked = jnp.concatenate([operand[0], operand[1]], axis=0)
    real_acc = jnp.dot(stacked, factor[0], preferred_element_type=jnp.float32)
    imag_acc = jnp.dot(stacked, factor[1], preferred_element_type=jnp.float32)
    return jnp.stack(
        [real_acc[:row_count] - imag_acc[row_count:], imag_acc[:row_count] + real_acc[row_count:]]
    )


def complex_dot_back(operand, factor):
    row_count = operand.shape[1]
    stacked = jnp.concatenate([operand[0], operand[1]], axis=0)
    contract = (((1,), (1,)), ((), ()))
    real_acc = lax.dot_general(stacked, factor[0], contract, preferred_element_type=jnp.float32)
    imag_acc = lax.dot_general(stacked, factor[1], contract, preferred_element_type=jnp.float32)
    return jnp.stack(
        [real_acc[:row_count] - imag_acc[row_count:], imag_acc[:row_count] + real_acc[row_count:]]
    )


def to_blocks(values_in, group_size):
    return (
        values_in.reshape(2, values_in.shape[1], group_size, -1)
        .transpose(2, 0, 1, 3)
        .reshape(group_size, -1)
    )


def from_blocks(blocks, columns):
    group_size = blocks.shape[0]
    return blocks.reshape(group_size, 2, columns, -1).transpose(1, 2, 0, 3).reshape(2, columns, -1)


def selector(dest_index, total_slots):
    return (dest_index[:, None] == jnp.arange(total_slots, dtype=jnp.int32)[None, :]).astype(
        jnp.float32
    )


def exchange_sum(blocks, global_dest, devices):
    routed = jnp.dot(selector(global_dest, devices).T, blocks, precision=exact_mode)
    received = lax.all_to_all(
        routed.astype(jnp.bfloat16), "leaf", split_axis=0, concat_axis=0, tiled=True
    ).astype(routed.dtype)
    return jnp.sum(received, axis=0)


def collect(blocks, local_dest, level_bits, device, devices):
    group_start = device >> level_bits << level_bits
    return exchange_sum(blocks, group_start + local_dest, devices)


def spread(own_block, level_bits, device, devices):
    group_size = 2**level_bits
    group_start = device >> level_bits << level_bits
    slot_index = jnp.arange(devices, dtype=jnp.int32)[:, None]
    inside = (slot_index >= group_start) & (slot_index < group_start + group_size)
    routed = jnp.where(inside, own_block[None, :], jnp.zeros_like(own_block)[None, :])
    received = lax.all_to_all(routed, "leaf", split_axis=0, concat_axis=0, tiled=True)
    return lax.dynamic_slice_in_dim(received, group_start, group_size, 0)


def level_by_level(leaf_rhs, sep_rhs, leaf_w, leaf_low, sep_inv, sep_low, leaf_live, targets):
    devices = lax.axis_size("leaf")
    tree_depth = devices.bit_length() - 1
    device = lax.axis_index("leaf")
    leaf_rows = leaf_low.shape[1]
    sep_width = sep_inv.shape[1]
    columns = leaf_rhs.shape[1]
    live_mask = (jnp.arange(leaf_rows) < leaf_live[0] * 128).astype(jnp.float32)
    leaf_z = (leaf_rhs * live_mask).astype(jnp.bfloat16)
    first_dest = lax.dynamic_slice_in_dim(targets[0], device, 1)
    arriving = collect(complex_dot(leaf_z, leaf_low).reshape(1, -1), first_dest, 1, device, devices)
    solved_w = []
    for level_now in range(1, tree_depth + 1):
        group_size = 2**level_now
        offset = sep_width * (group_size - 2)
        level_z = (
            sep_rhs[:, :, level_now - 1, :] - arriving.reshape(2, columns, sep_width)
        ).astype(jnp.bfloat16)
        inv_rows = sep_inv[:, :, offset : offset + sep_width * group_size]
        own_w = collect(
            to_blocks(complex_dot(level_z, inv_rows), group_size),
            jnp.arange(group_size, dtype=jnp.int32),
            level_now,
            device,
            devices,
        )
        solved_w.append(own_w.reshape(2, columns, sep_width))
        if level_now < tree_depth:
            low_rows = sep_low[:, :, offset : offset + sep_width * group_size]
            group_start = device >> level_now << level_now
            dest_index = lax.dynamic_slice_in_dim(targets[level_now], group_start, group_size)
            arriving = collect(
                to_blocks(complex_dot(level_z, low_rows), group_size),
                dest_index,
                level_now + 1,
                device,
                devices,
            )
    solved_x = [solved_w[level_now] for level_now in range(tree_depth)]
    for level_now in range(tree_depth - 1, 0, -1):
        group_size = 2**level_now
        offset = sep_width * (group_size - 2)
        low_rows = sep_low[:, :, offset : offset + sep_width * group_size]
        parent_x = spread(
            solved_x[level_now].astype(jnp.bfloat16).reshape(-1), level_now + 1, device, devices
        )
        group_start = device >> level_now << level_now
        dest_index = lax.dynamic_slice_in_dim(targets[level_now], group_start, group_size)
        picked = jnp.dot(
            selector(dest_index, 2 * group_size).astype(jnp.bfloat16),
            parent_x,
            preferred_element_type=jnp.float32,
        ).astype(jnp.bfloat16)
        solved_x[level_now - 1] = solved_w[level_now - 1] - complex_dot_back(
            from_blocks(picked, columns), low_rows
        )
    parent_x = spread(solved_x[0].astype(jnp.bfloat16).reshape(-1), 1, device, devices)
    picked = jnp.dot(
        selector(first_dest, 2).astype(jnp.bfloat16), parent_x, preferred_element_type=jnp.float32
    ).astype(jnp.bfloat16)
    leaf_x = (
        leaf_w - complex_dot_back(picked.reshape(2, columns, sep_width), leaf_low)
    ) * live_mask
    return leaf_x, jnp.stack(solved_x, axis=2)


def xor_permute(values_in, axis, offset):
    count = lax.axis_size(axis)
    return lax.ppermute(values_in, axis, [(source, source ^ offset) for source in range(count)])


def gather_pieces(own_piece, hold=lambda piece: piece):
    parts = lax.axis_size("rhs")
    pieces = {0: own_piece}
    offset = parts // 2
    while offset >= 1:
        for known in list(pieces):
            source = pieces[known] if known == 0 else hold(pieces[known])
            pieces[known] = source
            pieces[known ^ offset] = xor_permute(source, "rhs", offset)
        offset //= 2
    return [pieces[step] for step in range(parts)]


def in_vmem(values_in):
    return pltpu.with_memory_space_constraint(values_in, VMEM)


def masked_rows(leaf_rhs, live_ref):
    rows = leaf_rhs.shape[2]
    live = lax.broadcasted_iota(jnp.int32, (1, rows), 1) < live_ref[0] * 128
    stacked = jnp.concatenate([leaf_rhs[0], leaf_rhs[1]], axis=0)
    return jnp.where(live, stacked, 0.0).astype(jnp.bfloat16), live


def pack_kernel(live_ref, *refs):
    sources, (out_ref, z_ref), places, sems = refs[:5], refs[5:7], refs[7:12], refs[12]
    copies = [
        pltpu.make_async_copy(source, place, sems.at[which])
        for which, (source, place) in enumerate(zip(sources, places))
    ]
    for copy in copies:
        copy.start()
    for copy in copies:
        copy.wait()
    leaf_rhs_ref, low_ref, rhs_ref, inv_ref, sep_low_ref = places
    columns = leaf_rhs_ref.shape[1]
    depth = rhs_ref.shape[1]
    leaf_z, _ = masked_rows(leaf_rhs_ref[...], live_ref)
    z_ref[...] = leaf_z
    panel = jnp.concatenate([low_ref[0], low_ref[1]], axis=0)
    product = lax.dot_general(
        panel, leaf_z, (((1,), (1,)), ((), ())), preferred_element_type=jnp.float32
    )
    width = low_ref.shape[1]
    update = [
        product[:width, :columns] - product[width:, columns:],
        product[width:, :columns] + product[:width, columns:],
    ]
    used = (1 + depth) * columns + sep_low_ref.shape[2]
    halves = []
    for part in range(2):
        pieces = [update[part]] + [rhs_ref[part, level] for level in range(depth)]
        pieces.append(sep_low_ref[part].astype(jnp.float32))
        if used < 128:
            pieces.append(jnp.zeros((width, 128 - used), jnp.float32))
        pieces.append(inv_ref[part].astype(jnp.float32))
        if inv_ref.shape[2] < 128:
            pieces.append(jnp.zeros((width, 128 - inv_ref.shape[2]), jnp.float32))
        halves.append(jnp.concatenate(pieces, axis=1))
    out_ref[...] = jnp.concatenate(halves, axis=0).astype(jnp.bfloat16)


def leaf_kernel(parts, live_ref, z_ref, *refs):
    inv_refs, out_ref = refs[:parts], refs[parts]
    columns = out_ref.shape[1]
    depth = inv_refs[0].shape[1]
    mine = lax.axis_index("rhs")
    total = [None, None]
    for step in range(parts):
        owner = mine ^ step
        piece = z_ref[:, pl.ds(pl.multiple_of(owner * depth, 128), depth)]
        for part in range(2):
            term = jnp.dot(piece, inv_refs[step][part], preferred_element_type=jnp.float32)
            total[part] = term if step == 0 else total[part] + term
    real_acc, imag_acc = total
    live = lax.broadcasted_iota(jnp.int32, (1, z_ref.shape[1]), 1) < live_ref[0] * 128
    out_ref[0] = jnp.where(live, real_acc[:columns] - imag_acc[columns:], 0.0)
    out_ref[1] = jnp.where(live, imag_acc[:columns] + real_acc[columns:], 0.0)


def prepare_kernel(low_start, live_ref, targets_ref, low_ref, panel_ref, pick_ref, kept_ref):
    for level in range(targets_ref.shape[0]):
        for block in range(targets_ref.shape[1]):
            kept_ref[level, block] = targets_ref[level, block]
    depth, devices = targets_ref.shape
    width, leaf_rows = low_ref.shape[1:]
    slab = 2 * width
    device = lax.axis_index("leaf")
    live = lax.broadcasted_iota(jnp.int32, (1, leaf_rows), 1) < live_ref[0] * 128
    low = [jnp.where(live, low_ref[part].astype(jnp.float32), 0.0) for part in range(2)]
    rows = jnp.concatenate(
        [
            jnp.concatenate([low[0], low[1]], axis=1),
            jnp.concatenate([-low[1], low[0]], axis=1),
        ],
        axis=0,
    ).astype(jnp.bfloat16)
    panel_ref[...] = jnp.zeros_like(panel_ref)
    panel_ref[pl.ds(pl.multiple_of(device * slab, slab), slab), :] = rows
    size = devices * slab
    row = lax.broadcasted_iota(jnp.int32, (size, size), 0)
    lane_row = lax.broadcasted_iota(jnp.int32, (1, size), 1)
    for level in range(1, depth + 1):
        offset = width * (2**level - 2) + lane_row % width
        target_lane = jnp.zeros((1, size), jnp.int32)
        for block in range(devices):
            target_lane = jnp.where(lane_row // slab == block, targets_ref[level - 1, block], target_lane)
        pick_ref[level - 1] = jnp.where(row == offset + target_lane * width, 1.0, 0.0).astype(jnp.bfloat16)
        if level < depth:
            own_lane = (lane_row // slab) % 2**level
            pick_ref[depth + level - 1] = jnp.where(
                row == low_start + offset + own_lane * width, 1.0, 0.0
            ).astype(jnp.bfloat16)


def join_kernel(own_ref, other_ref, out_ref):
    rows = own_ref.shape[0]
    out_ref[:rows] = own_ref[...]
    out_ref[rows:] = other_ref[...]


def hold_kernel(piece_ref, _, out_ref):
    pass


def tree_kernel(
    targets_ref, near_ref, far_ref, leaf_w_ref, panel_ref, pick_ref, leaf_out_ref, sep_out_ref, all_ref, turn_ref
):
    depth, devices = targets_ref.shape
    size = panel_ref.shape[0]
    slab = size // devices
    width = slab // 2
    columns = leaf_w_ref.shape[1]
    device = lax.axis_index("leaf")
    row = lax.broadcasted_iota(jnp.int32, (size, size), 0)
    lane = lax.broadcasted_iota(jnp.int32, (size, size), 1)
    lane_row = lax.broadcasted_iota(jnp.int32, (1, size), 1)
    row_part, lane_part = (row // width) % 2, (lane // width) % 2
    all_ref[: size // 2, :] = near_ref[...]
    all_ref[size // 2 :, :] = far_ref[...]

    def owner(level, block):
        if level == 0:
            return jnp.int32(block)
        group = 2**level
        return block // group * group + targets_ref[level - 1, block]

    def rows_of(level):
        return jnp.concatenate(
            [
                all_ref[pl.ds(pl.multiple_of((owner(level, block) ^ device) * slab, slab), slab), :]
                for block in range(devices)
            ],
            axis=0,
        )

    raw = [rows_of(level) for level in range(depth + 1)]
    pick_row = lax.broadcasted_iota(jnp.int32, (columns, size), 0)
    pick_lane = lax.broadcasted_iota(jnp.int32, (columns, size), 1)
    back = (((1,), (1,)), ((), ()))

    def side(level):
        pick = jnp.where(pick_lane == pick_row + level * columns, 1.0, 0.0).astype(jnp.bfloat16)
        return lax.dot_general(pick, raw[level][:, :size], back, preferred_element_type=jnp.float32)

    def front_matrix(source, pick, level):
        plain = jnp.dot(source, pick, preferred_element_type=jnp.float32)
        swapped = plain.reshape(devices, 2, width, size)
        swapped = jnp.concatenate([swapped[:, 1:], swapped[:, :1]], axis=1).reshape(size, size)
        signed = jnp.where(row_part == 0, plain, -plain)
        full = jnp.where(lane_part == 0, signed, swapped)
        inside = row // (slab * 2**level) == lane // (slab * 2**level)
        return jnp.where(inside, full, 0.0).astype(jnp.bfloat16)

    inverse, lower = [None], [None]
    for level in range(1, depth + 1):
        inverse.append(front_matrix(raw[level][:, size:], pick_ref[level - 1], level))
        if level < depth:
            lower.append(front_matrix(raw[level][:, :size], pick_ref[depth + level - 1], level))

    arriving = side(0)
    partial = [None]
    for level in range(1, depth + 1):
        level_z = (side(level) - arriving).astype(jnp.bfloat16)
        partial.append(jnp.dot(level_z, inverse[level], preferred_element_type=jnp.float32))
        if level < depth:
            arriving = jnp.dot(level_z, lower[level], preferred_element_type=jnp.float32)

    sign = jnp.where((lane_row // width) % 2 == 0, 1.0, -1.0)
    solved = list(partial)
    for level in range(depth - 1, 0, -1):
        parent = (solved[level + 1] * sign).astype(jnp.bfloat16)
        product = lax.dot_general(parent, lower[level], back, preferred_element_type=jnp.float32)
        solved[level] = partial[level] - product * sign

    leaf_rows = leaf_w_ref.shape[2]
    product = jnp.dot(
        solved[1].astype(jnp.bfloat16), panel_ref[...], preferred_element_type=jnp.float32
    )
    for part in range(2):
        leaf_out_ref[part] = leaf_w_ref[part] - product[:, part * leaf_rows : (part + 1) * leaf_rows]

    stacked = jnp.concatenate(
        solved[1:] + [jnp.zeros((size - depth * columns, size), jnp.float32)], axis=0
    )
    turn_ref[...] = stacked.T
    for level in range(1, depth + 1):
        place = jnp.int32(0)
        for block in range(devices):
            place = jnp.where(owner(level, block) == device, block, place)
        block_rows = turn_ref[pl.ds(pl.multiple_of(place * slab, slab), slab), :]
        for part in range(2):
            sep_out_ref[part, level - 1] = block_rows[
                part * width : (part + 1) * width, (level - 1) * columns : level * columns
            ]


def whole(space):
    return pl.BlockSpec(memory_space=space)


def body(leaf_rhs, sep_rhs, leaf_inv, leaf_low, sep_inv, sep_low, leaf_live, targets):
    devices, parts = lax.axis_size("leaf"), lax.axis_size("rhs")
    columns, leaf_rows = leaf_rhs.shape[1:]
    width, depth = sep_inv.shape[1], sep_rhs.shape[2]
    slab = 2 * width
    size = devices * slab
    small_tree = (
        size == 128 and (1 + depth) * columns + sep_low.shape[2] <= 128 and sep_inv.shape[2] <= 128
    )
    panel = leaf_low.transpose(0, 2, 1)
    tree_rhs = sep_rhs.transpose(0, 2, 3, 1)

    def leaf_w_of(leaf_z, pieces):
        return pl.pallas_call(
            functools.partial(leaf_kernel, parts),
            out_shape=pltpu.VMEM((2, columns, leaf_rows), jnp.float32),
            in_specs=[whole(SMEM)] + [whole(VMEM)] * (1 + parts),
            out_specs=whole(VMEM),
            cost_estimate=pl.CostEstimate(
                flops=8 * columns * leaf_rows * leaf_rows,
                bytes_accessed=4 * leaf_rows * leaf_rows,
                transcendentals=0,
            ),
        )(leaf_live, *[in_vmem(ready) for ready in [leaf_z] + pieces])

    if not small_tree:
        live_mask = (jnp.arange(leaf_rows) < leaf_live[0] * 128).astype(jnp.float32)
        leaf_z = (leaf_rhs * live_mask).astype(jnp.bfloat16).reshape(2 * columns, leaf_rows)
        leaf_w = leaf_w_of(leaf_z, gather_pieces(leaf_inv))
        return level_by_level(leaf_rhs, sep_rhs, leaf_w, leaf_low, sep_inv, sep_low, leaf_live, targets)

    tree_parts = (leaf_rhs, panel, tree_rhs, sep_inv, sep_low)
    held, leaf_z = pl.pallas_call(
        pack_kernel,
        out_shape=(
            pltpu.VMEM((slab, 2 * size), jnp.bfloat16),
            pltpu.VMEM((2 * columns, leaf_rows), jnp.bfloat16),
        ),
        in_specs=[whole(SMEM)] + [whole(pl.ANY)] * 5,
        out_specs=(whole(VMEM),) * 2,
        scratch_shapes=[pltpu.VMEM(part.shape, part.dtype) for part in tree_parts]
        + [pltpu.SemaphoreType.DMA((5,))],
    )(leaf_live, *tree_parts)
    panel_rows, picks, kept_targets = pl.pallas_call(
        functools.partial(prepare_kernel, (1 + depth) * columns),
        out_shape=(
            pltpu.VMEM((size, 2 * leaf_rows), jnp.bfloat16),
            pltpu.VMEM((2 * depth - 1, size, size), jnp.bfloat16),
            pltpu.SMEM(targets.shape, jnp.int32),
        ),
        in_specs=[whole(SMEM), whole(SMEM), whole(VMEM)],
        out_specs=(whole(VMEM),) * 2 + (whole(SMEM),),
        cost_estimate=pl.CostEstimate(flops=0, bytes_accessed=2 * 1024 * 1024, transcendentals=0),
    )(leaf_live, targets, panel)

    def join(own, other):
        return pl.pallas_call(
            join_kernel,
            out_shape=pltpu.VMEM((2 * own.shape[0], own.shape[1]), own.dtype),
            in_specs=[whole(VMEM)] * 2,
            out_specs=whole(VMEM),
            cost_estimate=pl.CostEstimate(
                flops=0, bytes_accessed=32 * 1024 * 1024, transcendentals=0
            ),
        )(in_vmem(own), in_vmem(other))

    rounds = [held]
    offset = 1
    while offset < devices:
        rounds.append(xor_permute(held, "leaf", offset))
        offset *= 2
        if offset < devices:
            held = join(held, rounds[-1])

    def hold(piece):
        return pl.pallas_call(
            hold_kernel,
            out_shape=pltpu.VMEM(piece.shape, piece.dtype),
            in_specs=[whole(VMEM)] * 2,
            out_specs=whole(VMEM),
            input_output_aliases={0: 0},
        )(in_vmem(piece), in_vmem(held))

    leaf_w = leaf_w_of(leaf_z, gather_pieces(leaf_inv, hold))
    leaf_x, sep_x = pl.pallas_call(
        tree_kernel,
        out_shape=(
            jax.ShapeDtypeStruct((2, columns, leaf_rows), jnp.float32),
            jax.ShapeDtypeStruct((2, depth, width, columns), jnp.float32),
        ),
        in_specs=[whole(SMEM)] + [whole(VMEM)] * 5,
        out_specs=(whole(VMEM), whole(VMEM)),
        scratch_shapes=[
            pltpu.VMEM((size, 2 * size), jnp.bfloat16),
            pltpu.VMEM((size, size), jnp.float32),
        ],
    )(
        pltpu.with_memory_space_constraint(kept_targets, SMEM),
        *[in_vmem(ready) for ready in (held, rounds[-1], leaf_w, panel_rows, picks)],
    )
    return leaf_x, sep_x.transpose(0, 3, 1, 2)


def solution(mesh):
    placed = (
        P(None, "rhs", "leaf"),
        P(None, "rhs", None, "leaf"),
        P(None, "rhs", "leaf"),
        P(None, None, "leaf"),
        P(None, None, "leaf"),
        P(None, None, "leaf"),
        P("leaf"),
        P(),
    )
    return jax.shard_map(
        body,
        mesh=mesh,
        in_specs=placed,
        out_specs=(P(None, "rhs", "leaf"), P(None, "rhs", None, "leaf")),
        check_vma=False,
    )
```

```python
import functools

import jax
import jax.numpy as jnp
from jax import lax
from jax.experimental import pallas as pl
from jax.experimental.pallas import tpu as pltpu
from jax.sharding import PartitionSpec as P

exact_mode = lax.Precision.HIGHEST
VMEM = pltpu.MemorySpace.VMEM
SMEM = pltpu.MemorySpace.SMEM


def complex_dot(operand, factor):
    row_count = operand.shape[1]
    stacked = jnp.concatenate([operand[0], operand[1]], axis=0)
    real_acc = jnp.dot(stacked, factor[0], preferred_element_type=jnp.float32)
    imag_acc = jnp.dot(stacked, factor[1], preferred_element_type=jnp.float32)
    return jnp.stack(
        [real_acc[:row_count] - imag_acc[row_count:], imag_acc[:row_count] + real_acc[row_count:]]
    )


def complex_dot_back(operand, factor):
    row_count = operand.shape[1]
    stacked = jnp.concatenate([operand[0], operand[1]], axis=0)
    contract = (((1,), (1,)), ((), ()))
    real_acc = lax.dot_general(stacked, factor[0], contract, preferred_element_type=jnp.float32)
    imag_acc = lax.dot_general(stacked, factor[1], contract, preferred_element_type=jnp.float32)
    return jnp.stack(
        [real_acc[:row_count] - imag_acc[row_count:], imag_acc[:row_count] + real_acc[row_count:]]
    )


def to_blocks(values_in, group_size):
    return (
        values_in.reshape(2, values_in.shape[1], group_size, -1)
        .transpose(2, 0, 1, 3)
        .reshape(group_size, -1)
    )


def from_blocks(blocks, columns):
    group_size = blocks.shape[0]
    return blocks.reshape(group_size, 2, columns, -1).transpose(1, 2, 0, 3).reshape(2, columns, -1)


def selector(dest_index, total_slots):
    return (dest_index[:, None] == jnp.arange(total_slots, dtype=jnp.int32)[None, :]).astype(
        jnp.float32
    )


def exchange_sum(blocks, global_dest, devices):
    routed = jnp.dot(selector(global_dest, devices).T, blocks, precision=exact_mode)
    received = lax.all_to_all(
        routed.astype(jnp.bfloat16), "leaf", split_axis=0, concat_axis=0, tiled=True
    ).astype(routed.dtype)
    return jnp.sum(received, axis=0)


def collect(blocks, local_dest, level_bits, device, devices):
    group_start = device >> level_bits << level_bits
    return exchange_sum(blocks, group_start + local_dest, devices)


def spread(own_block, level_bits, device, devices):
    group_size = 2**level_bits
    group_start = device >> level_bits << level_bits
    slot_index = jnp.arange(devices, dtype=jnp.int32)[:, None]
    inside = (slot_index >= group_start) & (slot_index < group_start + group_size)
    routed = jnp.where(inside, own_block[None, :], jnp.zeros_like(own_block)[None, :])
    received = lax.all_to_all(routed, "leaf", split_axis=0, concat_axis=0, tiled=True)
    return lax.dynamic_slice_in_dim(received, group_start, group_size, 0)


def level_by_level(leaf_rhs, sep_rhs, leaf_w, leaf_low, sep_inv, sep_low, leaf_live, targets):
    devices = lax.axis_size("leaf")
    tree_depth = devices.bit_length() - 1
    device = lax.axis_index("leaf")
    leaf_rows = leaf_low.shape[1]
    sep_width = sep_inv.shape[1]
    columns = leaf_rhs.shape[1]
    live_mask = (jnp.arange(leaf_rows) < leaf_live[0] * 128).astype(jnp.float32)
    leaf_z = (leaf_rhs * live_mask).astype(jnp.bfloat16)
    first_dest = lax.dynamic_slice_in_dim(targets[0], device, 1)
    arriving = collect(complex_dot(leaf_z, leaf_low).reshape(1, -1), first_dest, 1, device, devices)
    solved_w = []
    for level_now in range(1, tree_depth + 1):
        group_size = 2**level_now
        offset = sep_width * (group_size - 2)
        level_z = (
            sep_rhs[:, :, level_now - 1, :] - arriving.reshape(2, columns, sep_width)
        ).astype(jnp.bfloat16)
        inv_rows = sep_inv[:, :, offset : offset + sep_width * group_size]
        own_w = collect(
            to_blocks(complex_dot(level_z, inv_rows), group_size),
            jnp.arange(group_size, dtype=jnp.int32),
            level_now,
            device,
            devices,
        )
        solved_w.append(own_w.reshape(2, columns, sep_width))
        if level_now < tree_depth:
            low_rows = sep_low[:, :, offset : offset + sep_width * group_size]
            group_start = device >> level_now << level_now
            dest_index = lax.dynamic_slice_in_dim(targets[level_now], group_start, group_size)
            arriving = collect(
                to_blocks(complex_dot(level_z, low_rows), group_size),
                dest_index,
                level_now + 1,
                device,
                devices,
            )
    solved_x = [solved_w[level_now] for level_now in range(tree_depth)]
    for level_now in range(tree_depth - 1, 0, -1):
        group_size = 2**level_now
        offset = sep_width * (group_size - 2)
        low_rows = sep_low[:, :, offset : offset + sep_width * group_size]
        parent_x = spread(
            solved_x[level_now].astype(jnp.bfloat16).reshape(-1), level_now + 1, device, devices
        )
        group_start = device >> level_now << level_now
        dest_index = lax.dynamic_slice_in_dim(targets[level_now], group_start, group_size)
        picked = jnp.dot(
            selector(dest_index, 2 * group_size).astype(jnp.bfloat16),
            parent_x,
            preferred_element_type=jnp.float32,
        ).astype(jnp.bfloat16)
        solved_x[level_now - 1] = solved_w[level_now - 1] - complex_dot_back(
            from_blocks(picked, columns), low_rows
        )
    parent_x = spread(solved_x[0].astype(jnp.bfloat16).reshape(-1), 1, device, devices)
    picked = jnp.dot(
        selector(first_dest, 2).astype(jnp.bfloat16), parent_x, preferred_element_type=jnp.float32
    ).astype(jnp.bfloat16)
    leaf_x = (
        leaf_w - complex_dot_back(picked.reshape(2, columns, sep_width), leaf_low)
    ) * live_mask
    return leaf_x, jnp.stack(solved_x, axis=2)


def xor_permute(values_in, axis, offset):
    count = lax.axis_size(axis)
    return lax.ppermute(values_in, axis, [(source, source ^ offset) for source in range(count)])


def gather_pieces(own_piece, hold=lambda piece: piece):
    parts = lax.axis_size("rhs")
    pieces = {0: own_piece}
    offset = parts // 2
    while offset >= 1:
        for known in list(pieces):
            source = pieces[known] if known == 0 else hold(pieces[known])
            pieces[known] = source
            pieces[known ^ offset] = xor_permute(source, "rhs", offset)
        offset //= 2
    return [pieces[step] for step in range(parts)]


def in_vmem(values_in):
    return pltpu.with_memory_space_constraint(values_in, VMEM)


def masked_rows(leaf_rhs, live_ref):
    rows = leaf_rhs.shape[2]
    live = lax.broadcasted_iota(jnp.int32, (1, rows), 1) < live_ref[0] * 128
    stacked = jnp.concatenate([leaf_rhs[0], leaf_rhs[1]], axis=0)
    return jnp.where(live, stacked, 0.0).astype(jnp.bfloat16), live


def first_kernel(out_ref):
    out_ref[...] = jnp.zeros_like(out_ref)


def pack_kernel(live_ref, _, leaf_rhs_ref, low_ref, rhs_ref, inv_ref, sep_low_ref, out_ref, z_ref):
    columns = leaf_rhs_ref.shape[1]
    depth = rhs_ref.shape[1]
    leaf_z, _ = masked_rows(leaf_rhs_ref[...], live_ref)
    z_ref[...] = leaf_z
    panel = jnp.concatenate([low_ref[0], low_ref[1]], axis=0)
    product = lax.dot_general(
        panel, leaf_z, (((1,), (1,)), ((), ())), preferred_element_type=jnp.float32
    )
    width = low_ref.shape[1]
    update = [
        product[:width, :columns] - product[width:, columns:],
        product[width:, :columns] + product[:width, columns:],
    ]
    used = (1 + depth) * columns + sep_low_ref.shape[2]
    halves = []
    for part in range(2):
        pieces = [update[part]] + [rhs_ref[part, level] for level in range(depth)]
        pieces.append(sep_low_ref[part].astype(jnp.float32))
        if used < 128:
            pieces.append(jnp.zeros((width, 128 - used), jnp.float32))
        pieces.append(inv_ref[part].astype(jnp.float32))
        if inv_ref.shape[2] < 128:
            pieces.append(jnp.zeros((width, 128 - inv_ref.shape[2]), jnp.float32))
        halves.append(jnp.concatenate(pieces, axis=1))
    out_ref[...] = jnp.concatenate(halves, axis=0).astype(jnp.bfloat16)


def leaf_kernel(parts, live_ref, z_ref, *refs):
    inv_refs, out_ref = refs[:parts], refs[parts]
    columns = out_ref.shape[1]
    depth = inv_refs[0].shape[1]
    mine = lax.axis_index("rhs")
    total = [None, None]
    for step in range(parts):
        owner = mine ^ step
        piece = z_ref[:, pl.ds(pl.multiple_of(owner * depth, 128), depth)]
        for part in range(2):
            term = jnp.dot(piece, inv_refs[step][part], preferred_element_type=jnp.float32)
            total[part] = term if step == 0 else total[part] + term
    real_acc, imag_acc = total
    live = lax.broadcasted_iota(jnp.int32, (1, z_ref.shape[1]), 1) < live_ref[0] * 128
    out_ref[0] = jnp.where(live, real_acc[:columns] - imag_acc[columns:], 0.0)
    out_ref[1] = jnp.where(live, imag_acc[:columns] + real_acc[columns:], 0.0)


def prepare_kernel(low_start, live_ref, targets_ref, low_ref, _, panel_ref, pick_ref, kept_ref):
    for level in range(targets_ref.shape[0]):
        for block in range(targets_ref.shape[1]):
            kept_ref[level, block] = targets_ref[level, block]
    depth, devices = targets_ref.shape
    width, leaf_rows = low_ref.shape[1:]
    slab = 2 * width
    device = lax.axis_index("leaf")
    live = lax.broadcasted_iota(jnp.int32, (1, leaf_rows), 1) < live_ref[0] * 128
    low = [jnp.where(live, low_ref[part].astype(jnp.float32), 0.0) for part in range(2)]
    rows = jnp.concatenate(
        [
            jnp.concatenate([low[0], low[1]], axis=1),
            jnp.concatenate([-low[1], low[0]], axis=1),
        ],
        axis=0,
    ).astype(jnp.bfloat16)
    panel_ref[...] = jnp.zeros_like(panel_ref)
    panel_ref[pl.ds(pl.multiple_of(device * slab, slab), slab), :] = rows
    size = devices * slab
    row = lax.broadcasted_iota(jnp.int32, (size, size), 0)
    lane_row = lax.broadcasted_iota(jnp.int32, (1, size), 1)
    for level in range(1, depth + 1):
        offset = width * (2**level - 2) + lane_row % width
        target_lane = jnp.zeros((1, size), jnp.int32)
        for block in range(devices):
            target_lane = jnp.where(lane_row // slab == block, targets_ref[level - 1, block], target_lane)
        pick_ref[level - 1] = jnp.where(row == offset + target_lane * width, 1.0, 0.0).astype(jnp.bfloat16)
        if level < depth:
            own_lane = (lane_row // slab) % 2**level
            pick_ref[depth + level - 1] = jnp.where(
                row == low_start + offset + own_lane * width, 1.0, 0.0
            ).astype(jnp.bfloat16)


def join_kernel(own_ref, other_ref, out_ref):
    rows = own_ref.shape[0]
    out_ref[:rows] = own_ref[...]
    out_ref[rows:] = other_ref[...]


def hold_kernel(piece_ref, _, out_ref):
    pass


def tree_kernel(
    targets_ref, near_ref, far_ref, leaf_w_ref, panel_ref, pick_ref, leaf_out_ref, sep_out_ref, all_ref, turn_ref
):
    depth, devices = targets_ref.shape
    size = panel_ref.shape[0]
    slab = size // devices
    width = slab // 2
    columns = leaf_w_ref.shape[1]
    device = lax.axis_index("leaf")
    row = lax.broadcasted_iota(jnp.int32, (size, size), 0)
    lane = lax.broadcasted_iota(jnp.int32, (size, size), 1)
    lane_row = lax.broadcasted_iota(jnp.int32, (1, size), 1)
    row_part, lane_part = (row // width) % 2, (lane // width) % 2
    all_ref[: size // 2, :] = near_ref[...]
    all_ref[size // 2 :, :] = far_ref[...]

    def owner(level, block):
        if level == 0:
            return jnp.int32(block)
        group = 2**level
        return block // group * group + targets_ref[level - 1, block]

    def rows_of(level):
        return jnp.concatenate(
            [
                all_ref[pl.ds(pl.multiple_of((owner(level, block) ^ device) * slab, slab), slab), :]
                for block in range(devices)
            ],
            axis=0,
        )

    raw = [rows_of(level) for level in range(depth + 1)]
    pick_row = lax.broadcasted_iota(jnp.int32, (columns, size), 0)
    pick_lane = lax.broadcasted_iota(jnp.int32, (columns, size), 1)
    back = (((1,), (1,)), ((), ()))

    def side(level):
        pick = jnp.where(pick_lane == pick_row + level * columns, 1.0, 0.0).astype(jnp.bfloat16)
        return lax.dot_general(pick, raw[level][:, :size], back, preferred_element_type=jnp.float32)

    def front_matrix(source, pick, level):
        plain = jnp.dot(source, pick, preferred_element_type=jnp.float32)
        swapped = plain.reshape(devices, 2, width, size)
        swapped = jnp.concatenate([swapped[:, 1:], swapped[:, :1]], axis=1).reshape(size, size)
        signed = jnp.where(row_part == 0, plain, -plain)
        full = jnp.where(lane_part == 0, signed, swapped)
        inside = row // (slab * 2**level) == lane // (slab * 2**level)
        return jnp.where(inside, full, 0.0).astype(jnp.bfloat16)

    inverse, lower = [None], [None]
    for level in range(1, depth + 1):
        inverse.append(front_matrix(raw[level][:, size:], pick_ref[level - 1], level))
        if level < depth:
            lower.append(front_matrix(raw[level][:, :size], pick_ref[depth + level - 1], level))

    arriving = side(0)
    partial = [None]
    for level in range(1, depth + 1):
        level_z = (side(level) - arriving).astype(jnp.bfloat16)
        partial.append(jnp.dot(level_z, inverse[level], preferred_element_type=jnp.float32))
        if level < depth:
            arriving = jnp.dot(level_z, lower[level], preferred_element_type=jnp.float32)

    sign = jnp.where((lane_row // width) % 2 == 0, 1.0, -1.0)
    solved = list(partial)
    for level in range(depth - 1, 0, -1):
        parent = (solved[level + 1] * sign).astype(jnp.bfloat16)
        product = lax.dot_general(parent, lower[level], back, preferred_element_type=jnp.float32)
        solved[level] = partial[level] - product * sign

    leaf_rows = leaf_w_ref.shape[2]
    product = jnp.dot(
        solved[1].astype(jnp.bfloat16), panel_ref[...], preferred_element_type=jnp.float32
    )
    for part in range(2):
        leaf_out_ref[part] = leaf_w_ref[part] - product[:, part * leaf_rows : (part + 1) * leaf_rows]

    stacked = jnp.concatenate(
        solved[1:] + [jnp.zeros((size - depth * columns, size), jnp.float32)], axis=0
    )
    turn_ref[...] = stacked.T
    for level in range(1, depth + 1):
        place = jnp.int32(0)
        for block in range(devices):
            place = jnp.where(owner(level, block) == device, block, place)
        block_rows = turn_ref[pl.ds(pl.multiple_of(place * slab, slab), slab), :]
        for part in range(2):
            sep_out_ref[part, level - 1] = block_rows[
                part * width : (part + 1) * width, (level - 1) * columns : level * columns
            ]


def whole(space):
    return pl.BlockSpec(memory_space=space)


def body(leaf_rhs, sep_rhs, leaf_inv, leaf_low, sep_inv, sep_low, leaf_live, targets):
    devices, parts = lax.axis_size("leaf"), lax.axis_size("rhs")
    columns, leaf_rows = leaf_rhs.shape[1:]
    width, depth = sep_inv.shape[1], sep_rhs.shape[2]
    slab = 2 * width
    size = devices * slab
    small_tree = (
        size == 128 and (1 + depth) * columns + sep_low.shape[2] <= 128 and sep_inv.shape[2] <= 128
    )
    panel = leaf_low.transpose(0, 2, 1)
    tree_rhs = sep_rhs.transpose(0, 2, 3, 1)

    def leaf_w_of(leaf_z, pieces):
        return pl.pallas_call(
            functools.partial(leaf_kernel, parts),
            out_shape=pltpu.VMEM((2, columns, leaf_rows), jnp.float32),
            in_specs=[whole(SMEM)] + [whole(VMEM)] * (1 + parts),
            out_specs=whole(VMEM),
            cost_estimate=pl.CostEstimate(
                flops=8 * columns * leaf_rows * leaf_rows,
                bytes_accessed=4 * leaf_rows * leaf_rows,
                transcendentals=0,
            ),
        )(leaf_live, *[in_vmem(ready) for ready in [leaf_z] + pieces])

    if not small_tree:
        live_mask = (jnp.arange(leaf_rows) < leaf_live[0] * 128).astype(jnp.float32)
        leaf_z = (leaf_rhs * live_mask).astype(jnp.bfloat16).reshape(2 * columns, leaf_rows)
        leaf_w = leaf_w_of(leaf_z, gather_pieces(leaf_inv))
        return level_by_level(leaf_rhs, sep_rhs, leaf_w, leaf_low, sep_inv, sep_low, leaf_live, targets)

    tree_parts = (leaf_rhs, panel, tree_rhs, sep_inv, sep_low)
    first = pl.pallas_call(
        first_kernel,
        out_shape=pltpu.VMEM((8, 128), jnp.float32),
        out_specs=whole(VMEM),
        cost_estimate=pl.CostEstimate(flops=10**9, bytes_accessed=0, transcendentals=0),
    )()
    held, leaf_z = pl.pallas_call(
        pack_kernel,
        out_shape=(
            pltpu.VMEM((slab, 2 * size), jnp.bfloat16),
            pltpu.VMEM((2 * columns, leaf_rows), jnp.bfloat16),
        ),
        in_specs=[whole(SMEM)] + [whole(VMEM)] * 6,
        out_specs=(whole(VMEM),) * 2,
    )(leaf_live, *[in_vmem(part) for part in (first,) + tree_parts])

    def join(own, other, flops):
        return pl.pallas_call(
            join_kernel,
            out_shape=pltpu.VMEM((2 * own.shape[0], own.shape[1]), own.dtype),
            in_specs=[whole(VMEM)] * 2,
            out_specs=whole(VMEM),
            cost_estimate=pl.CostEstimate(
                flops=flops, bytes_accessed=0, transcendentals=0
            ),
        )(in_vmem(own), in_vmem(other))

    rounds = [held]
    offset = 1
    while offset < devices:
        rounds.append(xor_permute(held, "leaf", offset))
        offset *= 2
        if offset < devices:
            held = join(held, rounds[-1], 10**11 if offset == 2 else 0)

    panel_rows, picks, kept_targets = pl.pallas_call(
        functools.partial(prepare_kernel, (1 + depth) * columns),
        out_shape=(
            pltpu.VMEM((size, 2 * leaf_rows), jnp.bfloat16),
            pltpu.VMEM((2 * depth - 1, size, size), jnp.bfloat16),
            pltpu.SMEM(targets.shape, jnp.int32),
        ),
        in_specs=[whole(SMEM), whole(SMEM), whole(VMEM), whole(VMEM)],
        out_specs=(whole(VMEM),) * 2 + (whole(SMEM),),
        cost_estimate=pl.CostEstimate(flops=10**11, bytes_accessed=0, transcendentals=0),
    )(leaf_live, targets, panel, in_vmem(held))

    def hold(piece):
        return pl.pallas_call(
            hold_kernel,
            out_shape=pltpu.VMEM(piece.shape, piece.dtype),
            in_specs=[whole(VMEM)] * 2,
            out_specs=whole(VMEM),
            input_output_aliases={0: 0},
        )(in_vmem(piece), in_vmem(held))

    leaf_w = leaf_w_of(leaf_z, gather_pieces(leaf_inv, hold))
    leaf_x, sep_x = pl.pallas_call(
        tree_kernel,
        out_shape=(
            jax.ShapeDtypeStruct((2, columns, leaf_rows), jnp.float32),
            jax.ShapeDtypeStruct((2, depth, width, columns), jnp.float32),
        ),
        in_specs=[whole(SMEM)] + [whole(VMEM)] * 5,
        out_specs=(whole(VMEM), whole(VMEM)),
        scratch_shapes=[
            pltpu.VMEM((size, 2 * size), jnp.bfloat16),
            pltpu.VMEM((size, size), jnp.float32),
        ],
    )(
        pltpu.with_memory_space_constraint(kept_targets, SMEM),
        *[in_vmem(ready) for ready in (held, rounds[-1], leaf_w, panel_rows, picks)],
    )
    return leaf_x, sep_x.transpose(0, 3, 1, 2)


def solution(mesh):
    placed = (
        P(None, "rhs", "leaf"),
        P(None, "rhs", None, "leaf"),
        P(None, "rhs", "leaf"),
        P(None, None, "leaf"),
        P(None, None, "leaf"),
        P(None, None, "leaf"),
        P("leaf"),
        P(),
    )
    return jax.shard_map(
        body,
        mesh=mesh,
        in_specs=placed,
        out_specs=(P(None, "rhs", "leaf"), P(None, "rhs", None, "leaf")),
        check_vma=False,
    )
```

```python
import functools

import jax
import jax.numpy as jnp
from jax import lax
from jax.experimental import pallas as pl
from jax.experimental.pallas import tpu as pltpu
from jax.sharding import PartitionSpec as P

exact_mode = lax.Precision.HIGHEST
VMEM = pltpu.MemorySpace.VMEM
SMEM = pltpu.MemorySpace.SMEM


def complex_dot(operand, factor):
    row_count = operand.shape[1]
    stacked = jnp.concatenate([operand[0], operand[1]], axis=0)
    real_acc = jnp.dot(stacked, factor[0], preferred_element_type=jnp.float32)
    imag_acc = jnp.dot(stacked, factor[1], preferred_element_type=jnp.float32)
    return jnp.stack(
        [real_acc[:row_count] - imag_acc[row_count:], imag_acc[:row_count] + real_acc[row_count:]]
    )


def complex_dot_back(operand, factor):
    row_count = operand.shape[1]
    stacked = jnp.concatenate([operand[0], operand[1]], axis=0)
    contract = (((1,), (1,)), ((), ()))
    real_acc = lax.dot_general(stacked, factor[0], contract, preferred_element_type=jnp.float32)
    imag_acc = lax.dot_general(stacked, factor[1], contract, preferred_element_type=jnp.float32)
    return jnp.stack(
        [real_acc[:row_count] - imag_acc[row_count:], imag_acc[:row_count] + real_acc[row_count:]]
    )


def to_blocks(values_in, group_size):
    return (
        values_in.reshape(2, values_in.shape[1], group_size, -1)
        .transpose(2, 0, 1, 3)
        .reshape(group_size, -1)
    )


def from_blocks(blocks, columns):
    group_size = blocks.shape[0]
    return blocks.reshape(group_size, 2, columns, -1).transpose(1, 2, 0, 3).reshape(2, columns, -1)


def selector(dest_index, total_slots):
    return (dest_index[:, None] == jnp.arange(total_slots, dtype=jnp.int32)[None, :]).astype(
        jnp.float32
    )


def exchange_sum(blocks, global_dest, devices):
    routed = jnp.dot(selector(global_dest, devices).T, blocks, precision=exact_mode)
    received = lax.all_to_all(
        routed.astype(jnp.bfloat16), "leaf", split_axis=0, concat_axis=0, tiled=True
    ).astype(routed.dtype)
    return jnp.sum(received, axis=0)


def collect(blocks, local_dest, level_bits, device, devices):
    group_start = device >> level_bits << level_bits
    return exchange_sum(blocks, group_start + local_dest, devices)


def spread(own_block, level_bits, device, devices):
    group_size = 2**level_bits
    group_start = device >> level_bits << level_bits
    slot_index = jnp.arange(devices, dtype=jnp.int32)[:, None]
    inside = (slot_index >= group_start) & (slot_index < group_start + group_size)
    routed = jnp.where(inside, own_block[None, :], jnp.zeros_like(own_block)[None, :])
    received = lax.all_to_all(routed, "leaf", split_axis=0, concat_axis=0, tiled=True)
    return lax.dynamic_slice_in_dim(received, group_start, group_size, 0)


def level_by_level(leaf_rhs, sep_rhs, leaf_w, leaf_low, sep_inv, sep_low, leaf_live, targets):
    devices = lax.axis_size("leaf")
    tree_depth = devices.bit_length() - 1
    device = lax.axis_index("leaf")
    leaf_rows = leaf_low.shape[1]
    sep_width = sep_inv.shape[1]
    columns = leaf_rhs.shape[1]
    live_mask = (jnp.arange(leaf_rows) < leaf_live[0] * 128).astype(jnp.float32)
    leaf_z = (leaf_rhs * live_mask).astype(jnp.bfloat16)
    first_dest = lax.dynamic_slice_in_dim(targets[0], device, 1)
    arriving = collect(complex_dot(leaf_z, leaf_low).reshape(1, -1), first_dest, 1, device, devices)
    solved_w = []
    for level_now in range(1, tree_depth + 1):
        group_size = 2**level_now
        offset = sep_width * (group_size - 2)
        level_z = (
            sep_rhs[:, :, level_now - 1, :] - arriving.reshape(2, columns, sep_width)
        ).astype(jnp.bfloat16)
        inv_rows = sep_inv[:, :, offset : offset + sep_width * group_size]
        own_w = collect(
            to_blocks(complex_dot(level_z, inv_rows), group_size),
            jnp.arange(group_size, dtype=jnp.int32),
            level_now,
            device,
            devices,
        )
        solved_w.append(own_w.reshape(2, columns, sep_width))
        if level_now < tree_depth:
            low_rows = sep_low[:, :, offset : offset + sep_width * group_size]
            group_start = device >> level_now << level_now
            dest_index = lax.dynamic_slice_in_dim(targets[level_now], group_start, group_size)
            arriving = collect(
                to_blocks(complex_dot(level_z, low_rows), group_size),
                dest_index,
                level_now + 1,
                device,
                devices,
            )
    solved_x = [solved_w[level_now] for level_now in range(tree_depth)]
    for level_now in range(tree_depth - 1, 0, -1):
        group_size = 2**level_now
        offset = sep_width * (group_size - 2)
        low_rows = sep_low[:, :, offset : offset + sep_width * group_size]
        parent_x = spread(
            solved_x[level_now].astype(jnp.bfloat16).reshape(-1), level_now + 1, device, devices
        )
        group_start = device >> level_now << level_now
        dest_index = lax.dynamic_slice_in_dim(targets[level_now], group_start, group_size)
        picked = jnp.dot(
            selector(dest_index, 2 * group_size).astype(jnp.bfloat16),
            parent_x,
            preferred_element_type=jnp.float32,
        ).astype(jnp.bfloat16)
        solved_x[level_now - 1] = solved_w[level_now - 1] - complex_dot_back(
            from_blocks(picked, columns), low_rows
        )
    parent_x = spread(solved_x[0].astype(jnp.bfloat16).reshape(-1), 1, device, devices)
    picked = jnp.dot(
        selector(first_dest, 2).astype(jnp.bfloat16), parent_x, preferred_element_type=jnp.float32
    ).astype(jnp.bfloat16)
    leaf_x = (
        leaf_w - complex_dot_back(picked.reshape(2, columns, sep_width), leaf_low)
    ) * live_mask
    return leaf_x, jnp.stack(solved_x, axis=2)


def xor_permute(values_in, axis, offset):
    count = lax.axis_size(axis)
    return lax.ppermute(values_in, axis, [(source, source ^ offset) for source in range(count)])


def in_vmem(values_in):
    return pltpu.with_memory_space_constraint(values_in, VMEM)


def masked_rows(leaf_rhs, live_ref):
    rows = leaf_rhs.shape[2]
    live = lax.broadcasted_iota(jnp.int32, (1, rows), 1) < live_ref[0] * 128
    stacked = jnp.concatenate([leaf_rhs[0], leaf_rhs[1]], axis=0)
    return jnp.where(live, stacked, 0.0).astype(jnp.bfloat16), live


def first_kernel(out_ref):
    out_ref[...] = jnp.zeros_like(out_ref)


def pack_kernel(live_ref, _, leaf_rhs_ref, low_ref, rhs_ref, inv_ref, sep_low_ref, out_ref, tile_ref, z_ref):
    columns = leaf_rhs_ref.shape[1]
    depth = rhs_ref.shape[1]
    leaf_z, _ = masked_rows(leaf_rhs_ref[...], live_ref)
    z_ref[...] = leaf_z
    panel = jnp.concatenate([low_ref[0], low_ref[1]], axis=0)
    product = lax.dot_general(
        panel, leaf_z, (((1,), (1,)), ((), ())), preferred_element_type=jnp.float32
    )
    width = low_ref.shape[1]
    update = [
        product[:width, :columns] - product[width:, columns:],
        product[width:, :columns] + product[:width, columns:],
    ]
    used = (1 + depth) * columns + sep_low_ref.shape[2]
    halves = []
    for part in range(2):
        pieces = [update[part]] + [rhs_ref[part, level] for level in range(depth)]
        pieces.append(sep_low_ref[part].astype(jnp.float32))
        if used < 128:
            pieces.append(jnp.zeros((width, 128 - used), jnp.float32))
        pieces.append(inv_ref[part].astype(jnp.float32))
        if inv_ref.shape[2] < 128:
            pieces.append(jnp.zeros((width, 128 - inv_ref.shape[2]), jnp.float32))
        halves.append(jnp.concatenate(pieces, axis=1))
    packed = jnp.concatenate(halves, axis=0).astype(jnp.bfloat16)
    out_ref[...] = packed
    tile_ref[...] = packed[:, : tile_ref.shape[1]]


def piece_product(step, z_ref, piece_ref):
    columns = z_ref.shape[0] // 2
    depth = piece_ref.shape[1]
    owner = lax.axis_index("rhs") ^ step
    rows = z_ref[:, pl.ds(pl.multiple_of(owner * depth, 128), depth)]
    real_acc = jnp.dot(rows, piece_ref[0], preferred_element_type=jnp.float32)
    imag_acc = jnp.dot(rows, piece_ref[1], preferred_element_type=jnp.float32)
    return real_acc[:columns] - imag_acc[columns:], imag_acc[:columns] + real_acc[columns:]


def leaf_kernel(steps, z_ref, *refs):
    out_ref = refs[-1]
    products = [piece_product(step, z_ref, piece_ref) for step, piece_ref in zip(steps, refs[:-1])]
    for part in range(2):
        out_ref[part] = sum(product[part] for product in products)


def prepare_kernel(low_start, live_ref, targets_ref, low_ref, _, panel_ref, pick_ref, kept_ref):
    for level in range(targets_ref.shape[0]):
        for block in range(targets_ref.shape[1]):
            kept_ref[level, block] = targets_ref[level, block]
    depth, devices = targets_ref.shape
    width, leaf_rows = low_ref.shape[1:]
    slab = 2 * width
    device = lax.axis_index("leaf")
    live = lax.broadcasted_iota(jnp.int32, (1, leaf_rows), 1) < live_ref[0] * 128
    low = [jnp.where(live, low_ref[part].astype(jnp.float32), 0.0) for part in range(2)]
    rows = jnp.concatenate(
        [
            jnp.concatenate([low[0], low[1]], axis=1),
            jnp.concatenate([-low[1], low[0]], axis=1),
        ],
        axis=0,
    ).astype(jnp.bfloat16)
    panel_ref[...] = jnp.zeros_like(panel_ref)
    panel_ref[pl.ds(pl.multiple_of(device * slab, slab), slab), :] = rows
    size = devices * slab
    row = lax.broadcasted_iota(jnp.int32, (size, size), 0)
    lane_row = lax.broadcasted_iota(jnp.int32, (1, size), 1)
    for level in range(1, depth + 1):
        offset = width * (2**level - 2) + lane_row % width
        target_lane = jnp.zeros((1, size), jnp.int32)
        for block in range(devices):
            target_lane = jnp.where(lane_row // slab == block, targets_ref[level - 1, block], target_lane)
        pick_ref[level - 1] = jnp.where(row == offset + target_lane * width, 1.0, 0.0).astype(jnp.bfloat16)
        if level < depth:
            own_lane = (lane_row // slab) % 2**level
            pick_ref[depth + level - 1] = jnp.where(
                row == low_start + offset + own_lane * width, 1.0, 0.0
            ).astype(jnp.bfloat16)


def join_first_kernel(own_ref, received_ref, pair_ref, out_ref, tile_ref):
    rows, lanes = own_ref.shape
    tile = pair_ref.shape[1]
    out_ref[:rows, :lanes] = own_ref[...]
    out_ref[rows:, :lanes] = received_ref[...]
    out_ref[:rows, lanes:] = pair_ref[...]
    out_ref[rows:, lanes:] = pair_ref[...]
    tile_ref[...] = received_ref[:, :tile]


def join_second_kernel(side_lanes, own_ref, first_ref, pair_ref, second_ref, _, out_ref):
    rows, lanes = own_ref.shape
    tile = pair_ref.shape[1]
    out_ref[:rows, :] = own_ref[...]
    out_ref[rows : 2 * rows, :tile] = pair_ref[...]
    out_ref[rows : 2 * rows, tile:] = first_ref[:, tile:]
    lane = lax.broadcasted_iota(jnp.int32, (rows, tile), 1)
    merged = jnp.where(
        lane < side_lanes,
        second_ref[:rows, lanes:].astype(jnp.float32),
        second_ref[:rows, :tile].astype(jnp.float32),
    )
    out_ref[2 * rows : 3 * rows, :tile] = merged.astype(jnp.bfloat16)
    out_ref[2 * rows : 3 * rows, tile:] = second_ref[:rows, tile:lanes]
    out_ref[3 * rows :, :] = second_ref[rows:, :lanes]


def hold_kernel(piece_ref, _, out_ref):
    out_ref[...] = piece_ref[...]


def tree_kernel(
    targets_ref, near_ref, far_ref, pick_ref, _, parent_ref, sep_out_ref, all_ref, turn_ref
):
    depth, devices = targets_ref.shape
    columns, size = parent_ref.shape
    slab = size // devices
    width = slab // 2
    device = lax.axis_index("leaf")
    row = lax.broadcasted_iota(jnp.int32, (size, size), 0)
    lane = lax.broadcasted_iota(jnp.int32, (size, size), 1)
    lane_row = lax.broadcasted_iota(jnp.int32, (1, size), 1)
    row_part, lane_part = (row // width) % 2, (lane // width) % 2
    all_ref[: size // 2, :] = near_ref[...]
    all_ref[size // 2 :, :] = far_ref[...]

    def owner(level, block):
        if level == 0:
            return jnp.int32(block)
        group = 2**level
        return block // group * group + targets_ref[level - 1, block]

    def rows_of(level):
        return jnp.concatenate(
            [
                all_ref[pl.ds(pl.multiple_of((owner(level, block) ^ device) * slab, slab), slab), :]
                for block in range(devices)
            ],
            axis=0,
        )

    raw = [rows_of(level) for level in range(depth + 1)]
    pick_row = lax.broadcasted_iota(jnp.int32, (columns, size), 0)
    pick_lane = lax.broadcasted_iota(jnp.int32, (columns, size), 1)
    back = (((1,), (1,)), ((), ()))

    def side(level):
        pick = jnp.where(pick_lane == pick_row + level * columns, 1.0, 0.0).astype(jnp.bfloat16)
        return lax.dot_general(pick, raw[level][:, :size], back, preferred_element_type=jnp.float32)

    def front_matrix(source, pick, level):
        plain = jnp.dot(source, pick, preferred_element_type=jnp.float32)
        swapped = plain.reshape(devices, 2, width, size)
        swapped = jnp.concatenate([swapped[:, 1:], swapped[:, :1]], axis=1).reshape(size, size)
        signed = jnp.where(row_part == 0, plain, -plain)
        full = jnp.where(lane_part == 0, signed, swapped)
        inside = row // (slab * 2**level) == lane // (slab * 2**level)
        return jnp.where(inside, full, 0.0).astype(jnp.bfloat16)

    inverse, lower = [None], [None]
    for level in range(1, depth + 1):
        inverse.append(front_matrix(raw[level][:, size:], pick_ref[level - 1], level))
        if level < depth:
            lower.append(front_matrix(raw[level][:, :size], pick_ref[depth + level - 1], level))

    arriving = side(0)
    partial = [None]
    for level in range(1, depth + 1):
        level_z = (side(level) - arriving).astype(jnp.bfloat16)
        partial.append(jnp.dot(level_z, inverse[level], preferred_element_type=jnp.float32))
        if level < depth:
            arriving = jnp.dot(level_z, lower[level], preferred_element_type=jnp.float32)

    sign = jnp.where((lane_row // width) % 2 == 0, 1.0, -1.0)
    solved = list(partial)
    for level in range(depth - 1, 0, -1):
        parent = (solved[level + 1] * sign).astype(jnp.bfloat16)
        product = lax.dot_general(parent, lower[level], back, preferred_element_type=jnp.float32)
        solved[level] = partial[level] - product * sign

    parent_ref[...] = solved[1].astype(jnp.bfloat16)
    stacked = jnp.concatenate(
        solved[1:] + [jnp.zeros((size - depth * columns, size), jnp.float32)], axis=0
    )
    turn_ref[...] = stacked.T
    for level in range(1, depth + 1):
        place = jnp.int32(0)
        for block in range(devices):
            place = jnp.where(owner(level, block) == device, block, place)
        block_rows = turn_ref[pl.ds(pl.multiple_of(place * slab, slab), slab), :]
        for part in range(2):
            sep_out_ref[part, level - 1] = block_rows[
                part * width : (part + 1) * width, (level - 1) * columns : level * columns
            ]


def finish_kernel(steps, live_ref, z_ref, partial_ref, parent_ref, panel_ref, sep_ref, *refs):
    leaf_out_ref, sep_out_ref = refs[-2:]
    leaf_rows = leaf_out_ref.shape[2]
    live = lax.broadcasted_iota(jnp.int32, (1, leaf_rows), 1) < live_ref[0] * 128
    products = [piece_product(step, z_ref, piece_ref) for step, piece_ref in zip(steps, refs[:-2])]
    from_tree = jnp.dot(parent_ref[...], panel_ref[...], preferred_element_type=jnp.float32)
    for part in range(2):
        leaf_w = partial_ref[part] + sum(product[part] for product in products)
        leaf_out_ref[part] = (
            jnp.where(live, leaf_w, 0.0) - from_tree[:, part * leaf_rows : (part + 1) * leaf_rows]
        )
    sep_out_ref[...] = sep_ref[...]


def whole(space):
    return pl.BlockSpec(memory_space=space)


def body(leaf_rhs, sep_rhs, leaf_inv, leaf_low, sep_inv, sep_low, leaf_live, targets):
    devices, parts = lax.axis_size("leaf"), lax.axis_size("rhs")
    columns, leaf_rows = leaf_rhs.shape[1:]
    width, depth = sep_inv.shape[1], sep_rhs.shape[2]
    slab = 2 * width
    size = devices * slab
    small_tree = (
        devices == 8 and parts % 2 == 0 and size == 128 and (1 + depth) * columns + sep_low.shape[2] <= 128 and sep_inv.shape[2] <= 128
    )
    panel = leaf_low.transpose(0, 2, 1)
    tree_rhs = sep_rhs.transpose(0, 2, 3, 1)

    if not small_tree:
        live_mask = (jnp.arange(leaf_rows) < leaf_live[0] * 128).astype(jnp.float32)
        leaf_z = (leaf_rhs * live_mask).astype(jnp.bfloat16)
        leaf_w = complex_dot(leaf_z, lax.all_gather(leaf_inv, "rhs", axis=1, tiled=True)) * live_mask
        return level_by_level(leaf_rhs, sep_rhs, leaf_w, leaf_low, sep_inv, sep_low, leaf_live, targets)

    tree_parts = (leaf_rhs, panel, tree_rhs, sep_inv, sep_low)
    first = pl.pallas_call(
        first_kernel,
        out_shape=pltpu.VMEM((8, 128), jnp.float32),
        out_specs=whole(VMEM),
        cost_estimate=pl.CostEstimate(flops=10**9, bytes_accessed=0, transcendentals=0),
    )()
    held, own_tile, leaf_z = pl.pallas_call(
        pack_kernel,
        out_shape=(
            pltpu.VMEM((slab, 2 * size), jnp.bfloat16),
            pltpu.VMEM((slab, size), jnp.bfloat16),
            pltpu.VMEM((2 * columns, leaf_rows), jnp.bfloat16),
        ),
        in_specs=[whole(SMEM)] + [whole(VMEM)] * 6,
        out_specs=(whole(VMEM),) * 3,
    )(leaf_live, *[in_vmem(part) for part in (first,) + tree_parts])

    def exchange(values_in, offset, flip):
        partners = [
            (source * parts + part, (source ^ offset) * parts + (part ^ flip))
            for source in range(devices)
            for part in range(parts)
        ]
        return lax.ppermute(values_in, ("leaf", "rhs"), partners)

    first_round = exchange(held, 1, 1)
    pair_tile = xor_permute(own_tile, "rhs", 1)
    second_part, first_tile = pl.pallas_call(
        join_first_kernel,
        out_shape=(
            pltpu.VMEM((2 * slab, 3 * size), jnp.bfloat16),
            pltpu.VMEM((slab, size), jnp.bfloat16),
        ),
        in_specs=[whole(VMEM)] * 3,
        out_specs=(whole(VMEM),) * 2,
        cost_estimate=pl.CostEstimate(flops=10**11, bytes_accessed=0, transcendentals=0),
    )(in_vmem(held), in_vmem(first_round), in_vmem(pair_tile))
    second_round = exchange(second_part, 2, 1)
    panel_rows, picks, kept_targets = pl.pallas_call(
        functools.partial(prepare_kernel, (1 + depth) * columns),
        out_shape=(
            pltpu.VMEM((size, 2 * leaf_rows), jnp.bfloat16),
            pltpu.VMEM((2 * depth - 1, size, size), jnp.bfloat16),
            pltpu.SMEM(targets.shape, jnp.int32),
        ),
        in_specs=[whole(SMEM), whole(SMEM), whole(VMEM), whole(VMEM)],
        out_specs=(whole(VMEM),) * 2 + (whole(SMEM),),
        cost_estimate=pl.CostEstimate(flops=0, bytes_accessed=0, transcendentals=0),
    )(leaf_live, targets, panel, in_vmem(first_tile))

    pair_first = xor_permute(first_tile, "rhs", 1)
    held = pl.pallas_call(
        functools.partial(join_second_kernel, (1 + depth) * columns),
        out_shape=pltpu.VMEM((4 * slab, 2 * size), jnp.bfloat16),
        in_specs=[whole(VMEM)] * 5,
        out_specs=whole(VMEM),
        cost_estimate=pl.CostEstimate(flops=0, bytes_accessed=0, transcendentals=0),
    )(*[in_vmem(ready) for ready in (held, first_round, pair_first, second_round, picks)])
    far = exchange(held, 4, 0)

    def hold(piece):
        return pl.pallas_call(
            hold_kernel,
            out_shape=pltpu.VMEM(piece.shape, piece.dtype),
            in_specs=[whole(VMEM)] * 2,
            out_specs=whole(VMEM),
        )(in_vmem(piece), in_vmem(held))

    far_piece = hold(xor_permute(leaf_inv, "rhs", 3))
    partial = pl.pallas_call(
        functools.partial(leaf_kernel, (0, 3)),
        out_shape=pltpu.VMEM((2, columns, leaf_rows), jnp.float32),
        in_specs=[whole(VMEM)] * 3,
        out_specs=whole(VMEM),
        cost_estimate=pl.CostEstimate(flops=0, bytes_accessed=0, transcendentals=0),
    )(*[in_vmem(ready) for ready in (leaf_z, leaf_inv, far_piece)])
    parent_x, tree_sep = pl.pallas_call(
        tree_kernel,
        out_shape=(
            pltpu.VMEM((columns, size), jnp.bfloat16),
            pltpu.VMEM((2, depth, width, columns), jnp.float32),
        ),
        in_specs=[whole(SMEM)] + [whole(VMEM)] * 4,
        out_specs=(whole(VMEM),) * 2,
        scratch_shapes=[
            pltpu.VMEM((size, 2 * size), jnp.bfloat16),
            pltpu.VMEM((size, size), jnp.float32),
        ],
        cost_estimate=pl.CostEstimate(flops=3*10**9, bytes_accessed=0, transcendentals=0),
    )(
        pltpu.with_memory_space_constraint(kept_targets, SMEM),
        *[in_vmem(ready) for ready in (held, far, picks, partial)],
    )
    pair_pieces = (xor_permute(leaf_inv, "rhs", 1), xor_permute(far_piece, "rhs", 1))
    leaf_x, sep_x = pl.pallas_call(
        functools.partial(finish_kernel, (1, 2)),
        out_shape=(
            jax.ShapeDtypeStruct((2, columns, leaf_rows), jnp.float32),
            jax.ShapeDtypeStruct((2, depth, width, columns), jnp.float32),
        ),
        in_specs=[whole(SMEM)] + [whole(VMEM)] * 7,
        out_specs=(whole(VMEM),) * 2,
    )(
        leaf_live,
        *[in_vmem(ready) for ready in (leaf_z, partial, parent_x, panel_rows, tree_sep) + pair_pieces],
    )
    return leaf_x, sep_x.transpose(0, 3, 1, 2)


def solution(mesh):
    placed = (
        P(None, "rhs", "leaf"),
        P(None, "rhs", None, "leaf"),
        P(None, "rhs", "leaf"),
        P(None, None, "leaf"),
        P(None, None, "leaf"),
        P(None, None, "leaf"),
        P("leaf"),
        P(),
    )
    return jax.shard_map(
        body,
        mesh=mesh,
        in_specs=placed,
        out_specs=(P(None, "rhs", "leaf"), P(None, "rhs", None, "leaf")),
        check_vma=False,
    )
```

```python
import functools

import jax
import jax.numpy as jnp
from jax import lax
from jax.experimental import pallas as pl
from jax.experimental.pallas import tpu as pltpu
from jax.sharding import PartitionSpec as P

exact_mode = lax.Precision.HIGHEST
VMEM = pltpu.MemorySpace.VMEM
SMEM = pltpu.MemorySpace.SMEM


def complex_dot(operand, factor):
    row_count = operand.shape[1]
    stacked = jnp.concatenate([operand[0], operand[1]], axis=0)
    real_acc = jnp.dot(stacked, factor[0], preferred_element_type=jnp.float32)
    imag_acc = jnp.dot(stacked, factor[1], preferred_element_type=jnp.float32)
    return jnp.stack(
        [real_acc[:row_count] - imag_acc[row_count:], imag_acc[:row_count] + real_acc[row_count:]]
    )


def complex_dot_back(operand, factor):
    row_count = operand.shape[1]
    stacked = jnp.concatenate([operand[0], operand[1]], axis=0)
    contract = (((1,), (1,)), ((), ()))
    real_acc = lax.dot_general(stacked, factor[0], contract, preferred_element_type=jnp.float32)
    imag_acc = lax.dot_general(stacked, factor[1], contract, preferred_element_type=jnp.float32)
    return jnp.stack(
        [real_acc[:row_count] - imag_acc[row_count:], imag_acc[:row_count] + real_acc[row_count:]]
    )


def to_blocks(values_in, group_size):
    return (
        values_in.reshape(2, values_in.shape[1], group_size, -1)
        .transpose(2, 0, 1, 3)
        .reshape(group_size, -1)
    )


def from_blocks(blocks, columns):
    group_size = blocks.shape[0]
    return blocks.reshape(group_size, 2, columns, -1).transpose(1, 2, 0, 3).reshape(2, columns, -1)


def selector(dest_index, total_slots):
    return (dest_index[:, None] == jnp.arange(total_slots, dtype=jnp.int32)[None, :]).astype(
        jnp.float32
    )


def exchange_sum(blocks, global_dest, devices):
    routed = jnp.dot(selector(global_dest, devices).T, blocks, precision=exact_mode)
    received = lax.all_to_all(
        routed.astype(jnp.bfloat16), "leaf", split_axis=0, concat_axis=0, tiled=True
    ).astype(routed.dtype)
    return jnp.sum(received, axis=0)


def collect(blocks, local_dest, level_bits, device, devices):
    group_start = device >> level_bits << level_bits
    return exchange_sum(blocks, group_start + local_dest, devices)


def spread(own_block, level_bits, device, devices):
    group_size = 2**level_bits
    group_start = device >> level_bits << level_bits
    slot_index = jnp.arange(devices, dtype=jnp.int32)[:, None]
    inside = (slot_index >= group_start) & (slot_index < group_start + group_size)
    routed = jnp.where(inside, own_block[None, :], jnp.zeros_like(own_block)[None, :])
    received = lax.all_to_all(routed, "leaf", split_axis=0, concat_axis=0, tiled=True)
    return lax.dynamic_slice_in_dim(received, group_start, group_size, 0)


def level_by_level(leaf_rhs, sep_rhs, leaf_w, leaf_low, sep_inv, sep_low, leaf_live, targets):
    devices = lax.axis_size("leaf")
    tree_depth = devices.bit_length() - 1
    device = lax.axis_index("leaf")
    leaf_rows = leaf_low.shape[1]
    sep_width = sep_inv.shape[1]
    columns = leaf_rhs.shape[1]
    live_mask = (jnp.arange(leaf_rows) < leaf_live[0] * 128).astype(jnp.float32)
    leaf_z = (leaf_rhs * live_mask).astype(jnp.bfloat16)
    first_dest = lax.dynamic_slice_in_dim(targets[0], device, 1)
    arriving = collect(complex_dot(leaf_z, leaf_low).reshape(1, -1), first_dest, 1, device, devices)
    solved_w = []
    for level_now in range(1, tree_depth + 1):
        group_size = 2**level_now
        offset = sep_width * (group_size - 2)
        level_z = (
            sep_rhs[:, :, level_now - 1, :] - arriving.reshape(2, columns, sep_width)
        ).astype(jnp.bfloat16)
        inv_rows = sep_inv[:, :, offset : offset + sep_width * group_size]
        own_w = collect(
            to_blocks(complex_dot(level_z, inv_rows), group_size),
            jnp.arange(group_size, dtype=jnp.int32),
            level_now,
            device,
            devices,
        )
        solved_w.append(own_w.reshape(2, columns, sep_width))
        if level_now < tree_depth:
            low_rows = sep_low[:, :, offset : offset + sep_width * group_size]
            group_start = device >> level_now << level_now
            dest_index = lax.dynamic_slice_in_dim(targets[level_now], group_start, group_size)
            arriving = collect(
                to_blocks(complex_dot(level_z, low_rows), group_size),
                dest_index,
                level_now + 1,
                device,
                devices,
            )
    solved_x = [solved_w[level_now] for level_now in range(tree_depth)]
    for level_now in range(tree_depth - 1, 0, -1):
        group_size = 2**level_now
        offset = sep_width * (group_size - 2)
        low_rows = sep_low[:, :, offset : offset + sep_width * group_size]
        parent_x = spread(
            solved_x[level_now].astype(jnp.bfloat16).reshape(-1), level_now + 1, device, devices
        )
        group_start = device >> level_now << level_now
        dest_index = lax.dynamic_slice_in_dim(targets[level_now], group_start, group_size)
        picked = jnp.dot(
            selector(dest_index, 2 * group_size).astype(jnp.bfloat16),
            parent_x,
            preferred_element_type=jnp.float32,
        ).astype(jnp.bfloat16)
        solved_x[level_now - 1] = solved_w[level_now - 1] - complex_dot_back(
            from_blocks(picked, columns), low_rows
        )
    parent_x = spread(solved_x[0].astype(jnp.bfloat16).reshape(-1), 1, device, devices)
    picked = jnp.dot(
        selector(first_dest, 2).astype(jnp.bfloat16), parent_x, preferred_element_type=jnp.float32
    ).astype(jnp.bfloat16)
    leaf_x = (
        leaf_w - complex_dot_back(picked.reshape(2, columns, sep_width), leaf_low)
    ) * live_mask
    return leaf_x, jnp.stack(solved_x, axis=2)


def xor_permute(values_in, axis, offset):
    count = lax.axis_size(axis)
    return lax.ppermute(values_in, axis, [(source, source ^ offset) for source in range(count)])


def in_vmem(values_in):
    return pltpu.with_memory_space_constraint(values_in, VMEM)


def masked_rows(leaf_rhs, live_ref):
    rows = leaf_rhs.shape[2]
    live = lax.broadcasted_iota(jnp.int32, (1, rows), 1) < live_ref[0] * 128
    stacked = jnp.concatenate([leaf_rhs[0], leaf_rhs[1]], axis=0)
    return jnp.where(live, stacked, 0.0).astype(jnp.bfloat16), live


def first_kernel(out_ref):
    out_ref[...] = jnp.zeros_like(out_ref)


def pack_kernel(live_ref, _, leaf_rhs_ref, low_ref, rhs_ref, inv_ref, sep_low_ref, out_ref, tile_ref, z_ref):
    columns = leaf_rhs_ref.shape[1]
    depth = rhs_ref.shape[1]
    leaf_z, _ = masked_rows(leaf_rhs_ref[...], live_ref)
    z_ref[...] = leaf_z
    panel = jnp.concatenate([low_ref[0], low_ref[1]], axis=0)
    product = lax.dot_general(
        panel, leaf_z, (((1,), (1,)), ((), ())), preferred_element_type=jnp.float32
    )
    width = low_ref.shape[1]
    update = [
        product[:width, :columns] - product[width:, columns:],
        product[width:, :columns] + product[:width, columns:],
    ]
    used = (1 + depth) * columns + sep_low_ref.shape[2]
    halves = []
    for part in range(2):
        pieces = [update[part]] + [rhs_ref[part, level] for level in range(depth)]
        pieces.append(sep_low_ref[part].astype(jnp.float32))
        if used < 128:
            pieces.append(jnp.zeros((width, 128 - used), jnp.float32))
        pieces.append(inv_ref[part].astype(jnp.float32))
        if inv_ref.shape[2] < 128:
            pieces.append(jnp.zeros((width, 128 - inv_ref.shape[2]), jnp.float32))
        halves.append(jnp.concatenate(pieces, axis=1))
    packed = jnp.concatenate(halves, axis=0).astype(jnp.bfloat16)
    out_ref[...] = packed
    tile_ref[...] = packed[:, : tile_ref.shape[1]]


def piece_product(step, z_ref, piece_ref):
    columns = z_ref.shape[0] // 2
    depth = piece_ref.shape[1]
    owner = lax.axis_index("rhs") ^ step
    rows = z_ref[:, pl.ds(pl.multiple_of(owner * depth, 128), depth)]
    real_acc = jnp.dot(rows, piece_ref[0], preferred_element_type=jnp.float32)
    imag_acc = jnp.dot(rows, piece_ref[1], preferred_element_type=jnp.float32)
    return real_acc[:columns] - imag_acc[columns:], imag_acc[:columns] + real_acc[columns:]


def leaf_kernel(steps, z_ref, *refs):
    out_ref = refs[-1]
    products = [piece_product(step, z_ref, piece_ref) for step, piece_ref in zip(steps, refs[:-1])]
    for part in range(2):
        out_ref[part] = sum(product[part] for product in products)


def prepare_kernel(low_start, live_ref, targets_ref, low_ref, _, panel_ref, pick_ref, kept_ref):
    for level in range(targets_ref.shape[0]):
        for block in range(targets_ref.shape[1]):
            kept_ref[level, block] = targets_ref[level, block]
    depth, devices = targets_ref.shape
    width, leaf_rows = low_ref.shape[1:]
    slab = 2 * width
    device = lax.axis_index("leaf")
    live = lax.broadcasted_iota(jnp.int32, (1, leaf_rows), 1) < live_ref[0] * 128
    low = [jnp.where(live, low_ref[part].astype(jnp.float32), 0.0) for part in range(2)]
    rows = jnp.concatenate(
        [
            jnp.concatenate([low[0], low[1]], axis=1),
            jnp.concatenate([low[1], -low[0]], axis=1),
        ],
        axis=0,
    ).astype(jnp.bfloat16)
    panel_ref[...] = jnp.zeros_like(panel_ref)
    panel_ref[pl.ds(pl.multiple_of(device * slab, slab), slab), :] = rows
    size = devices * slab
    row = lax.broadcasted_iota(jnp.int32, (size, size), 0)
    lane_row = lax.broadcasted_iota(jnp.int32, (1, size), 1)
    for level in range(1, depth + 1):
        offset = width * (2**level - 2) + lane_row % width
        target_lane = jnp.zeros((1, size), jnp.int32)
        for block in range(devices):
            target_lane = jnp.where(lane_row // slab == block, targets_ref[level - 1, block], target_lane)
        pick_ref[level - 1] = jnp.where(row == offset + target_lane * width, 1.0, 0.0).astype(jnp.bfloat16)
        if level < depth:
            own_lane = (lane_row // slab) % 2**level
            pick_ref[depth + level - 1] = jnp.where(
                row == low_start + offset + own_lane * width, 1.0, 0.0
            ).astype(jnp.bfloat16)


def join_first_kernel(own_ref, received_ref, pair_ref, out_ref, tile_ref):
    rows, lanes = own_ref.shape
    tile = pair_ref.shape[1]
    out_ref[:rows, :lanes] = own_ref[...]
    out_ref[rows:, :lanes] = received_ref[...]
    out_ref[:rows, lanes:] = pair_ref[...]
    out_ref[rows:, lanes:] = pair_ref[...]
    tile_ref[...] = received_ref[:, :tile]


def join_second_kernel(side_lanes, own_ref, first_ref, pair_ref, second_ref, _, out_ref):
    rows, lanes = own_ref.shape
    tile = pair_ref.shape[1]
    out_ref[:rows, :] = own_ref[...]
    out_ref[rows : 2 * rows, :tile] = pair_ref[...]
    out_ref[rows : 2 * rows, tile:] = first_ref[:, tile:]
    lane = lax.broadcasted_iota(jnp.int32, (rows, tile), 1)
    merged = jnp.where(
        lane < side_lanes,
        second_ref[:rows, lanes:].astype(jnp.float32),
        second_ref[:rows, :tile].astype(jnp.float32),
    )
    out_ref[2 * rows : 3 * rows, :tile] = merged.astype(jnp.bfloat16)
    out_ref[2 * rows : 3 * rows, tile:] = second_ref[:rows, tile:lanes]
    out_ref[3 * rows :, :] = second_ref[rows:, :lanes]


def hold_kernel(piece_ref, _, out_ref):
    out_ref[...] = piece_ref[...]


def owner(targets_ref, level, block):
    if level == 0:
        return jnp.int32(block)
    group = 2**level
    return block // group * group + targets_ref[level - 1, block]


def rows_of(targets_ref, level, source_ref, slab):
    device = lax.axis_index("leaf")
    return jnp.concatenate(
        [
            source_ref[
                pl.ds(pl.multiple_of((owner(targets_ref, level, block) ^ device) * slab, slab), slab), :
            ]
            for block in range(targets_ref.shape[1])
        ],
        axis=0,
    )


def side_of(raw, level, columns):
    size = raw.shape[0]
    row = lax.broadcasted_iota(jnp.int32, (columns, size), 0)
    lane = lax.broadcasted_iota(jnp.int32, (columns, size), 1)
    pick = jnp.where(lane == row + level * columns, 1.0, 0.0).astype(jnp.bfloat16)
    return times_transposed(pick, raw[:, :size])


def times_transposed(left, right):
    return lax.dot_general(left, right, (((1,), (1,)), ((), ())), preferred_element_type=jnp.float32)


def front_matrix(source, pick, level, slab):
    size, width = pick.shape[0], slab // 2
    row = lax.broadcasted_iota(jnp.int32, (size, size), 0)
    lane = lax.broadcasted_iota(jnp.int32, (size, size), 1)
    plain = jnp.dot(source, pick, preferred_element_type=jnp.float32)
    swapped = plain.reshape(size // slab, 2, width, size)
    swapped = jnp.concatenate([swapped[:, 1:], swapped[:, :1]], axis=1).reshape(size, size)
    signed = jnp.where((row // width) % 2 == 0, plain, -plain)
    full = jnp.where((lane // width) % 2 == 0, signed, swapped)
    inside = row // (slab * 2**level) == lane // (slab * 2**level)
    return jnp.where(inside, full, 0.0).astype(jnp.bfloat16)


def conjugate(values_in, width):
    lane = lax.broadcasted_iota(jnp.int32, (1, values_in.shape[1]), 1)
    return jnp.where((lane // width) % 2 == 0, values_in, -values_in)


def near_kernel(
    targets_ref,
    near_ref,
    pick_ref,
    panel_ref,
    update_ref,
    solved_ref,
    lower_ref,
    leaf_ref,
    operator_ref,
    all_ref,
):
    depth, devices = targets_ref.shape
    columns, size = update_ref.shape
    slab = size // devices
    width = slab // 2
    top = depth - 1
    all_ref[: size // 2, :] = near_ref[...]
    all_ref[size // 2 :, :] = jnp.zeros_like(near_ref)
    arriving = side_of(rows_of(targets_ref, 0, all_ref, slab), 0, columns)
    partial, lower = [None], [None]
    for level in range(1, depth):
        raw = rows_of(targets_ref, level, all_ref, slab)
        level_z = (side_of(raw, level, columns) - arriving).astype(jnp.bfloat16)
        inverse = front_matrix(raw[:, size:], pick_ref[level - 1], level, slab)
        lower.append(front_matrix(raw[:, :size], pick_ref[depth + level - 1], level, slab))
        partial.append(jnp.dot(level_z, inverse, preferred_element_type=jnp.float32))
        arriving = jnp.dot(level_z, lower[level], preferred_element_type=jnp.float32)
    update_ref[...] = arriving
    known, operator = partial[top], lower[top]
    solved = {top: known}
    lower_ref[top - 1] = operator
    for level in range(top - 1, 0, -1):
        parent = conjugate(known, width).astype(jnp.bfloat16)
        known = partial[level] - conjugate(times_transposed(parent, lower[level]), width)
        operator = -jnp.dot(lower[level], operator, preferred_element_type=jnp.float32)
        operator = operator.astype(jnp.bfloat16)
        solved[level] = known
        lower_ref[level - 1] = operator
    stacked = [solved[level] for level in range(1, depth)]
    stacked.append(jnp.zeros((size - top * columns, size), jnp.float32))
    solved_ref[...] = jnp.concatenate(stacked, axis=0).T
    parent = conjugate(known, width).astype(jnp.bfloat16)
    leaf_ref[...] = jnp.dot(parent, panel_ref[...], preferred_element_type=jnp.float32)
    operator_ref[...] = lax.dot_general(
        operator, panel_ref[...], (((0,), (0,)), ((), ())), preferred_element_type=jnp.float32
    ).astype(jnp.bfloat16)


def top_kernel(targets_ref, near_ref, far_ref, pick_ref, update_ref, _, parent_ref, solved_ref, half_ref, all_ref):
    depth, devices = targets_ref.shape
    columns, size = update_ref.shape
    slab = size // devices
    half_ref[: size // 2, :] = jnp.zeros_like(near_ref)
    half_ref[size // 2 :, :] = far_ref[...]
    all_ref[: size // 2, :] = near_ref[...]
    all_ref[size // 2 :, :] = far_ref[...]
    raw = rows_of(targets_ref, depth, all_ref, slab)
    inverse = front_matrix(raw[:, size:], pick_ref[depth - 1], depth, slab)
    waiting = side_of(raw, depth, columns) - update_ref[...]
    arriving = side_of(rows_of(targets_ref, 0, half_ref, slab), 0, columns)
    for level in range(1, depth):
        raw = rows_of(targets_ref, level, half_ref, slab)
        level_z = (side_of(raw, level, columns) - arriving).astype(jnp.bfloat16)
        lower = front_matrix(raw[:, :size], pick_ref[depth + level - 1], level, slab)
        arriving = jnp.dot(level_z, lower, preferred_element_type=jnp.float32)
    level_z = (waiting - arriving).astype(jnp.bfloat16)
    solved = jnp.dot(level_z, inverse, preferred_element_type=jnp.float32)
    solved_ref[...] = lax.dot_general(
        inverse, level_z, (((0,), (1,)), ((), ())), preferred_element_type=jnp.float32
    )
    parent_ref[...] = conjugate(solved, slab // 2).astype(jnp.bfloat16)


def finish_kernel(
    steps,
    live_ref,
    targets_ref,
    z_ref,
    partial_ref,
    parent_ref,
    top_ref,
    solved_ref,
    lower_ref,
    leaf_ref,
    operator_ref,
    *refs,
):
    piece_refs, (leaf_out_ref, sep_out_ref) = refs[: len(steps)], refs[len(steps) : len(steps) + 2]
    leaf_place, sep_place, sems = refs[len(steps) + 2 :]
    depth, devices = targets_ref.shape
    columns, size = parent_ref.shape
    leaf_rows = leaf_place.shape[2]
    slab = size // devices
    width = slab // 2
    device = lax.axis_index("leaf")
    live = lax.broadcasted_iota(jnp.int32, (1, leaf_rows), 1) < live_ref[0] * 128
    parent = parent_ref[...]
    for level in range(1, depth + 1):
        place = jnp.int32(0)
        for block in range(devices):
            place = jnp.where(owner(targets_ref, level, block) == device, block, place)
        rows = pl.ds(pl.multiple_of(place * slab, slab), slab)
        if level < depth:
            known = solved_ref[rows, :][:, (level - 1) * columns : level * columns]
            change = times_transposed(lower_ref[level - 1, rows, :], parent)
            halves = known[:width] - change[:width], known[width:] + change[width:]
        else:
            solved = top_ref[rows, :]
            halves = solved[:width], solved[width:]
        for part in range(2):
            sep_place[part, level - 1] = halves[part]
    from_tree = leaf_ref[...] - jnp.dot(parent, operator_ref[...], preferred_element_type=jnp.float32)
    products = [piece_product(step, z_ref, piece_ref) for step, piece_ref in zip(steps, piece_refs)]
    copies = []
    for part in range(2):
        leaf_w = partial_ref[part] + sum(product[part] for product in products)
        leaf_place[part] = (
            jnp.where(live, leaf_w, 0.0) - from_tree[:, part * leaf_rows : (part + 1) * leaf_rows]
        )
        copies.append(pltpu.make_async_copy(leaf_place.at[part], leaf_out_ref.at[part], sems.at[part]))
        copies[-1].start()
    copies.append(pltpu.make_async_copy(sep_place, sep_out_ref, sems.at[2]))
    copies[-1].start()
    for copy in copies:
        copy.wait()


def whole(space):
    return pl.BlockSpec(memory_space=space)


def body(leaf_rhs, sep_rhs, leaf_inv, leaf_low, sep_inv, sep_low, leaf_live, targets):
    devices, parts = lax.axis_size("leaf"), lax.axis_size("rhs")
    columns, leaf_rows = leaf_rhs.shape[1:]
    width, depth = sep_inv.shape[1], sep_rhs.shape[2]
    slab = 2 * width
    size = devices * slab
    small_tree = (
        devices == 8 and parts % 2 == 0 and size == 128 and (1 + depth) * columns + sep_low.shape[2] <= 128 and sep_inv.shape[2] <= 128
    )
    panel = leaf_low.transpose(0, 2, 1)
    tree_rhs = sep_rhs.transpose(0, 2, 3, 1)

    if not small_tree:
        live_mask = (jnp.arange(leaf_rows) < leaf_live[0] * 128).astype(jnp.float32)
        leaf_z = (leaf_rhs * live_mask).astype(jnp.bfloat16)
        leaf_w = complex_dot(leaf_z, lax.all_gather(leaf_inv, "rhs", axis=1, tiled=True)) * live_mask
        return level_by_level(leaf_rhs, sep_rhs, leaf_w, leaf_low, sep_inv, sep_low, leaf_live, targets)

    tree_parts = (leaf_rhs, panel, tree_rhs, sep_inv, sep_low)
    first = pl.pallas_call(
        first_kernel,
        out_shape=pltpu.VMEM((8, 128), jnp.float32),
        out_specs=whole(VMEM),
        cost_estimate=pl.CostEstimate(flops=10**9, bytes_accessed=0, transcendentals=0),
    )()
    held, own_tile, leaf_z = pl.pallas_call(
        pack_kernel,
        out_shape=(
            pltpu.VMEM((slab, 2 * size), jnp.bfloat16),
            pltpu.VMEM((slab, size), jnp.bfloat16),
            pltpu.VMEM((2 * columns, leaf_rows), jnp.bfloat16),
        ),
        in_specs=[whole(SMEM)] + [whole(VMEM)] * 6,
        out_specs=(whole(VMEM),) * 3,
    )(leaf_live, *[in_vmem(part) for part in (first,) + tree_parts])

    def exchange(values_in, offset, flip):
        partners = [
            (source * parts + part, (source ^ offset) * parts + (part ^ flip))
            for source in range(devices)
            for part in range(parts)
        ]
        return lax.ppermute(values_in, ("leaf", "rhs"), partners)

    first_round = exchange(held, 1, 1)
    pair_tile = xor_permute(own_tile, "rhs", 1)
    second_part, first_tile = pl.pallas_call(
        join_first_kernel,
        out_shape=(
            pltpu.VMEM((2 * slab, 3 * size), jnp.bfloat16),
            pltpu.VMEM((slab, size), jnp.bfloat16),
        ),
        in_specs=[whole(VMEM)] * 3,
        out_specs=(whole(VMEM),) * 2,
        cost_estimate=pl.CostEstimate(flops=10**11, bytes_accessed=0, transcendentals=0),
    )(in_vmem(held), in_vmem(first_round), in_vmem(pair_tile))
    second_round = exchange(second_part, 2, 1)
    panel_rows, picks, kept_targets = pl.pallas_call(
        functools.partial(prepare_kernel, (1 + depth) * columns),
        out_shape=(
            pltpu.VMEM((size, 2 * leaf_rows), jnp.bfloat16),
            pltpu.VMEM((2 * depth - 1, size, size), jnp.bfloat16),
            pltpu.SMEM(targets.shape, jnp.int32),
        ),
        in_specs=[whole(SMEM), whole(SMEM), whole(VMEM), whole(VMEM)],
        out_specs=(whole(VMEM),) * 2 + (whole(SMEM),),
        cost_estimate=pl.CostEstimate(flops=0, bytes_accessed=0, transcendentals=0),
    )(leaf_live, targets, panel, in_vmem(first_tile))

    pair_first = xor_permute(first_tile, "rhs", 1)
    held = pl.pallas_call(
        functools.partial(join_second_kernel, (1 + depth) * columns),
        out_shape=pltpu.VMEM((4 * slab, 2 * size), jnp.bfloat16),
        in_specs=[whole(VMEM)] * 5,
        out_specs=whole(VMEM),
        cost_estimate=pl.CostEstimate(flops=0, bytes_accessed=0, transcendentals=0),
    )(*[in_vmem(ready) for ready in (held, first_round, pair_first, second_round, picks)])
    far = exchange(held, 4, 0)

    def hold(piece):
        return pl.pallas_call(
            hold_kernel,
            out_shape=pltpu.VMEM(piece.shape, piece.dtype),
            in_specs=[whole(VMEM)] * 2,
            out_specs=whole(VMEM),
        )(in_vmem(piece), in_vmem(held))

    far_piece = hold(xor_permute(leaf_inv, "rhs", 3))
    partial = pl.pallas_call(
        functools.partial(leaf_kernel, (0, 3)),
        out_shape=pltpu.VMEM((2, columns, leaf_rows), jnp.float32),
        in_specs=[whole(VMEM)] * 3,
        out_specs=whole(VMEM),
        cost_estimate=pl.CostEstimate(flops=0, bytes_accessed=0, transcendentals=0),
    )(*[in_vmem(ready) for ready in (leaf_z, leaf_inv, far_piece)])
    kept_targets = pltpu.with_memory_space_constraint(kept_targets, SMEM)
    update, known, lower, known_leaf, operator = pl.pallas_call(
        near_kernel,
        out_shape=(
            pltpu.VMEM((columns, size), jnp.float32),
            pltpu.VMEM((size, size), jnp.float32),
            pltpu.VMEM((depth - 1, size, size), jnp.bfloat16),
            pltpu.VMEM((columns, 2 * leaf_rows), jnp.float32),
            pltpu.VMEM((size, 2 * leaf_rows), jnp.bfloat16),
        ),
        in_specs=[whole(SMEM)] + [whole(VMEM)] * 3,
        out_specs=(whole(VMEM),) * 5,
        scratch_shapes=[pltpu.VMEM((size, 2 * size), jnp.bfloat16)],
        cost_estimate=pl.CostEstimate(flops=0, bytes_accessed=0, transcendentals=0),
    )(kept_targets, *[in_vmem(ready) for ready in (held, picks, panel_rows)])
    parent_x, top_x = pl.pallas_call(
        top_kernel,
        out_shape=(
            pltpu.VMEM((columns, size), jnp.bfloat16),
            pltpu.VMEM((size, columns), jnp.float32),
        ),
        in_specs=[whole(SMEM)] + [whole(VMEM)] * 5,
        out_specs=(whole(VMEM),) * 2,
        scratch_shapes=[pltpu.VMEM((size, 2 * size), jnp.bfloat16)] * 2,
        cost_estimate=pl.CostEstimate(flops=3 * 10**9, bytes_accessed=0, transcendentals=0),
    )(kept_targets, *[in_vmem(ready) for ready in (held, far, picks, update, partial)])
    pair_pieces = (xor_permute(leaf_inv, "rhs", 1), xor_permute(far_piece, "rhs", 1))
    leaf_x, sep_x = pl.pallas_call(
        functools.partial(finish_kernel, (1, 2)),
        out_shape=(
            jax.ShapeDtypeStruct((2, columns, leaf_rows), jnp.float32),
            jax.ShapeDtypeStruct((2, depth, width, columns), jnp.float32),
        ),
        in_specs=[whole(SMEM)] * 2 + [whole(VMEM)] * 10,
        out_specs=(whole(pl.ANY),) * 2,
        scratch_shapes=[
            pltpu.VMEM((2, columns, leaf_rows), jnp.float32),
            pltpu.VMEM((2, depth, width, columns), jnp.float32),
            pltpu.SemaphoreType.DMA((3,)),
        ],
    )(
        leaf_live,
        kept_targets,
        *[
            in_vmem(ready)
            for ready in (leaf_z, partial, parent_x, top_x, known, lower, known_leaf, operator) + pair_pieces
        ],
    )
    return leaf_x, sep_x.transpose(0, 3, 1, 2)


def solution(mesh):
    placed = (
        P(None, "rhs", "leaf"),
        P(None, "rhs", None, "leaf"),
        P(None, "rhs", "leaf"),
        P(None, None, "leaf"),
        P(None, None, "leaf"),
        P(None, None, "leaf"),
        P("leaf"),
        P(),
    )
    return jax.shard_map(
        body,
        mesh=mesh,
        in_specs=placed,
        out_specs=(P(None, "rhs", "leaf"), P(None, "rhs", None, "leaf")),
        check_vma=False,
    )
```

```python
import functools

import jax
import jax.numpy as jnp
from jax import lax
from jax.experimental import pallas as pl
from jax.experimental.pallas import tpu as pltpu
from jax.sharding import PartitionSpec as P

exact_mode = lax.Precision.HIGHEST
VMEM = pltpu.MemorySpace.VMEM
SMEM = pltpu.MemorySpace.SMEM


def complex_dot(operand, factor):
    row_count = operand.shape[1]
    stacked = jnp.concatenate([operand[0], operand[1]], axis=0)
    real_acc = jnp.dot(stacked, factor[0], preferred_element_type=jnp.float32)
    imag_acc = jnp.dot(stacked, factor[1], preferred_element_type=jnp.float32)
    return jnp.stack(
        [real_acc[:row_count] - imag_acc[row_count:], imag_acc[:row_count] + real_acc[row_count:]]
    )


def complex_dot_back(operand, factor):
    row_count = operand.shape[1]
    stacked = jnp.concatenate([operand[0], operand[1]], axis=0)
    contract = (((1,), (1,)), ((), ()))
    real_acc = lax.dot_general(stacked, factor[0], contract, preferred_element_type=jnp.float32)
    imag_acc = lax.dot_general(stacked, factor[1], contract, preferred_element_type=jnp.float32)
    return jnp.stack(
        [real_acc[:row_count] - imag_acc[row_count:], imag_acc[:row_count] + real_acc[row_count:]]
    )


def to_blocks(values_in, group_size):
    return (
        values_in.reshape(2, values_in.shape[1], group_size, -1)
        .transpose(2, 0, 1, 3)
        .reshape(group_size, -1)
    )


def from_blocks(blocks, columns):
    group_size = blocks.shape[0]
    return blocks.reshape(group_size, 2, columns, -1).transpose(1, 2, 0, 3).reshape(2, columns, -1)


def selector(dest_index, total_slots):
    return (dest_index[:, None] == jnp.arange(total_slots, dtype=jnp.int32)[None, :]).astype(
        jnp.float32
    )


def exchange_sum(blocks, global_dest, devices):
    routed = jnp.dot(selector(global_dest, devices).T, blocks, precision=exact_mode)
    received = lax.all_to_all(
        routed.astype(jnp.bfloat16), "leaf", split_axis=0, concat_axis=0, tiled=True
    ).astype(routed.dtype)
    return jnp.sum(received, axis=0)


def collect(blocks, local_dest, level_bits, device, devices):
    group_start = device >> level_bits << level_bits
    return exchange_sum(blocks, group_start + local_dest, devices)


def spread(own_block, level_bits, device, devices):
    group_size = 2**level_bits
    group_start = device >> level_bits << level_bits
    slot_index = jnp.arange(devices, dtype=jnp.int32)[:, None]
    inside = (slot_index >= group_start) & (slot_index < group_start + group_size)
    routed = jnp.where(inside, own_block[None, :], jnp.zeros_like(own_block)[None, :])
    received = lax.all_to_all(routed, "leaf", split_axis=0, concat_axis=0, tiled=True)
    return lax.dynamic_slice_in_dim(received, group_start, group_size, 0)


def level_by_level(leaf_rhs, sep_rhs, leaf_w, leaf_low, sep_inv, sep_low, leaf_live, targets):
    devices = lax.axis_size("leaf")
    tree_depth = devices.bit_length() - 1
    device = lax.axis_index("leaf")
    leaf_rows = leaf_low.shape[1]
    sep_width = sep_inv.shape[1]
    columns = leaf_rhs.shape[1]
    live_mask = (jnp.arange(leaf_rows) < leaf_live[0] * 128).astype(jnp.float32)
    leaf_z = (leaf_rhs * live_mask).astype(jnp.bfloat16)
    first_dest = lax.dynamic_slice_in_dim(targets[0], device, 1)
    arriving = collect(complex_dot(leaf_z, leaf_low).reshape(1, -1), first_dest, 1, device, devices)
    solved_w = []
    for level_now in range(1, tree_depth + 1):
        group_size = 2**level_now
        offset = sep_width * (group_size - 2)
        level_z = (
            sep_rhs[:, :, level_now - 1, :] - arriving.reshape(2, columns, sep_width)
        ).astype(jnp.bfloat16)
        inv_rows = sep_inv[:, :, offset : offset + sep_width * group_size]
        own_w = collect(
            to_blocks(complex_dot(level_z, inv_rows), group_size),
            jnp.arange(group_size, dtype=jnp.int32),
            level_now,
            device,
            devices,
        )
        solved_w.append(own_w.reshape(2, columns, sep_width))
        if level_now < tree_depth:
            low_rows = sep_low[:, :, offset : offset + sep_width * group_size]
            group_start = device >> level_now << level_now
            dest_index = lax.dynamic_slice_in_dim(targets[level_now], group_start, group_size)
            arriving = collect(
                to_blocks(complex_dot(level_z, low_rows), group_size),
                dest_index,
                level_now + 1,
                device,
                devices,
            )
    solved_x = [solved_w[level_now] for level_now in range(tree_depth)]
    for level_now in range(tree_depth - 1, 0, -1):
        group_size = 2**level_now
        offset = sep_width * (group_size - 2)
        low_rows = sep_low[:, :, offset : offset + sep_width * group_size]
        parent_x = spread(
            solved_x[level_now].astype(jnp.bfloat16).reshape(-1), level_now + 1, device, devices
        )
        group_start = device >> level_now << level_now
        dest_index = lax.dynamic_slice_in_dim(targets[level_now], group_start, group_size)
        picked = jnp.dot(
            selector(dest_index, 2 * group_size).astype(jnp.bfloat16),
            parent_x,
            preferred_element_type=jnp.float32,
        ).astype(jnp.bfloat16)
        solved_x[level_now - 1] = solved_w[level_now - 1] - complex_dot_back(
            from_blocks(picked, columns), low_rows
        )
    parent_x = spread(solved_x[0].astype(jnp.bfloat16).reshape(-1), 1, device, devices)
    picked = jnp.dot(
        selector(first_dest, 2).astype(jnp.bfloat16), parent_x, preferred_element_type=jnp.float32
    ).astype(jnp.bfloat16)
    leaf_x = (
        leaf_w - complex_dot_back(picked.reshape(2, columns, sep_width), leaf_low)
    ) * live_mask
    return leaf_x, jnp.stack(solved_x, axis=2)


def xor_permute(values_in, axis, offset):
    count = lax.axis_size(axis)
    return lax.ppermute(values_in, axis, [(source, source ^ offset) for source in range(count)])


def in_vmem(values_in):
    return pltpu.with_memory_space_constraint(values_in, VMEM)


def masked_rows(leaf_rhs, live_ref):
    rows = leaf_rhs.shape[2]
    live = lax.broadcasted_iota(jnp.int32, (1, rows), 1) < live_ref[0] * 128
    stacked = jnp.concatenate([leaf_rhs[0], leaf_rhs[1]], axis=0)
    return jnp.where(live, stacked, 0.0).astype(jnp.bfloat16), live


def first_kernel(out_ref):
    out_ref[...] = jnp.zeros_like(out_ref)


def pack_kernel(live_ref, _, leaf_rhs_ref, low_ref, rhs_ref, inv_ref, sep_low_ref, out_ref, tile_ref, z_ref):
    columns = leaf_rhs_ref.shape[1]
    depth = rhs_ref.shape[1]
    leaf_z, _ = masked_rows(leaf_rhs_ref[...], live_ref)
    z_ref[...] = leaf_z
    panel = jnp.concatenate([low_ref[0], low_ref[1]], axis=0)
    product = lax.dot_general(
        panel, leaf_z, (((1,), (1,)), ((), ())), preferred_element_type=jnp.float32
    )
    width = low_ref.shape[1]
    update = [
        product[:width, :columns] - product[width:, columns:],
        product[width:, :columns] + product[:width, columns:],
    ]
    used = (1 + depth) * columns + sep_low_ref.shape[2]
    halves = []
    for part in range(2):
        pieces = [update[part]] + [rhs_ref[part, level] for level in range(depth)]
        pieces.append(sep_low_ref[part].astype(jnp.float32))
        if used < 128:
            pieces.append(jnp.zeros((width, 128 - used), jnp.float32))
        pieces.append(inv_ref[part].astype(jnp.float32))
        if inv_ref.shape[2] < 128:
            pieces.append(jnp.zeros((width, 128 - inv_ref.shape[2]), jnp.float32))
        halves.append(jnp.concatenate(pieces, axis=1))
    packed = jnp.concatenate(halves, axis=0).astype(jnp.bfloat16)
    out_ref[...] = packed
    tile_ref[...] = packed[:, : tile_ref.shape[1]]


def piece_product(step, z_ref, piece_ref):
    columns = z_ref.shape[0] // 2
    depth = piece_ref.shape[1]
    owner = lax.axis_index("rhs") ^ step
    rows = z_ref[:, pl.ds(pl.multiple_of(owner * depth, 128), depth)]
    real_acc = jnp.dot(rows, piece_ref[0], preferred_element_type=jnp.float32)
    imag_acc = jnp.dot(rows, piece_ref[1], preferred_element_type=jnp.float32)
    return real_acc[:columns] - imag_acc[columns:], imag_acc[:columns] + real_acc[columns:]


def leaf_kernel(steps, z_ref, *refs):
    out_ref = refs[-1]
    products = [piece_product(step, z_ref, piece_ref) for step, piece_ref in zip(steps, refs[:-1])]
    for part in range(2):
        out_ref[part] = sum(product[part] for product in products)


def prepare_kernel(low_start, live_ref, targets_ref, low_ref, _, panel_ref, pick_ref, kept_ref):
    for level in range(targets_ref.shape[0]):
        for block in range(targets_ref.shape[1]):
            kept_ref[level, block] = targets_ref[level, block]
    depth, devices = targets_ref.shape
    width, leaf_rows = low_ref.shape[1:]
    slab = 2 * width
    device = lax.axis_index("leaf")
    live = lax.broadcasted_iota(jnp.int32, (1, leaf_rows), 1) < live_ref[0] * 128
    low = [jnp.where(live, low_ref[part].astype(jnp.float32), 0.0) for part in range(2)]
    rows = jnp.concatenate(
        [
            jnp.concatenate([low[0], low[1]], axis=1),
            jnp.concatenate([low[1], -low[0]], axis=1),
        ],
        axis=0,
    ).astype(jnp.bfloat16)
    panel_ref[...] = jnp.zeros_like(panel_ref)
    panel_ref[pl.ds(pl.multiple_of(device * slab, slab), slab), :] = rows
    size = devices * slab
    row = lax.broadcasted_iota(jnp.int32, (size, size), 0)
    lane_row = lax.broadcasted_iota(jnp.int32, (1, size), 1)
    for level in range(1, depth + 1):
        offset = width * (2**level - 2) + lane_row % width
        target_lane = jnp.zeros((1, size), jnp.int32)
        for block in range(devices):
            target_lane = jnp.where(lane_row // slab == block, targets_ref[level - 1, block], target_lane)
        pick_ref[level - 1] = jnp.where(row == offset + target_lane * width, 1.0, 0.0).astype(jnp.bfloat16)
        if level < depth:
            own_lane = (lane_row // slab) % 2**level
            pick_ref[depth + level - 1] = jnp.where(
                row == low_start + offset + own_lane * width, 1.0, 0.0
            ).astype(jnp.bfloat16)


def join_first_kernel(own_ref, received_ref, pair_ref, out_ref, tile_ref):
    rows, lanes = own_ref.shape
    tile = pair_ref.shape[1]
    out_ref[:rows, :lanes] = own_ref[...]
    out_ref[rows:, :lanes] = received_ref[...]
    out_ref[:rows, lanes:] = pair_ref[...]
    out_ref[rows:, lanes:] = pair_ref[...]
    tile_ref[...] = received_ref[:, :tile]


def join_second_kernel(side_lanes, own_ref, first_ref, pair_ref, second_ref, _, out_ref):
    rows, lanes = own_ref.shape
    tile = pair_ref.shape[1]
    out_ref[:rows, :] = own_ref[...]
    out_ref[rows : 2 * rows, :tile] = pair_ref[...]
    out_ref[rows : 2 * rows, tile:] = first_ref[:, tile:]
    lane = lax.broadcasted_iota(jnp.int32, (rows, tile), 1)
    merged = jnp.where(
        lane < side_lanes,
        second_ref[:rows, lanes:].astype(jnp.float32),
        second_ref[:rows, :tile].astype(jnp.float32),
    )
    out_ref[2 * rows : 3 * rows, :tile] = merged.astype(jnp.bfloat16)
    out_ref[2 * rows : 3 * rows, tile:] = second_ref[:rows, tile:lanes]
    out_ref[3 * rows :, :] = second_ref[rows:, :lanes]


def hold_kernel(piece_ref, _, out_ref):
    out_ref[...] = piece_ref[...]


def owner(targets_ref, level, block):
    if level == 0:
        return jnp.int32(block)
    group = 2**level
    return block // group * group + targets_ref[level - 1, block]


def rows_of(targets_ref, level, source_ref, slab):
    device = lax.axis_index("leaf")
    return jnp.concatenate(
        [
            source_ref[
                pl.ds(pl.multiple_of((owner(targets_ref, level, block) ^ device) * slab, slab), slab), :
            ]
            for block in range(targets_ref.shape[1])
        ],
        axis=0,
    )


def side_of(raw, level, columns):
    size = raw.shape[0]
    row = lax.broadcasted_iota(jnp.int32, (columns, size), 0)
    lane = lax.broadcasted_iota(jnp.int32, (columns, size), 1)
    pick = jnp.where(lane == row + level * columns, 1.0, 0.0).astype(jnp.bfloat16)
    return times_transposed(pick, raw[:, :size])


def times_transposed(left, right):
    return lax.dot_general(left, right, (((1,), (1,)), ((), ())), preferred_element_type=jnp.float32)


def front_matrix(source, pick, level, slab):
    size, width = pick.shape[0], slab // 2
    row = lax.broadcasted_iota(jnp.int32, (size, size), 0)
    lane = lax.broadcasted_iota(jnp.int32, (size, size), 1)
    plain = jnp.dot(source, pick, preferred_element_type=jnp.float32)
    swapped = plain.reshape(size // slab, 2, width, size)
    swapped = jnp.concatenate([swapped[:, 1:], swapped[:, :1]], axis=1).reshape(size, size)
    signed = jnp.where((row // width) % 2 == 0, plain, -plain)
    full = jnp.where((lane // width) % 2 == 0, signed, swapped)
    inside = row // (slab * 2**level) == lane // (slab * 2**level)
    return jnp.where(inside, full, 0.0).astype(jnp.bfloat16)


def conjugate(values_in, width):
    lane = lax.broadcasted_iota(jnp.int32, (1, values_in.shape[1]), 1)
    return jnp.where((lane // width) % 2 == 0, values_in, -values_in)


def near_kernel(targets_ref, near_ref, pick_ref, update_ref, partial_ref, lower_ref, all_ref):
    depth, devices = targets_ref.shape
    columns, size = update_ref.shape
    slab = size // devices
    all_ref[: size // 2, :] = near_ref[...]
    all_ref[size // 2 :, :] = jnp.zeros_like(near_ref)
    arriving = side_of(rows_of(targets_ref, 0, all_ref, slab), 0, columns)
    for level in range(1, depth):
        raw = rows_of(targets_ref, level, all_ref, slab)
        level_z = (side_of(raw, level, columns) - arriving).astype(jnp.bfloat16)
        inverse = front_matrix(raw[:, size:], pick_ref[level - 1], level, slab)
        lower = front_matrix(raw[:, :size], pick_ref[depth + level - 1], level, slab)
        lower_ref[level - 1] = lower
        partial_ref[level - 1] = jnp.dot(level_z, inverse, preferred_element_type=jnp.float32)
        arriving = jnp.dot(level_z, lower, preferred_element_type=jnp.float32)
    update_ref[...] = arriving


def operator_kernel(partial_ref, lower_ref, panel_ref, _, solved_ref, back_ref, leaf_ref, operator_ref):
    top, columns, size = partial_ref.shape
    width = size // 16
    known, operator = partial_ref[top - 1], lower_ref[top - 1]
    solved = {top: known}
    back_ref[top - 1] = operator
    for level in range(top - 1, 0, -1):
        parent = conjugate(known, width).astype(jnp.bfloat16)
        known = partial_ref[level - 1] - conjugate(times_transposed(parent, lower_ref[level - 1]), width)
        operator = -jnp.dot(lower_ref[level - 1], operator, preferred_element_type=jnp.float32)
        operator = operator.astype(jnp.bfloat16)
        solved[level] = known
        back_ref[level - 1] = operator
    stacked = [solved[level] for level in range(1, top + 1)]
    stacked.append(jnp.zeros((size - top * columns, size), jnp.float32))
    solved_ref[...] = jnp.concatenate(stacked, axis=0).T
    parent = conjugate(known, width).astype(jnp.bfloat16)
    leaf_ref[...] = jnp.dot(parent, panel_ref[...], preferred_element_type=jnp.float32)
    operator_ref[...] = lax.dot_general(
        operator, panel_ref[...], (((0,), (0,)), ((), ())), preferred_element_type=jnp.float32
    ).astype(jnp.bfloat16)


def top_kernel(
    targets_ref, near_ref, far_ref, pick_ref, update_ref, _, __, parent_ref, solved_ref, half_ref, all_ref
):
    depth, devices = targets_ref.shape
    columns, size = update_ref.shape
    slab = size // devices
    half_ref[: size // 2, :] = jnp.zeros_like(near_ref)
    half_ref[size // 2 :, :] = far_ref[...]
    all_ref[: size // 2, :] = near_ref[...]
    all_ref[size // 2 :, :] = far_ref[...]
    raw = rows_of(targets_ref, depth, all_ref, slab)
    inverse = front_matrix(raw[:, size:], pick_ref[depth - 1], depth, slab)
    waiting = side_of(raw, depth, columns) - update_ref[...]
    arriving = side_of(rows_of(targets_ref, 0, half_ref, slab), 0, columns)
    for level in range(1, depth):
        raw = rows_of(targets_ref, level, half_ref, slab)
        level_z = (side_of(raw, level, columns) - arriving).astype(jnp.bfloat16)
        lower = front_matrix(raw[:, :size], pick_ref[depth + level - 1], level, slab)
        arriving = jnp.dot(level_z, lower, preferred_element_type=jnp.float32)
    level_z = (waiting - arriving).astype(jnp.bfloat16)
    solved = jnp.dot(level_z, inverse, preferred_element_type=jnp.float32)
    solved_ref[...] = lax.dot_general(
        inverse, level_z, (((0,), (1,)), ((), ())), preferred_element_type=jnp.float32
    )
    parent_ref[...] = conjugate(solved, slab // 2).astype(jnp.bfloat16)


def finish_kernel(
    steps,
    live_ref,
    targets_ref,
    z_ref,
    partial_ref,
    parent_ref,
    top_ref,
    solved_ref,
    lower_ref,
    leaf_ref,
    operator_ref,
    *refs,
):
    piece_refs, (leaf_out_ref, sep_out_ref) = refs[: len(steps)], refs[len(steps) : len(steps) + 2]
    leaf_place, sep_place, sems = refs[len(steps) + 2 :]
    depth, devices = targets_ref.shape
    columns, size = parent_ref.shape
    leaf_rows = leaf_place.shape[2]
    slab = size // devices
    width = slab // 2
    device = lax.axis_index("leaf")
    live = lax.broadcasted_iota(jnp.int32, (1, leaf_rows), 1) < live_ref[0] * 128
    parent = parent_ref[...]
    for level in range(1, depth + 1):
        place = jnp.int32(0)
        for block in range(devices):
            place = jnp.where(owner(targets_ref, level, block) == device, block, place)
        rows = pl.ds(pl.multiple_of(place * slab, slab), slab)
        if level < depth:
            known = solved_ref[rows, :][:, (level - 1) * columns : level * columns]
            change = times_transposed(lower_ref[level - 1, rows, :], parent)
            halves = known[:width] - change[:width], known[width:] + change[width:]
        else:
            solved = top_ref[rows, :]
            halves = solved[:width], solved[width:]
        for part in range(2):
            sep_place[part, level - 1] = halves[part]
    from_tree = leaf_ref[...] - jnp.dot(parent, operator_ref[...], preferred_element_type=jnp.float32)
    products = [piece_product(step, z_ref, piece_ref) for step, piece_ref in zip(steps, piece_refs)]
    copies = []
    for part in range(2):
        leaf_w = partial_ref[part] + sum(product[part] for product in products)
        leaf_place[part] = (
            jnp.where(live, leaf_w, 0.0) - from_tree[:, part * leaf_rows : (part + 1) * leaf_rows]
        )
        copies.append(pltpu.make_async_copy(leaf_place.at[part], leaf_out_ref.at[part], sems.at[part]))
        copies[-1].start()
    copies.append(pltpu.make_async_copy(sep_place, sep_out_ref, sems.at[2]))
    copies[-1].start()
    for copy in copies:
        copy.wait()


def whole(space):
    return pl.BlockSpec(memory_space=space)


def body(leaf_rhs, sep_rhs, leaf_inv, leaf_low, sep_inv, sep_low, leaf_live, targets):
    devices, parts = lax.axis_size("leaf"), lax.axis_size("rhs")
    columns, leaf_rows = leaf_rhs.shape[1:]
    width, depth = sep_inv.shape[1], sep_rhs.shape[2]
    slab = 2 * width
    size = devices * slab
    small_tree = (
        devices == 8 and parts % 2 == 0 and size == 128 and (1 + depth) * columns + sep_low.shape[2] <= 128 and sep_inv.shape[2] <= 128
    )
    panel = leaf_low.transpose(0, 2, 1)
    tree_rhs = sep_rhs.transpose(0, 2, 3, 1)

    if not small_tree:
        live_mask = (jnp.arange(leaf_rows) < leaf_live[0] * 128).astype(jnp.float32)
        leaf_z = (leaf_rhs * live_mask).astype(jnp.bfloat16)
        leaf_w = complex_dot(leaf_z, lax.all_gather(leaf_inv, "rhs", axis=1, tiled=True)) * live_mask
        return level_by_level(leaf_rhs, sep_rhs, leaf_w, leaf_low, sep_inv, sep_low, leaf_live, targets)

    tree_parts = (leaf_rhs, panel, tree_rhs, sep_inv, sep_low)
    first = pl.pallas_call(
        first_kernel,
        out_shape=pltpu.VMEM((8, 128), jnp.float32),
        out_specs=whole(VMEM),
        cost_estimate=pl.CostEstimate(flops=10**9, bytes_accessed=0, transcendentals=0),
    )()
    held, own_tile, leaf_z = pl.pallas_call(
        pack_kernel,
        out_shape=(
            pltpu.VMEM((slab, 2 * size), jnp.bfloat16),
            pltpu.VMEM((slab, size), jnp.bfloat16),
            pltpu.VMEM((2 * columns, leaf_rows), jnp.bfloat16),
        ),
        in_specs=[whole(SMEM)] + [whole(VMEM)] * 6,
        out_specs=(whole(VMEM),) * 3,
    )(leaf_live, *[in_vmem(part) for part in (first,) + tree_parts])

    def exchange(values_in, offset, flip):
        partners = [
            (source * parts + part, (source ^ offset) * parts + (part ^ flip))
            for source in range(devices)
            for part in range(parts)
        ]
        return lax.ppermute(values_in, ("leaf", "rhs"), partners)

    first_round = exchange(held, 1, 1)
    pair_tile = xor_permute(own_tile, "rhs", 1)
    second_part, first_tile = pl.pallas_call(
        join_first_kernel,
        out_shape=(
            pltpu.VMEM((2 * slab, 3 * size), jnp.bfloat16),
            pltpu.VMEM((slab, size), jnp.bfloat16),
        ),
        in_specs=[whole(VMEM)] * 3,
        out_specs=(whole(VMEM),) * 2,
        cost_estimate=pl.CostEstimate(flops=10**11, bytes_accessed=0, transcendentals=0),
    )(in_vmem(held), in_vmem(first_round), in_vmem(pair_tile))
    second_round = exchange(second_part, 2, 1)
    panel_rows, picks, kept_targets = pl.pallas_call(
        functools.partial(prepare_kernel, (1 + depth) * columns),
        out_shape=(
            pltpu.VMEM((size, 2 * leaf_rows), jnp.bfloat16),
            pltpu.VMEM((2 * depth - 1, size, size), jnp.bfloat16),
            pltpu.SMEM(targets.shape, jnp.int32),
        ),
        in_specs=[whole(SMEM), whole(SMEM), whole(VMEM), whole(VMEM)],
        out_specs=(whole(VMEM),) * 2 + (whole(SMEM),),
        cost_estimate=pl.CostEstimate(flops=0, bytes_accessed=0, transcendentals=0),
    )(leaf_live, targets, panel, in_vmem(first_tile))

    pair_first = xor_permute(first_tile, "rhs", 1)
    held = pl.pallas_call(
        functools.partial(join_second_kernel, (1 + depth) * columns),
        out_shape=pltpu.VMEM((4 * slab, 2 * size), jnp.bfloat16),
        in_specs=[whole(VMEM)] * 5,
        out_specs=whole(VMEM),
        cost_estimate=pl.CostEstimate(flops=0, bytes_accessed=0, transcendentals=0),
    )(*[in_vmem(ready) for ready in (held, first_round, pair_first, second_round, picks)])
    far = exchange(held, 4, 0)

    kept_targets = pltpu.with_memory_space_constraint(kept_targets, SMEM)
    update, partial_x, lower = pl.pallas_call(
        near_kernel,
        out_shape=(
            pltpu.VMEM((columns, size), jnp.float32),
            pltpu.VMEM((depth - 1, columns, size), jnp.float32),
            pltpu.VMEM((depth - 1, size, size), jnp.bfloat16),
        ),
        in_specs=[whole(SMEM)] + [whole(VMEM)] * 2,
        out_specs=(whole(VMEM),) * 3,
        scratch_shapes=[pltpu.VMEM((size, 2 * size), jnp.bfloat16)],
        cost_estimate=pl.CostEstimate(flops=0, bytes_accessed=0, transcendentals=0),
    )(kept_targets, *[in_vmem(ready) for ready in (held, picks)])
    far_piece = pl.pallas_call(
        hold_kernel,
        out_shape=pltpu.VMEM(leaf_inv.shape, leaf_inv.dtype),
        in_specs=[whole(VMEM)] * 2,
        out_specs=whole(VMEM),
    )(in_vmem(xor_permute(leaf_inv, "rhs", 3)), in_vmem(update))
    known, back, known_leaf, operator = pl.pallas_call(
        operator_kernel,
        out_shape=(
            pltpu.VMEM((size, size), jnp.float32),
            pltpu.VMEM((depth - 1, size, size), jnp.bfloat16),
            pltpu.VMEM((columns, 2 * leaf_rows), jnp.float32),
            pltpu.VMEM((size, 2 * leaf_rows), jnp.bfloat16),
        ),
        in_specs=[whole(VMEM)] * 4,
        out_specs=(whole(VMEM),) * 4,
        cost_estimate=pl.CostEstimate(flops=0, bytes_accessed=0, transcendentals=0),
    )(*[in_vmem(ready) for ready in (partial_x, lower, panel_rows, far_piece)])
    partial = pl.pallas_call(
        functools.partial(leaf_kernel, (0, 3)),
        out_shape=pltpu.VMEM((2, columns, leaf_rows), jnp.float32),
        in_specs=[whole(VMEM)] * 3,
        out_specs=whole(VMEM),
        cost_estimate=pl.CostEstimate(flops=0, bytes_accessed=0, transcendentals=0),
    )(*[in_vmem(ready) for ready in (leaf_z, leaf_inv, far_piece)])
    parent_x, top_x = pl.pallas_call(
        top_kernel,
        out_shape=(
            pltpu.VMEM((columns, size), jnp.bfloat16),
            pltpu.VMEM((size, columns), jnp.float32),
        ),
        in_specs=[whole(SMEM)] + [whole(VMEM)] * 6,
        out_specs=(whole(VMEM),) * 2,
        scratch_shapes=[
            pltpu.VMEM((size, 2 * size), jnp.bfloat16),
            pltpu.VMEM((size, 2 * size), jnp.bfloat16),
        ],
        cost_estimate=pl.CostEstimate(flops=3 * 10**9, bytes_accessed=0, transcendentals=0),
    )(kept_targets, *[in_vmem(ready) for ready in (held, far, picks, update, partial, known_leaf)])
    pair_pieces = (xor_permute(leaf_inv, "rhs", 1), xor_permute(far_piece, "rhs", 1))
    leaf_x, sep_x = pl.pallas_call(
        functools.partial(finish_kernel, (1, 2)),
        out_shape=(
            jax.ShapeDtypeStruct((2, columns, leaf_rows), jnp.float32),
            jax.ShapeDtypeStruct((2, depth, width, columns), jnp.float32),
        ),
        in_specs=[whole(SMEM)] * 2 + [whole(VMEM)] * 10,
        out_specs=(whole(pl.ANY),) * 2,
        scratch_shapes=[
            pltpu.VMEM((2, columns, leaf_rows), jnp.float32),
            pltpu.VMEM((2, depth, width, columns), jnp.float32),
            pltpu.SemaphoreType.DMA((3,)),
        ],
    )(
        leaf_live,
        kept_targets,
        *[
            in_vmem(ready)
            for ready in (leaf_z, partial, parent_x, top_x, known, back, known_leaf, operator) + pair_pieces
        ],
    )
    return leaf_x, sep_x.transpose(0, 3, 1, 2)


def solution(mesh):
    placed = (
        P(None, "rhs", "leaf"),
        P(None, "rhs", None, "leaf"),
        P(None, "rhs", "leaf"),
        P(None, None, "leaf"),
        P(None, None, "leaf"),
        P(None, None, "leaf"),
        P("leaf"),
        P(),
    )
    return jax.shard_map(
        body,
        mesh=mesh,
        in_specs=placed,
        out_specs=(P(None, "rhs", "leaf"), P(None, "rhs", None, "leaf")),
        check_vma=False,
    )
```

```python
import functools

import jax
import jax.numpy as jnp
from jax import lax
from jax.experimental import pallas as pl
from jax.experimental.pallas import tpu as pltpu
from jax.sharding import PartitionSpec as P

exact_mode = lax.Precision.HIGHEST
VMEM = pltpu.MemorySpace.VMEM
SMEM = pltpu.MemorySpace.SMEM


def complex_dot(operand, factor):
    row_count = operand.shape[1]
    stacked = jnp.concatenate([operand[0], operand[1]], axis=0)
    real_acc = jnp.dot(stacked, factor[0], preferred_element_type=jnp.float32)
    imag_acc = jnp.dot(stacked, factor[1], preferred_element_type=jnp.float32)
    return jnp.stack(
        [real_acc[:row_count] - imag_acc[row_count:], imag_acc[:row_count] + real_acc[row_count:]]
    )


def complex_dot_back(operand, factor):
    row_count = operand.shape[1]
    stacked = jnp.concatenate([operand[0], operand[1]], axis=0)
    contract = (((1,), (1,)), ((), ()))
    real_acc = lax.dot_general(stacked, factor[0], contract, preferred_element_type=jnp.float32)
    imag_acc = lax.dot_general(stacked, factor[1], contract, preferred_element_type=jnp.float32)
    return jnp.stack(
        [real_acc[:row_count] - imag_acc[row_count:], imag_acc[:row_count] + real_acc[row_count:]]
    )


def to_blocks(values_in, group_size):
    return (
        values_in.reshape(2, values_in.shape[1], group_size, -1)
        .transpose(2, 0, 1, 3)
        .reshape(group_size, -1)
    )


def from_blocks(blocks, columns):
    group_size = blocks.shape[0]
    return blocks.reshape(group_size, 2, columns, -1).transpose(1, 2, 0, 3).reshape(2, columns, -1)


def selector(dest_index, total_slots):
    return (dest_index[:, None] == jnp.arange(total_slots, dtype=jnp.int32)[None, :]).astype(
        jnp.float32
    )


def exchange_sum(blocks, global_dest, devices):
    routed = jnp.dot(selector(global_dest, devices).T, blocks, precision=exact_mode)
    received = lax.all_to_all(
        routed.astype(jnp.bfloat16), "leaf", split_axis=0, concat_axis=0, tiled=True
    ).astype(routed.dtype)
    return jnp.sum(received, axis=0)


def collect(blocks, local_dest, level_bits, device, devices):
    group_start = device >> level_bits << level_bits
    return exchange_sum(blocks, group_start + local_dest, devices)


def spread(own_block, level_bits, device, devices):
    group_size = 2**level_bits
    group_start = device >> level_bits << level_bits
    slot_index = jnp.arange(devices, dtype=jnp.int32)[:, None]
    inside = (slot_index >= group_start) & (slot_index < group_start + group_size)
    routed = jnp.where(inside, own_block[None, :], jnp.zeros_like(own_block)[None, :])
    received = lax.all_to_all(routed, "leaf", split_axis=0, concat_axis=0, tiled=True)
    return lax.dynamic_slice_in_dim(received, group_start, group_size, 0)


def level_by_level(leaf_rhs, sep_rhs, leaf_w, leaf_low, sep_inv, sep_low, leaf_live, targets):
    devices = lax.axis_size("leaf")
    tree_depth = devices.bit_length() - 1
    device = lax.axis_index("leaf")
    leaf_rows = leaf_low.shape[1]
    sep_width = sep_inv.shape[1]
    columns = leaf_rhs.shape[1]
    live_mask = (jnp.arange(leaf_rows) < leaf_live[0] * 128).astype(jnp.float32)
    leaf_z = (leaf_rhs * live_mask).astype(jnp.bfloat16)
    first_dest = lax.dynamic_slice_in_dim(targets[0], device, 1)
    arriving = collect(complex_dot(leaf_z, leaf_low).reshape(1, -1), first_dest, 1, device, devices)
    solved_w = []
    for level_now in range(1, tree_depth + 1):
        group_size = 2**level_now
        offset = sep_width * (group_size - 2)
        level_z = (
            sep_rhs[:, :, level_now - 1, :] - arriving.reshape(2, columns, sep_width)
        ).astype(jnp.bfloat16)
        inv_rows = sep_inv[:, :, offset : offset + sep_width * group_size]
        own_w = collect(
            to_blocks(complex_dot(level_z, inv_rows), group_size),
            jnp.arange(group_size, dtype=jnp.int32),
            level_now,
            device,
            devices,
        )
        solved_w.append(own_w.reshape(2, columns, sep_width))
        if level_now < tree_depth:
            low_rows = sep_low[:, :, offset : offset + sep_width * group_size]
            group_start = device >> level_now << level_now
            dest_index = lax.dynamic_slice_in_dim(targets[level_now], group_start, group_size)
            arriving = collect(
                to_blocks(complex_dot(level_z, low_rows), group_size),
                dest_index,
                level_now + 1,
                device,
                devices,
            )
    solved_x = [solved_w[level_now] for level_now in range(tree_depth)]
    for level_now in range(tree_depth - 1, 0, -1):
        group_size = 2**level_now
        offset = sep_width * (group_size - 2)
        low_rows = sep_low[:, :, offset : offset + sep_width * group_size]
        parent_x = spread(
            solved_x[level_now].astype(jnp.bfloat16).reshape(-1), level_now + 1, device, devices
        )
        group_start = device >> level_now << level_now
        dest_index = lax.dynamic_slice_in_dim(targets[level_now], group_start, group_size)
        picked = jnp.dot(
            selector(dest_index, 2 * group_size).astype(jnp.bfloat16),
            parent_x,
            preferred_element_type=jnp.float32,
        ).astype(jnp.bfloat16)
        solved_x[level_now - 1] = solved_w[level_now - 1] - complex_dot_back(
            from_blocks(picked, columns), low_rows
        )
    parent_x = spread(solved_x[0].astype(jnp.bfloat16).reshape(-1), 1, device, devices)
    picked = jnp.dot(
        selector(first_dest, 2).astype(jnp.bfloat16), parent_x, preferred_element_type=jnp.float32
    ).astype(jnp.bfloat16)
    leaf_x = (
        leaf_w - complex_dot_back(picked.reshape(2, columns, sep_width), leaf_low)
    ) * live_mask
    return leaf_x, jnp.stack(solved_x, axis=2)


def xor_permute(values_in, axis, offset):
    count = lax.axis_size(axis)
    return lax.ppermute(values_in, axis, [(source, source ^ offset) for source in range(count)])


def in_vmem(values_in):
    return pltpu.with_memory_space_constraint(values_in, VMEM)


def masked_rows(leaf_rhs, live_ref):
    rows = leaf_rhs.shape[2]
    live = lax.broadcasted_iota(jnp.int32, (1, rows), 1) < live_ref[0] * 128
    stacked = jnp.concatenate([leaf_rhs[0], leaf_rhs[1]], axis=0)
    return jnp.where(live, stacked, 0.0).astype(jnp.bfloat16), live


def first_kernel(out_ref):
    out_ref[...] = jnp.zeros_like(out_ref)


def pack_kernel(live_ref, _, leaf_rhs_ref, low_ref, rhs_ref, inv_ref, sep_low_ref, out_ref, tile_ref, send_ref, z_ref):
    columns = leaf_rhs_ref.shape[1]
    depth = rhs_ref.shape[1]
    leaf_z, _ = masked_rows(leaf_rhs_ref[...], live_ref)
    z_ref[...] = leaf_z
    panel = jnp.concatenate([low_ref[0], low_ref[1]], axis=0)
    product = lax.dot_general(
        panel, leaf_z, (((1,), (1,)), ((), ())), preferred_element_type=jnp.float32
    )
    width = low_ref.shape[1]
    update = [
        product[:width, :columns] - product[width:, columns:],
        product[width:, :columns] + product[:width, columns:],
    ]
    used = (1 + depth) * columns + sep_low_ref.shape[2]
    halves, turned = [], []
    for part in range(2):
        pieces = [update[part]] + [rhs_ref[part, level] for level in range(depth)]
        pieces.append(sep_low_ref[part].astype(jnp.float32))
        if used < 128:
            pieces.append(jnp.zeros((width, 128 - used), jnp.float32))
        inverse = inv_ref[part].astype(jnp.float32)
        below = width * (2**depth - 2)
        gap = jnp.zeros((width, 128 - inverse.shape[1]), jnp.float32)
        pieces += [inverse[:, below:], inverse[:, :below], gap]
        turned.append(jnp.concatenate([inverse[:, :below], gap, inverse[:, below:]], axis=1))
        halves.append(jnp.concatenate(pieces, axis=1))
    packed = jnp.concatenate(halves, axis=0).astype(jnp.bfloat16)
    out_ref[...] = packed
    tile_ref[...] = packed[:, : tile_ref.shape[1]]
    send_ref[:, : tile_ref.shape[1]] = packed[:, : tile_ref.shape[1]]
    send_ref[:, tile_ref.shape[1] :] = jnp.concatenate(turned, axis=0).astype(jnp.bfloat16)


def piece_product(step, z_ref, piece_ref):
    columns = z_ref.shape[0] // 2
    depth = piece_ref.shape[1]
    owner = lax.axis_index("rhs") ^ step
    rows = z_ref[:, pl.ds(pl.multiple_of(owner * depth, 128), depth)]
    real_acc = jnp.dot(rows, piece_ref[0], preferred_element_type=jnp.float32)
    imag_acc = jnp.dot(rows, piece_ref[1], preferred_element_type=jnp.float32)
    return real_acc[:columns] - imag_acc[columns:], imag_acc[:columns] + real_acc[columns:]


def leaf_kernel(steps, z_ref, *refs):
    out_ref = refs[-1]
    products = [piece_product(step, z_ref, piece_ref) for step, piece_ref in zip(steps, refs[:-1])]
    for part in range(2):
        out_ref[part] = sum(product[part] for product in products)


def prepare_kernel(low_start, live_ref, targets_ref, low_ref, _, panel_ref, pick_ref, kept_ref):
    for level in range(targets_ref.shape[0]):
        for block in range(targets_ref.shape[1]):
            kept_ref[level, block] = targets_ref[level, block]
    depth, devices = targets_ref.shape
    width, leaf_rows = low_ref.shape[1:]
    slab = 2 * width
    device = lax.axis_index("leaf")
    live = lax.broadcasted_iota(jnp.int32, (1, leaf_rows), 1) < live_ref[0] * 128
    low = [jnp.where(live, low_ref[part].astype(jnp.float32), 0.0) for part in range(2)]
    rows = jnp.concatenate(
        [
            jnp.concatenate([low[0], low[1]], axis=1),
            jnp.concatenate([low[1], -low[0]], axis=1),
        ],
        axis=0,
    ).astype(jnp.bfloat16)
    panel_ref[...] = jnp.zeros_like(panel_ref)
    panel_ref[pl.ds(pl.multiple_of(device * slab, slab), slab), :] = rows
    size = devices * slab
    row = lax.broadcasted_iota(jnp.int32, (size, size), 0)
    lane_row = lax.broadcasted_iota(jnp.int32, (1, size), 1)
    for level in range(1, depth + 1):
        offset = width * (2**level - 2) + lane_row % width
        inverse_offset = lane_row % width if level == depth else offset + width * devices
        target_lane = jnp.zeros((1, size), jnp.int32)
        for block in range(devices):
            target_lane = jnp.where(lane_row // slab == block, targets_ref[level - 1, block], target_lane)
        pick_ref[level - 1] = jnp.where(row == inverse_offset + target_lane * width, 1.0, 0.0).astype(
            jnp.bfloat16
        )
        if level == depth:
            pick_ref[2 * depth - 1] = jnp.where(
                row == size // 2 + inverse_offset + target_lane * width, 1.0, 0.0
            ).astype(jnp.bfloat16)
        if level < depth:
            own_lane = (lane_row // slab) % 2**level
            pick_ref[depth + level - 1] = jnp.where(
                row == low_start + offset + own_lane * width, 1.0, 0.0
            ).astype(jnp.bfloat16)


def join_first_kernel(own_ref, received_ref, pair_ref, out_ref, tile_ref):
    rows, lanes = own_ref.shape
    tile = pair_ref.shape[1]
    out_ref[:rows, :lanes] = own_ref[...]
    out_ref[rows:, :lanes] = received_ref[...]
    out_ref[:rows, lanes:] = pair_ref[...]
    out_ref[rows:, lanes:] = pair_ref[...]
    tile_ref[...] = received_ref[:, :tile]


def join_second_kernel(side_lanes, own_ref, first_ref, pair_ref, second_ref, _, out_ref, send_ref):
    rows, lanes = own_ref.shape
    tile = pair_ref.shape[1]
    out_ref[:rows, :] = own_ref[...]
    out_ref[rows : 2 * rows, :tile] = pair_ref[...]
    out_ref[rows : 2 * rows, tile:] = first_ref[:, tile:]
    lane = lax.broadcasted_iota(jnp.int32, (rows, tile), 1)
    merged = jnp.where(
        lane < side_lanes,
        second_ref[:rows, lanes:].astype(jnp.float32),
        second_ref[:rows, :tile].astype(jnp.float32),
    )
    out_ref[2 * rows : 3 * rows, :tile] = merged.astype(jnp.bfloat16)
    out_ref[2 * rows : 3 * rows, tile:] = second_ref[:rows, tile:lanes]
    out_ref[3 * rows :, :] = second_ref[rows:, :lanes]
    half = tile // 2
    send_ref[:rows, :] = own_ref[:, :tile]
    send_ref[rows : 2 * rows, :] = pair_ref[...]
    send_ref[2 * rows : 3 * rows, :] = merged.astype(jnp.bfloat16)
    send_ref[3 * rows : 4 * rows, :] = second_ref[rows:, :tile]
    send_ref[4 * rows : 5 * rows, :half] = own_ref[:, tile : tile + half]
    send_ref[4 * rows : 5 * rows, half:] = first_ref[:, tile + half :]
    send_ref[5 * rows :, :half] = second_ref[:rows, tile : tile + half]
    send_ref[5 * rows :, half:] = second_ref[rows:, tile + half : 2 * tile]


def hold_kernel(piece_ref, _, out_ref):
    out_ref[...] = piece_ref[...]


def owner(targets_ref, level, block):
    if level == 0:
        return jnp.int32(block)
    group = 2**level
    return block // group * group + targets_ref[level - 1, block]


def rows_of(targets_ref, level, source_ref, slab):
    device = lax.axis_index("leaf")
    return jnp.concatenate(
        [
            source_ref[
                pl.ds(pl.multiple_of((owner(targets_ref, level, block) ^ device) * slab, slab), slab), :
            ]
            for block in range(targets_ref.shape[1])
        ],
        axis=0,
    )


def side_of(raw, level, columns):
    size = raw.shape[0]
    row = lax.broadcasted_iota(jnp.int32, (columns, size), 0)
    lane = lax.broadcasted_iota(jnp.int32, (columns, size), 1)
    pick = jnp.where(lane == row + level * columns, 1.0, 0.0).astype(jnp.bfloat16)
    return times_transposed(pick, raw[:, :size])


def times_transposed(left, right):
    return lax.dot_general(left, right, (((1,), (1,)), ((), ())), preferred_element_type=jnp.float32)


def front_matrix(source, pick, level, slab):
    return front_of(jnp.dot(source, pick, preferred_element_type=jnp.float32), level, slab)


def front_of(plain, level, slab):
    size, width = plain.shape[0], slab // 2
    row = lax.broadcasted_iota(jnp.int32, (size, size), 0)
    lane = lax.broadcasted_iota(jnp.int32, (size, size), 1)
    swapped = plain.reshape(size // slab, 2, width, size)
    swapped = jnp.concatenate([swapped[:, 1:], swapped[:, :1]], axis=1).reshape(size, size)
    signed = jnp.where((row // width) % 2 == 0, plain, -plain)
    full = jnp.where((lane // width) % 2 == 0, signed, swapped)
    inside = row // (slab * 2**level) == lane // (slab * 2**level)
    return jnp.where(inside, full, 0.0).astype(jnp.bfloat16)


def conjugate(values_in, width):
    lane = lax.broadcasted_iota(jnp.int32, (1, values_in.shape[1]), 1)
    return jnp.where((lane // width) % 2 == 0, values_in, -values_in)


def near_kernel(targets_ref, near_ref, pick_ref, update_ref, partial_ref, lower_ref, kept_ref, all_ref):
    depth, devices = targets_ref.shape
    columns, size = update_ref.shape
    slab = size // devices
    half = size // 2
    for place_ref in (kept_ref, all_ref):
        place_ref[:half, :] = near_ref[...]
        for slot in range(1, devices // 2, 2):
            rows = slice(slot * slab, (slot + 1) * slab)
            turned = pltpu.roll(near_ref[rows, size:].astype(jnp.float32), half, 1)
            place_ref[rows, size:] = turned.astype(jnp.bfloat16)
    all_ref[half:, :] = jnp.zeros_like(near_ref)
    arriving = side_of(rows_of(targets_ref, 0, all_ref, slab), 0, columns)
    for level in range(1, depth):
        raw = rows_of(targets_ref, level, all_ref, slab)
        level_z = (side_of(raw, level, columns) - arriving).astype(jnp.bfloat16)
        inverse = front_matrix(raw[:, size:], pick_ref[level - 1], level, slab)
        lower = front_matrix(raw[:, :size], pick_ref[depth + level - 1], level, slab)
        lower_ref[level - 1] = lower
        partial_ref[level - 1] = jnp.dot(level_z, inverse, preferred_element_type=jnp.float32)
        arriving = jnp.dot(level_z, lower, preferred_element_type=jnp.float32)
    update_ref[...] = arriving


def operator_kernel(partial_ref, lower_ref, panel_ref, _, solved_ref, back_ref, leaf_ref, operator_ref):
    top, columns, size = partial_ref.shape
    width = size // 16
    known, operator = partial_ref[top - 1], lower_ref[top - 1]
    solved = {top: known}
    back_ref[top - 1] = operator
    for level in range(top - 1, 0, -1):
        parent = conjugate(known, width).astype(jnp.bfloat16)
        known = partial_ref[level - 1] - conjugate(times_transposed(parent, lower_ref[level - 1]), width)
        operator = -jnp.dot(lower_ref[level - 1], operator, preferred_element_type=jnp.float32)
        operator = operator.astype(jnp.bfloat16)
        solved[level] = known
        back_ref[level - 1] = operator
    stacked = [solved[level] for level in range(1, top + 1)]
    stacked.append(jnp.zeros((size - top * columns, size), jnp.float32))
    solved_ref[...] = jnp.concatenate(stacked, axis=0).T
    parent = conjugate(known, width).astype(jnp.bfloat16)
    leaf_ref[...] = jnp.dot(parent, panel_ref[...], preferred_element_type=jnp.float32)
    operator_ref[...] = lax.dot_general(
        operator, panel_ref[...], (((0,), (0,)), ((), ())), preferred_element_type=jnp.float32
    ).astype(jnp.bfloat16)


def top_kernel(
    targets_ref, near_ref, far_ref, pick_ref, update_ref, _, __, parent_ref, solved_ref, half_ref, all_ref
):
    depth, devices = targets_ref.shape
    columns, size = update_ref.shape
    slab = size // devices
    half = size // 2
    half_ref[:half, :] = jnp.zeros((half, size), jnp.bfloat16)
    half_ref[half:, :] = far_ref[:half]
    all_ref[:half, :] = near_ref[...]
    all_ref[half:, :size] = far_ref[:half]
    for slot in range(devices // 2):
        rows = slice(half + slot // 2 * slab, half + (slot // 2 + 1) * slab)
        all_ref[half + slot * slab : half + (slot + 1) * slab, size:] = far_ref[rows]
    raw = rows_of(targets_ref, depth, all_ref, slab)
    row_block = lax.broadcasted_iota(jnp.int32, (size, size), 0) // slab
    upper = jnp.zeros((size, size), jnp.int32)
    for block in range(devices):
        slot = owner(targets_ref, depth, block) ^ lax.axis_index("leaf")
        upper = jnp.where(row_block == block, slot, upper)
    plain = jnp.where(
        (upper >= devices // 2) & (upper % 2 == 1),
        jnp.dot(raw[:, size:], pick_ref[2 * depth - 1], preferred_element_type=jnp.float32),
        jnp.dot(raw[:, size:], pick_ref[depth - 1], preferred_element_type=jnp.float32),
    )
    inverse = front_of(plain, depth, slab)
    waiting = side_of(raw, depth, columns) - update_ref[...]
    arriving = side_of(rows_of(targets_ref, 0, half_ref, slab), 0, columns)
    for level in range(1, depth):
        raw = rows_of(targets_ref, level, half_ref, slab)
        level_z = (side_of(raw, level, columns) - arriving).astype(jnp.bfloat16)
        lower = front_matrix(raw, pick_ref[depth + level - 1], level, slab)
        arriving = jnp.dot(level_z, lower, preferred_element_type=jnp.float32)
    level_z = (waiting - arriving).astype(jnp.bfloat16)
    solved = jnp.dot(level_z, inverse, preferred_element_type=jnp.float32)
    solved_ref[...] = lax.dot_general(
        inverse, level_z, (((0,), (1,)), ((), ())), preferred_element_type=jnp.float32
    )
    parent_ref[...] = conjugate(solved, slab // 2).astype(jnp.bfloat16)


def finish_kernel(
    steps,
    live_ref,
    targets_ref,
    z_ref,
    partial_ref,
    parent_ref,
    top_ref,
    solved_ref,
    lower_ref,
    leaf_ref,
    operator_ref,
    *refs,
):
    piece_refs, (leaf_out_ref, sep_out_ref) = refs[: len(steps)], refs[len(steps) : len(steps) + 2]
    leaf_place, sep_place, sems = refs[len(steps) + 2 :]
    depth, devices = targets_ref.shape
    columns, size = parent_ref.shape
    leaf_rows = leaf_place.shape[2]
    slab = size // devices
    width = slab // 2
    device = lax.axis_index("leaf")
    live = lax.broadcasted_iota(jnp.int32, (1, leaf_rows), 1) < live_ref[0] * 128
    parent = parent_ref[...]
    for level in range(1, depth + 1):
        place = jnp.int32(0)
        for block in range(devices):
            place = jnp.where(owner(targets_ref, level, block) == device, block, place)
        rows = pl.ds(pl.multiple_of(place * slab, slab), slab)
        if level < depth:
            known = solved_ref[rows, :][:, (level - 1) * columns : level * columns]
            change = times_transposed(lower_ref[level - 1, rows, :], parent)
            halves = known[:width] - change[:width], known[width:] + change[width:]
        else:
            solved = top_ref[rows, :]
            halves = solved[:width], solved[width:]
        for part in range(2):
            sep_place[part, level - 1] = halves[part]
    from_tree = leaf_ref[...] - jnp.dot(parent, operator_ref[...], preferred_element_type=jnp.float32)
    products = [piece_product(step, z_ref, piece_ref) for step, piece_ref in zip(steps, piece_refs)]
    copies = []
    for part in range(2):
        leaf_w = partial_ref[part] + sum(product[part] for product in products)
        leaf_place[part] = (
            jnp.where(live, leaf_w, 0.0) - from_tree[:, part * leaf_rows : (part + 1) * leaf_rows]
        )
        copies.append(pltpu.make_async_copy(leaf_place.at[part], leaf_out_ref.at[part], sems.at[part]))
        copies[-1].start()
    copies.append(pltpu.make_async_copy(sep_place, sep_out_ref, sems.at[2]))
    copies[-1].start()
    for copy in copies:
        copy.wait()


def whole(space):
    return pl.BlockSpec(memory_space=space)


def body(leaf_rhs, sep_rhs, leaf_inv, leaf_low, sep_inv, sep_low, leaf_live, targets):
    devices, parts = lax.axis_size("leaf"), lax.axis_size("rhs")
    columns, leaf_rows = leaf_rhs.shape[1:]
    width, depth = sep_inv.shape[1], sep_rhs.shape[2]
    slab = 2 * width
    size = devices * slab
    small_tree = (
        devices == 8 and parts % 2 == 0 and size == 128 and (1 + depth) * columns + sep_low.shape[2] <= 128 and sep_inv.shape[2] <= 128
    )
    panel = leaf_low.transpose(0, 2, 1)
    tree_rhs = sep_rhs.transpose(0, 2, 3, 1)

    if not small_tree:
        live_mask = (jnp.arange(leaf_rows) < leaf_live[0] * 128).astype(jnp.float32)
        leaf_z = (leaf_rhs * live_mask).astype(jnp.bfloat16)
        leaf_w = complex_dot(leaf_z, lax.all_gather(leaf_inv, "rhs", axis=1, tiled=True)) * live_mask
        return level_by_level(leaf_rhs, sep_rhs, leaf_w, leaf_low, sep_inv, sep_low, leaf_live, targets)

    tree_parts = (leaf_rhs, panel, tree_rhs, sep_inv, sep_low)
    first = pl.pallas_call(
        first_kernel,
        out_shape=pltpu.VMEM((8, 128), jnp.float32),
        out_specs=whole(VMEM),
        cost_estimate=pl.CostEstimate(flops=10**9, bytes_accessed=0, transcendentals=0),
    )()
    held, own_tile, sent, leaf_z = pl.pallas_call(
        pack_kernel,
        out_shape=(
            pltpu.VMEM((slab, 2 * size), jnp.bfloat16),
            pltpu.VMEM((slab, size), jnp.bfloat16),
            pltpu.VMEM((slab, 2 * size), jnp.bfloat16),
            pltpu.VMEM((2 * columns, leaf_rows), jnp.bfloat16),
        ),
        in_specs=[whole(SMEM)] + [whole(VMEM)] * 6,
        out_specs=(whole(VMEM),) * 4,
    )(leaf_live, *[in_vmem(part) for part in (first,) + tree_parts])

    def exchange(values_in, offset, flip):
        partners = [
            (source * parts + part, (source ^ offset) * parts + (part ^ flip))
            for source in range(devices)
            for part in range(parts)
        ]
        return lax.ppermute(values_in, ("leaf", "rhs"), partners)

    first_round = exchange(sent, 1, 1)
    pair_tile = xor_permute(own_tile, "rhs", 1)
    second_part, first_tile = pl.pallas_call(
        join_first_kernel,
        out_shape=(
            pltpu.VMEM((2 * slab, 3 * size), jnp.bfloat16),
            pltpu.VMEM((slab, size), jnp.bfloat16),
        ),
        in_specs=[whole(VMEM)] * 3,
        out_specs=(whole(VMEM),) * 2,
        cost_estimate=pl.CostEstimate(flops=10**11, bytes_accessed=0, transcendentals=0),
    )(*[in_vmem(ready) for ready in (held, first_round, pair_tile)])
    second_round = exchange(second_part, 2, 1)
    panel_rows, picks, kept_targets = pl.pallas_call(
        functools.partial(prepare_kernel, (1 + depth) * columns),
        out_shape=(
            pltpu.VMEM((size, 2 * leaf_rows), jnp.bfloat16),
            pltpu.VMEM((2 * depth, size, size), jnp.bfloat16),
            pltpu.SMEM(targets.shape, jnp.int32),
        ),
        in_specs=[whole(SMEM), whole(SMEM), whole(VMEM), whole(VMEM)],
        out_specs=(whole(VMEM),) * 2 + (whole(SMEM),),
        cost_estimate=pl.CostEstimate(flops=0, bytes_accessed=0, transcendentals=0),
    )(leaf_live, targets, panel, in_vmem(first_tile))

    pair_first = xor_permute(first_tile, "rhs", 1)
    held, sent = pl.pallas_call(
        functools.partial(join_second_kernel, (1 + depth) * columns),
        out_shape=(
            pltpu.VMEM((4 * slab, 2 * size), jnp.bfloat16),
            pltpu.VMEM((6 * slab, size), jnp.bfloat16),
        ),
        in_specs=[whole(VMEM)] * 5,
        out_specs=(whole(VMEM),) * 2,
        cost_estimate=pl.CostEstimate(flops=0, bytes_accessed=0, transcendentals=0),
    )(*[in_vmem(ready) for ready in (held, first_round, pair_first, second_round, picks)])
    far = exchange(sent, 4, 0)

    kept_targets = pltpu.with_memory_space_constraint(kept_targets, SMEM)
    update, partial_x, lower, kept_near = pl.pallas_call(
        near_kernel,
        out_shape=(
            pltpu.VMEM((columns, size), jnp.float32),
            pltpu.VMEM((depth - 1, columns, size), jnp.float32),
            pltpu.VMEM((depth - 1, size, size), jnp.bfloat16),
            pltpu.VMEM((size // 2, 2 * size), jnp.bfloat16),
        ),
        in_specs=[whole(SMEM)] + [whole(VMEM)] * 2,
        out_specs=(whole(VMEM),) * 4,
        scratch_shapes=[pltpu.VMEM((size, 2 * size), jnp.bfloat16)],
        cost_estimate=pl.CostEstimate(flops=0, bytes_accessed=0, transcendentals=0),
    )(kept_targets, *[in_vmem(ready) for ready in (held, picks)])
    far_piece = pl.pallas_call(
        hold_kernel,
        out_shape=pltpu.VMEM(leaf_inv.shape, leaf_inv.dtype),
        in_specs=[whole(VMEM)] * 2,
        out_specs=whole(VMEM),
    )(in_vmem(xor_permute(leaf_inv, "rhs", 3)), in_vmem(update))
    known, back, known_leaf, operator = pl.pallas_call(
        operator_kernel,
        out_shape=(
            pltpu.VMEM((size, size), jnp.float32),
            pltpu.VMEM((depth - 1, size, size), jnp.bfloat16),
            pltpu.VMEM((columns, 2 * leaf_rows), jnp.float32),
            pltpu.VMEM((size, 2 * leaf_rows), jnp.bfloat16),
        ),
        in_specs=[whole(VMEM)] * 4,
        out_specs=(whole(VMEM),) * 4,
        cost_estimate=pl.CostEstimate(flops=0, bytes_accessed=0, transcendentals=0),
    )(*[in_vmem(ready) for ready in (partial_x, lower, panel_rows, far_piece)])
    partial = pl.pallas_call(
        functools.partial(leaf_kernel, (0, 3)),
        out_shape=pltpu.VMEM((2, columns, leaf_rows), jnp.float32),
        in_specs=[whole(VMEM)] * 3,
        out_specs=whole(VMEM),
        cost_estimate=pl.CostEstimate(flops=0, bytes_accessed=0, transcendentals=0),
    )(*[in_vmem(ready) for ready in (leaf_z, leaf_inv, far_piece)])
    parent_x, top_x = pl.pallas_call(
        top_kernel,
        out_shape=(
            pltpu.VMEM((columns, size), jnp.bfloat16),
            pltpu.VMEM((size, columns), jnp.float32),
        ),
        in_specs=[whole(SMEM)] + [whole(VMEM)] * 6,
        out_specs=(whole(VMEM),) * 2,
        scratch_shapes=[
            pltpu.VMEM((size, size), jnp.bfloat16),
            pltpu.VMEM((size, 2 * size), jnp.bfloat16),
        ],
        cost_estimate=pl.CostEstimate(flops=3 * 10**9, bytes_accessed=0, transcendentals=0),
    )(kept_targets, *[in_vmem(ready) for ready in (kept_near, far, picks, update, partial, known_leaf)])
    pair_pieces = (xor_permute(leaf_inv, "rhs", 1), xor_permute(far_piece, "rhs", 1))
    leaf_x, sep_x = pl.pallas_call(
        functools.partial(finish_kernel, (1, 2)),
        out_shape=(
            jax.ShapeDtypeStruct((2, columns, leaf_rows), jnp.float32),
            jax.ShapeDtypeStruct((2, depth, width, columns), jnp.float32),
        ),
        in_specs=[whole(SMEM)] * 2 + [whole(VMEM)] * 10,
        out_specs=(whole(pl.ANY),) * 2,
        scratch_shapes=[
            pltpu.VMEM((2, columns, leaf_rows), jnp.float32),
            pltpu.VMEM((2, depth, width, columns), jnp.float32),
            pltpu.SemaphoreType.DMA((3,)),
        ],
    )(
        leaf_live,
        kept_targets,
        *[
            in_vmem(ready)
            for ready in (leaf_z, partial, parent_x, top_x, known, back, known_leaf, operator) + pair_pieces
        ],
    )
    return leaf_x, sep_x.transpose(0, 3, 1, 2)


def solution(mesh):
    placed = (
        P(None, "rhs", "leaf"),
        P(None, "rhs", None, "leaf"),
        P(None, "rhs", "leaf"),
        P(None, None, "leaf"),
        P(None, None, "leaf"),
        P(None, None, "leaf"),
        P("leaf"),
        P(),
    )
    return jax.shard_map(
        body,
        mesh=mesh,
        in_specs=placed,
        out_specs=(P(None, "rhs", "leaf"), P(None, "rhs", None, "leaf")),
        check_vma=False,
    )
```

```python
import functools

import jax
import jax.numpy as jnp
from jax import lax
from jax.experimental import pallas as pl
from jax.experimental.pallas import tpu as pltpu
from jax.sharding import PartitionSpec as P

exact_mode = lax.Precision.HIGHEST
VMEM = pltpu.MemorySpace.VMEM
SMEM = pltpu.MemorySpace.SMEM


def complex_dot(operand, factor):
    row_count = operand.shape[1]
    stacked = jnp.concatenate([operand[0], operand[1]], axis=0)
    real_acc = jnp.dot(stacked, factor[0], preferred_element_type=jnp.float32)
    imag_acc = jnp.dot(stacked, factor[1], preferred_element_type=jnp.float32)
    return jnp.stack(
        [real_acc[:row_count] - imag_acc[row_count:], imag_acc[:row_count] + real_acc[row_count:]]
    )


def complex_dot_back(operand, factor):
    row_count = operand.shape[1]
    stacked = jnp.concatenate([operand[0], operand[1]], axis=0)
    contract = (((1,), (1,)), ((), ()))
    real_acc = lax.dot_general(stacked, factor[0], contract, preferred_element_type=jnp.float32)
    imag_acc = lax.dot_general(stacked, factor[1], contract, preferred_element_type=jnp.float32)
    return jnp.stack(
        [real_acc[:row_count] - imag_acc[row_count:], imag_acc[:row_count] + real_acc[row_count:]]
    )


def to_blocks(values_in, group_size):
    return (
        values_in.reshape(2, values_in.shape[1], group_size, -1)
        .transpose(2, 0, 1, 3)
        .reshape(group_size, -1)
    )


def from_blocks(blocks, columns):
    group_size = blocks.shape[0]
    return blocks.reshape(group_size, 2, columns, -1).transpose(1, 2, 0, 3).reshape(2, columns, -1)


def selector(dest_index, total_slots):
    return (dest_index[:, None] == jnp.arange(total_slots, dtype=jnp.int32)[None, :]).astype(
        jnp.float32
    )


def exchange_sum(blocks, global_dest, devices):
    routed = jnp.dot(selector(global_dest, devices).T, blocks, precision=exact_mode)
    received = lax.all_to_all(
        routed.astype(jnp.bfloat16), "leaf", split_axis=0, concat_axis=0, tiled=True
    ).astype(routed.dtype)
    return jnp.sum(received, axis=0)


def collect(blocks, local_dest, level_bits, device, devices):
    group_start = device >> level_bits << level_bits
    return exchange_sum(blocks, group_start + local_dest, devices)


def spread(own_block, level_bits, device, devices):
    group_size = 2**level_bits
    group_start = device >> level_bits << level_bits
    slot_index = jnp.arange(devices, dtype=jnp.int32)[:, None]
    inside = (slot_index >= group_start) & (slot_index < group_start + group_size)
    routed = jnp.where(inside, own_block[None, :], jnp.zeros_like(own_block)[None, :])
    received = lax.all_to_all(routed, "leaf", split_axis=0, concat_axis=0, tiled=True)
    return lax.dynamic_slice_in_dim(received, group_start, group_size, 0)


def level_by_level(leaf_rhs, sep_rhs, leaf_w, leaf_low, sep_inv, sep_low, leaf_live, targets):
    devices = lax.axis_size("leaf")
    tree_depth = devices.bit_length() - 1
    device = lax.axis_index("leaf")
    leaf_rows = leaf_low.shape[1]
    sep_width = sep_inv.shape[1]
    columns = leaf_rhs.shape[1]
    live_mask = (jnp.arange(leaf_rows) < leaf_live[0] * 128).astype(jnp.float32)
    leaf_z = (leaf_rhs * live_mask).astype(jnp.bfloat16)
    first_dest = lax.dynamic_slice_in_dim(targets[0], device, 1)
    arriving = collect(complex_dot(leaf_z, leaf_low).reshape(1, -1), first_dest, 1, device, devices)
    solved_w = []
    for level_now in range(1, tree_depth + 1):
        group_size = 2**level_now
        offset = sep_width * (group_size - 2)
        level_z = (
            sep_rhs[:, :, level_now - 1, :] - arriving.reshape(2, columns, sep_width)
        ).astype(jnp.bfloat16)
        inv_rows = sep_inv[:, :, offset : offset + sep_width * group_size]
        own_w = collect(
            to_blocks(complex_dot(level_z, inv_rows), group_size),
            jnp.arange(group_size, dtype=jnp.int32),
            level_now,
            device,
            devices,
        )
        solved_w.append(own_w.reshape(2, columns, sep_width))
        if level_now < tree_depth:
            low_rows = sep_low[:, :, offset : offset + sep_width * group_size]
            group_start = device >> level_now << level_now
            dest_index = lax.dynamic_slice_in_dim(targets[level_now], group_start, group_size)
            arriving = collect(
                to_blocks(complex_dot(level_z, low_rows), group_size),
                dest_index,
                level_now + 1,
                device,
                devices,
            )
    solved_x = [solved_w[level_now] for level_now in range(tree_depth)]
    for level_now in range(tree_depth - 1, 0, -1):
        group_size = 2**level_now
        offset = sep_width * (group_size - 2)
        low_rows = sep_low[:, :, offset : offset + sep_width * group_size]
        parent_x = spread(
            solved_x[level_now].astype(jnp.bfloat16).reshape(-1), level_now + 1, device, devices
        )
        group_start = device >> level_now << level_now
        dest_index = lax.dynamic_slice_in_dim(targets[level_now], group_start, group_size)
        picked = jnp.dot(
            selector(dest_index, 2 * group_size).astype(jnp.bfloat16),
            parent_x,
            preferred_element_type=jnp.float32,
        ).astype(jnp.bfloat16)
        solved_x[level_now - 1] = solved_w[level_now - 1] - complex_dot_back(
            from_blocks(picked, columns), low_rows
        )
    parent_x = spread(solved_x[0].astype(jnp.bfloat16).reshape(-1), 1, device, devices)
    picked = jnp.dot(
        selector(first_dest, 2).astype(jnp.bfloat16), parent_x, preferred_element_type=jnp.float32
    ).astype(jnp.bfloat16)
    leaf_x = (
        leaf_w - complex_dot_back(picked.reshape(2, columns, sep_width), leaf_low)
    ) * live_mask
    return leaf_x, jnp.stack(solved_x, axis=2)


def xor_permute(values_in, axis, offset):
    count = lax.axis_size(axis)
    return lax.ppermute(values_in, axis, [(source, source ^ offset) for source in range(count)])


def in_vmem(values_in):
    return pltpu.with_memory_space_constraint(values_in, VMEM)


def masked_rows(leaf_rhs, live_ref):
    rows = leaf_rhs.shape[2]
    live = lax.broadcasted_iota(jnp.int32, (1, rows), 1) < live_ref[0] * 128
    stacked = jnp.concatenate([leaf_rhs[0], leaf_rhs[1]], axis=0)
    return jnp.where(live, stacked, 0.0).astype(jnp.bfloat16), live


def first_kernel(out_ref):
    out_ref[...] = jnp.zeros_like(out_ref)


def pack_kernel(live_ref, _, leaf_rhs_ref, low_ref, rhs_ref, inv_ref, sep_low_ref, out_ref, tile_ref, send_ref, z_ref):
    columns = leaf_rhs_ref.shape[1]
    depth = rhs_ref.shape[1]
    leaf_z, _ = masked_rows(leaf_rhs_ref[...], live_ref)
    z_ref[...] = leaf_z
    panel = jnp.concatenate([low_ref[0], low_ref[1]], axis=0)
    product = lax.dot_general(
        panel, leaf_z, (((1,), (1,)), ((), ())), preferred_element_type=jnp.float32
    )
    width = low_ref.shape[1]
    update = [
        product[:width, :columns] - product[width:, columns:],
        product[width:, :columns] + product[:width, columns:],
    ]
    used = (1 + depth) * columns + sep_low_ref.shape[2]
    halves, turned = [], []
    for part in range(2):
        pieces = [update[part]] + [rhs_ref[part, level] for level in range(depth)]
        pieces.append(sep_low_ref[part].astype(jnp.float32))
        if used < 128:
            pieces.append(jnp.zeros((width, 128 - used), jnp.float32))
        inverse = inv_ref[part].astype(jnp.float32)
        below = width * (2**depth - 2)
        gap = jnp.zeros((width, 128 - inverse.shape[1]), jnp.float32)
        pieces += [inverse[:, below:], inverse[:, :below], gap]
        turned.append(jnp.concatenate([inverse[:, :below], gap, inverse[:, below:]], axis=1))
        halves.append(jnp.concatenate(pieces, axis=1))
    packed = jnp.concatenate(halves, axis=0).astype(jnp.bfloat16)
    out_ref[...] = packed
    tile_ref[...] = packed[:, : tile_ref.shape[1]]
    send_ref[:, : tile_ref.shape[1]] = packed[:, : tile_ref.shape[1]]
    send_ref[:, tile_ref.shape[1] :] = jnp.concatenate(turned, axis=0).astype(jnp.bfloat16)


def piece_product(step, z_ref, piece_ref):
    columns = z_ref.shape[0] // 2
    depth = piece_ref.shape[1]
    owner = lax.axis_index("rhs") ^ step
    rows = z_ref[:, pl.ds(pl.multiple_of(owner * depth, 128), depth)]
    real_acc = jnp.dot(rows, piece_ref[0], preferred_element_type=jnp.float32)
    imag_acc = jnp.dot(rows, piece_ref[1], preferred_element_type=jnp.float32)
    return real_acc[:columns] - imag_acc[columns:], imag_acc[:columns] + real_acc[columns:]


def leaf_kernel(step, z_ref, piece_ref, _, out_ref):
    product = piece_product(step, z_ref, piece_ref)
    for part in range(2):
        out_ref[part] = product[part]


def prepare_kernel(low_start, live_ref, targets_ref, low_ref, _, panel_ref, pick_ref, kept_ref):
    for level in range(targets_ref.shape[0]):
        for block in range(targets_ref.shape[1]):
            kept_ref[level, block] = targets_ref[level, block]
    depth, devices = targets_ref.shape
    width, leaf_rows = low_ref.shape[1:]
    slab = 2 * width
    device = lax.axis_index("leaf")
    live = lax.broadcasted_iota(jnp.int32, (1, leaf_rows), 1) < live_ref[0] * 128
    low = [jnp.where(live, low_ref[part].astype(jnp.float32), 0.0) for part in range(2)]
    rows = jnp.concatenate(
        [
            jnp.concatenate([low[0], low[1]], axis=1),
            jnp.concatenate([low[1], -low[0]], axis=1),
        ],
        axis=0,
    ).astype(jnp.bfloat16)
    panel_ref[...] = jnp.zeros_like(panel_ref)
    panel_ref[pl.ds(pl.multiple_of(device * slab, slab), slab), :] = rows
    size = devices * slab
    row = lax.broadcasted_iota(jnp.int32, (size, size), 0)
    lane_row = lax.broadcasted_iota(jnp.int32, (1, size), 1)
    for level in range(1, depth + 1):
        offset = width * (2**level - 2) + lane_row % width
        inverse_offset = lane_row % width if level == depth else offset + width * devices
        target_lane = jnp.zeros((1, size), jnp.int32)
        for block in range(devices):
            target_lane = jnp.where(lane_row // slab == block, targets_ref[level - 1, block], target_lane)
        pick_ref[level - 1] = jnp.where(row == inverse_offset + target_lane * width, 1.0, 0.0).astype(
            jnp.bfloat16
        )
        if level == depth:
            pick_ref[2 * depth - 1] = jnp.where(
                row == size // 2 + inverse_offset + target_lane * width, 1.0, 0.0
            ).astype(jnp.bfloat16)
        if level < depth:
            own_lane = (lane_row // slab) % 2**level
            pick_ref[depth + level - 1] = jnp.where(
                row == low_start + offset + own_lane * width, 1.0, 0.0
            ).astype(jnp.bfloat16)


def join_first_kernel(own_ref, received_ref, pair_ref, out_ref, tile_ref):
    rows, lanes = own_ref.shape
    tile = pair_ref.shape[1]
    out_ref[:rows, :lanes] = own_ref[...]
    out_ref[rows:, :lanes] = received_ref[...]
    out_ref[:rows, lanes:] = pair_ref[...]
    out_ref[rows:, lanes:] = pair_ref[...]
    tile_ref[...] = received_ref[:, :tile]


def join_second_kernel(side_lanes, own_ref, first_ref, pair_ref, second_ref, _, out_ref, send_ref):
    rows, lanes = own_ref.shape
    tile = pair_ref.shape[1]
    out_ref[:rows, :] = own_ref[...]
    out_ref[rows : 2 * rows, :tile] = pair_ref[...]
    out_ref[rows : 2 * rows, tile:] = first_ref[:, tile:]
    lane = lax.broadcasted_iota(jnp.int32, (rows, tile), 1)
    merged = jnp.where(
        lane < side_lanes,
        second_ref[:rows, lanes:].astype(jnp.float32),
        second_ref[:rows, :tile].astype(jnp.float32),
    )
    out_ref[2 * rows : 3 * rows, :tile] = merged.astype(jnp.bfloat16)
    out_ref[2 * rows : 3 * rows, tile:] = second_ref[:rows, tile:lanes]
    out_ref[3 * rows :, :] = second_ref[rows:, :lanes]
    half = tile // 2
    send_ref[:rows, :] = own_ref[:, :tile]
    send_ref[rows : 2 * rows, :] = pair_ref[...]
    send_ref[2 * rows : 3 * rows, :] = merged.astype(jnp.bfloat16)
    send_ref[3 * rows : 4 * rows, :] = second_ref[rows:, :tile]
    send_ref[4 * rows : 5 * rows, :half] = own_ref[:, tile : tile + half]
    send_ref[4 * rows : 5 * rows, half:] = first_ref[:, tile + half :]
    send_ref[5 * rows :, :half] = second_ref[:rows, tile : tile + half]
    send_ref[5 * rows :, half:] = second_ref[rows:, tile + half : 2 * tile]


def far_kernel(step, z_ref, pair_z_ref, piece_ref, own_ref, out_ref, pair_out_ref):
    own_product, pair_product = [
        piece_product(step, source_ref, piece_ref) for source_ref in (z_ref, pair_z_ref)
    ]
    for part in range(2):
        out_ref[part] = own_ref[part] + own_product[part]
        pair_out_ref[part] = pair_product[part]


def owner(targets_ref, level, block):
    if level == 0:
        return jnp.int32(block)
    group = 2**level
    return block // group * group + targets_ref[level - 1, block]


def rows_of(targets_ref, level, source_ref, slab):
    device = lax.axis_index("leaf")
    return jnp.concatenate(
        [
            source_ref[
                pl.ds(pl.multiple_of((owner(targets_ref, level, block) ^ device) * slab, slab), slab), :
            ]
            for block in range(targets_ref.shape[1])
        ],
        axis=0,
    )


def side_of(raw, level, columns):
    size = raw.shape[0]
    row = lax.broadcasted_iota(jnp.int32, (columns, size), 0)
    lane = lax.broadcasted_iota(jnp.int32, (columns, size), 1)
    pick = jnp.where(lane == row + level * columns, 1.0, 0.0).astype(jnp.bfloat16)
    return times_transposed(pick, raw[:, :size])


def times_transposed(left, right):
    return lax.dot_general(left, right, (((1,), (1,)), ((), ())), preferred_element_type=jnp.float32)


def front_matrix(source, pick, level, slab):
    return front_of(jnp.dot(source, pick, preferred_element_type=jnp.float32), level, slab)


def front_of(plain, level, slab):
    size, width = plain.shape[0], slab // 2
    row = lax.broadcasted_iota(jnp.int32, (size, size), 0)
    lane = lax.broadcasted_iota(jnp.int32, (size, size), 1)
    swapped = plain.reshape(size // slab, 2, width, size)
    swapped = jnp.concatenate([swapped[:, 1:], swapped[:, :1]], axis=1).reshape(size, size)
    signed = jnp.where((row // width) % 2 == 0, plain, -plain)
    full = jnp.where((lane // width) % 2 == 0, signed, swapped)
    inside = row // (slab * 2**level) == lane // (slab * 2**level)
    return jnp.where(inside, full, 0.0).astype(jnp.bfloat16)


def conjugate(values_in, width):
    lane = lax.broadcasted_iota(jnp.int32, (1, values_in.shape[1]), 1)
    return jnp.where((lane // width) % 2 == 0, values_in, -values_in)


def near_kernel(targets_ref, near_ref, pick_ref, update_ref, partial_ref, lower_ref, kept_ref, all_ref):
    depth, devices = targets_ref.shape
    columns, size = update_ref.shape
    slab = size // devices
    half = size // 2
    for place_ref in (kept_ref, all_ref):
        place_ref[:half, :] = near_ref[...]
        for slot in range(1, devices // 2, 2):
            rows = slice(slot * slab, (slot + 1) * slab)
            turned = pltpu.roll(near_ref[rows, size:].astype(jnp.float32), half, 1)
            place_ref[rows, size:] = turned.astype(jnp.bfloat16)
    all_ref[half:, :] = jnp.zeros_like(near_ref)
    arriving = side_of(rows_of(targets_ref, 0, all_ref, slab), 0, columns)
    for level in range(1, depth):
        raw = rows_of(targets_ref, level, all_ref, slab)
        level_z = (side_of(raw, level, columns) - arriving).astype(jnp.bfloat16)
        inverse = front_matrix(raw[:, size:], pick_ref[level - 1], level, slab)
        lower = front_matrix(raw[:, :size], pick_ref[depth + level - 1], level, slab)
        lower_ref[level - 1] = lower
        partial_ref[level - 1] = jnp.dot(level_z, inverse, preferred_element_type=jnp.float32)
        arriving = jnp.dot(level_z, lower, preferred_element_type=jnp.float32)
    update_ref[...] = arriving


def operator_kernel(partial_ref, lower_ref, panel_ref, _, solved_ref, back_ref, leaf_ref, operator_ref):
    top, columns, size = partial_ref.shape
    width = size // 16
    known, operator = partial_ref[top - 1], lower_ref[top - 1]
    solved = {top: known}
    back_ref[top - 1] = operator
    for level in range(top - 1, 0, -1):
        parent = conjugate(known, width).astype(jnp.bfloat16)
        known = partial_ref[level - 1] - conjugate(times_transposed(parent, lower_ref[level - 1]), width)
        operator = -jnp.dot(lower_ref[level - 1], operator, preferred_element_type=jnp.float32)
        operator = operator.astype(jnp.bfloat16)
        solved[level] = known
        back_ref[level - 1] = operator
    stacked = [solved[level] for level in range(1, top + 1)]
    stacked.append(jnp.zeros((size - top * columns, size), jnp.float32))
    solved_ref[...] = jnp.concatenate(stacked, axis=0).T
    parent = conjugate(known, width).astype(jnp.bfloat16)
    leaf_ref[...] = jnp.dot(parent, panel_ref[...], preferred_element_type=jnp.float32)
    operator_ref[...] = lax.dot_general(
        operator, panel_ref[...], (((0,), (0,)), ((), ())), preferred_element_type=jnp.float32
    ).astype(jnp.bfloat16)


def top_kernel(
    targets_ref, near_ref, far_ref, pick_ref, update_ref, _, __, parent_ref, solved_ref, half_ref, all_ref
):
    depth, devices = targets_ref.shape
    columns, size = update_ref.shape
    slab = size // devices
    half = size // 2
    half_ref[:half, :] = jnp.zeros((half, size), jnp.bfloat16)
    half_ref[half:, :] = far_ref[:half]
    all_ref[:half, :] = near_ref[...]
    all_ref[half:, :size] = far_ref[:half]
    for slot in range(devices // 2):
        rows = slice(half + slot // 2 * slab, half + (slot // 2 + 1) * slab)
        all_ref[half + slot * slab : half + (slot + 1) * slab, size:] = far_ref[rows]
    raw = rows_of(targets_ref, depth, all_ref, slab)
    row_block = lax.broadcasted_iota(jnp.int32, (size, size), 0) // slab
    upper = jnp.zeros((size, size), jnp.int32)
    for block in range(devices):
        slot = owner(targets_ref, depth, block) ^ lax.axis_index("leaf")
        upper = jnp.where(row_block == block, slot, upper)
    plain = jnp.where(
        (upper >= devices // 2) & (upper % 2 == 1),
        jnp.dot(raw[:, size:], pick_ref[2 * depth - 1], preferred_element_type=jnp.float32),
        jnp.dot(raw[:, size:], pick_ref[depth - 1], preferred_element_type=jnp.float32),
    )
    inverse = front_of(plain, depth, slab)
    waiting = side_of(raw, depth, columns) - update_ref[...]
    arriving = side_of(rows_of(targets_ref, 0, half_ref, slab), 0, columns)
    for level in range(1, depth):
        raw = rows_of(targets_ref, level, half_ref, slab)
        level_z = (side_of(raw, level, columns) - arriving).astype(jnp.bfloat16)
        lower = front_matrix(raw, pick_ref[depth + level - 1], level, slab)
        arriving = jnp.dot(level_z, lower, preferred_element_type=jnp.float32)
    level_z = (waiting - arriving).astype(jnp.bfloat16)
    solved = jnp.dot(level_z, inverse, preferred_element_type=jnp.float32)
    solved_ref[...] = lax.dot_general(
        inverse, level_z, (((0,), (1,)), ((), ())), preferred_element_type=jnp.float32
    )
    parent_ref[...] = conjugate(solved, slab // 2).astype(jnp.bfloat16)


def finish_kernel(
    steps,
    live_ref,
    targets_ref,
    z_ref,
    partial_ref,
    parent_ref,
    top_ref,
    solved_ref,
    lower_ref,
    leaf_ref,
    operator_ref,
    far_ref,
    *refs,
):
    piece_refs, (leaf_out_ref, sep_out_ref) = refs[: len(steps)], refs[len(steps) : len(steps) + 2]
    leaf_place, sep_place, sems = refs[len(steps) + 2 :]
    depth, devices = targets_ref.shape
    columns, size = parent_ref.shape
    leaf_rows = leaf_place.shape[2]
    slab = size // devices
    width = slab // 2
    device = lax.axis_index("leaf")
    live = lax.broadcasted_iota(jnp.int32, (1, leaf_rows), 1) < live_ref[0] * 128
    parent = parent_ref[...]
    for level in range(1, depth + 1):
        place = jnp.int32(0)
        for block in range(devices):
            place = jnp.where(owner(targets_ref, level, block) == device, block, place)
        rows = pl.ds(pl.multiple_of(place * slab, slab), slab)
        if level < depth:
            known = solved_ref[rows, :][:, (level - 1) * columns : level * columns]
            change = times_transposed(lower_ref[level - 1, rows, :], parent)
            halves = known[:width] - change[:width], known[width:] + change[width:]
        else:
            solved = top_ref[rows, :]
            halves = solved[:width], solved[width:]
        for part in range(2):
            sep_place[part, level - 1] = halves[part]
    from_tree = leaf_ref[...] - jnp.dot(parent, operator_ref[...], preferred_element_type=jnp.float32)
    products = [piece_product(step, z_ref, piece_ref) for step, piece_ref in zip(steps, piece_refs)]
    copies = []
    for part in range(2):
        leaf_w = partial_ref[part] + far_ref[part] + sum(product[part] for product in products)
        leaf_place[part] = (
            jnp.where(live, leaf_w, 0.0) - from_tree[:, part * leaf_rows : (part + 1) * leaf_rows]
        )
        copies.append(pltpu.make_async_copy(leaf_place.at[part], leaf_out_ref.at[part], sems.at[part]))
        copies[-1].start()
    copies.append(pltpu.make_async_copy(sep_place, sep_out_ref, sems.at[2]))
    copies[-1].start()
    for copy in copies:
        copy.wait()


def whole(space):
    return pl.BlockSpec(memory_space=space)


def body(leaf_rhs, sep_rhs, leaf_inv, leaf_low, sep_inv, sep_low, leaf_live, targets):
    devices, parts = lax.axis_size("leaf"), lax.axis_size("rhs")
    columns, leaf_rows = leaf_rhs.shape[1:]
    width, depth = sep_inv.shape[1], sep_rhs.shape[2]
    slab = 2 * width
    size = devices * slab
    small_tree = (
        devices == 8 and parts % 2 == 0 and size == 128 and (1 + depth) * columns + sep_low.shape[2] <= 128 and sep_inv.shape[2] <= 128
    )
    panel = leaf_low.transpose(0, 2, 1)
    tree_rhs = sep_rhs.transpose(0, 2, 3, 1)

    if not small_tree:
        live_mask = (jnp.arange(leaf_rows) < leaf_live[0] * 128).astype(jnp.float32)
        leaf_z = (leaf_rhs * live_mask).astype(jnp.bfloat16)
        leaf_w = complex_dot(leaf_z, lax.all_gather(leaf_inv, "rhs", axis=1, tiled=True)) * live_mask
        return level_by_level(leaf_rhs, sep_rhs, leaf_w, leaf_low, sep_inv, sep_low, leaf_live, targets)

    tree_parts = (leaf_rhs, panel, tree_rhs, sep_inv, sep_low)
    first = pl.pallas_call(
        first_kernel,
        out_shape=pltpu.VMEM((8, 128), jnp.float32),
        out_specs=whole(VMEM),
        cost_estimate=pl.CostEstimate(flops=10**9, bytes_accessed=0, transcendentals=0),
    )()
    held, own_tile, sent, leaf_z = pl.pallas_call(
        pack_kernel,
        out_shape=(
            pltpu.VMEM((slab, 2 * size), jnp.bfloat16),
            pltpu.VMEM((slab, size), jnp.bfloat16),
            pltpu.VMEM((slab, 2 * size), jnp.bfloat16),
            pltpu.VMEM((2 * columns, leaf_rows), jnp.bfloat16),
        ),
        in_specs=[whole(SMEM)] + [whole(VMEM)] * 6,
        out_specs=(whole(VMEM),) * 4,
    )(leaf_live, *[in_vmem(part) for part in (first,) + tree_parts])

    def exchange(values_in, offset, flip):
        partners = [
            (source * parts + part, (source ^ offset) * parts + (part ^ flip))
            for source in range(devices)
            for part in range(parts)
        ]
        return lax.ppermute(values_in, ("leaf", "rhs"), partners)

    first_round = exchange(sent, 1, 1)
    pair_tile = xor_permute(own_tile, "rhs", 1)
    second_part, first_tile = pl.pallas_call(
        join_first_kernel,
        out_shape=(
            pltpu.VMEM((2 * slab, 3 * size), jnp.bfloat16),
            pltpu.VMEM((slab, size), jnp.bfloat16),
        ),
        in_specs=[whole(VMEM)] * 3,
        out_specs=(whole(VMEM),) * 2,
        cost_estimate=pl.CostEstimate(flops=10**11, bytes_accessed=0, transcendentals=0),
    )(*[in_vmem(ready) for ready in (held, first_round, pair_tile)])
    second_round = exchange(second_part, 2, 1)
    panel_rows, picks, kept_targets = pl.pallas_call(
        functools.partial(prepare_kernel, (1 + depth) * columns),
        out_shape=(
            pltpu.VMEM((size, 2 * leaf_rows), jnp.bfloat16),
            pltpu.VMEM((2 * depth, size, size), jnp.bfloat16),
            pltpu.SMEM(targets.shape, jnp.int32),
        ),
        in_specs=[whole(SMEM), whole(SMEM), whole(VMEM), whole(VMEM)],
        out_specs=(whole(VMEM),) * 2 + (whole(SMEM),),
        cost_estimate=pl.CostEstimate(flops=0, bytes_accessed=0, transcendentals=0),
    )(leaf_live, targets, panel, in_vmem(first_tile))

    pair_first = xor_permute(first_tile, "rhs", 1)
    held, sent = pl.pallas_call(
        functools.partial(join_second_kernel, (1 + depth) * columns),
        out_shape=(
            pltpu.VMEM((4 * slab, 2 * size), jnp.bfloat16),
            pltpu.VMEM((6 * slab, size), jnp.bfloat16),
        ),
        in_specs=[whole(VMEM)] * 5,
        out_specs=(whole(VMEM),) * 2,
        cost_estimate=pl.CostEstimate(flops=0, bytes_accessed=0, transcendentals=0),
    )(*[in_vmem(ready) for ready in (held, first_round, pair_first, second_round, picks)])
    far = exchange(sent, 4, 0)

    kept_targets = pltpu.with_memory_space_constraint(kept_targets, SMEM)
    update, partial_x, lower, kept_near = pl.pallas_call(
        near_kernel,
        out_shape=(
            pltpu.VMEM((columns, size), jnp.float32),
            pltpu.VMEM((depth - 1, columns, size), jnp.float32),
            pltpu.VMEM((depth - 1, size, size), jnp.bfloat16),
            pltpu.VMEM((size // 2, 2 * size), jnp.bfloat16),
        ),
        in_specs=[whole(SMEM)] + [whole(VMEM)] * 2,
        out_specs=(whole(VMEM),) * 4,
        scratch_shapes=[pltpu.VMEM((size, 2 * size), jnp.bfloat16)],
        cost_estimate=pl.CostEstimate(flops=0, bytes_accessed=0, transcendentals=0),
    )(kept_targets, *[in_vmem(ready) for ready in (held, picks)])
    own_part = pl.pallas_call(
        functools.partial(leaf_kernel, 0),
        out_shape=pltpu.VMEM((2, columns, leaf_rows), jnp.float32),
        in_specs=[whole(VMEM)] * 3,
        out_specs=whole(VMEM),
        cost_estimate=pl.CostEstimate(flops=0, bytes_accessed=0, transcendentals=0),
    )(*[in_vmem(ready) for ready in (leaf_z, leaf_inv, update)])
    partial, pair_far = pl.pallas_call(
        functools.partial(far_kernel, 3),
        out_shape=(pltpu.VMEM((2, columns, leaf_rows), jnp.float32),) * 2,
        in_specs=[whole(VMEM)] * 4,
        out_specs=(whole(VMEM),) * 2,
        cost_estimate=pl.CostEstimate(flops=0, bytes_accessed=0, transcendentals=0),
    )(
        *[
            in_vmem(ready)
            for ready in (leaf_z, xor_permute(leaf_z, "rhs", 1), xor_permute(leaf_inv, "rhs", 3), own_part)
        ]
    )
    known, back, known_leaf, operator = pl.pallas_call(
        operator_kernel,
        out_shape=(
            pltpu.VMEM((size, size), jnp.float32),
            pltpu.VMEM((depth - 1, size, size), jnp.bfloat16),
            pltpu.VMEM((columns, 2 * leaf_rows), jnp.float32),
            pltpu.VMEM((size, 2 * leaf_rows), jnp.bfloat16),
        ),
        in_specs=[whole(VMEM)] * 4,
        out_specs=(whole(VMEM),) * 4,
        cost_estimate=pl.CostEstimate(flops=0, bytes_accessed=0, transcendentals=0),
    )(*[in_vmem(ready) for ready in (partial_x, lower, panel_rows, partial)])
    parent_x, top_x = pl.pallas_call(
        top_kernel,
        out_shape=(
            pltpu.VMEM((columns, size), jnp.bfloat16),
            pltpu.VMEM((size, columns), jnp.float32),
        ),
        in_specs=[whole(SMEM)] + [whole(VMEM)] * 6,
        out_specs=(whole(VMEM),) * 2,
        scratch_shapes=[
            pltpu.VMEM((size, size), jnp.bfloat16),
            pltpu.VMEM((size, 2 * size), jnp.bfloat16),
        ],
        cost_estimate=pl.CostEstimate(flops=3 * 10**9, bytes_accessed=0, transcendentals=0),
    )(kept_targets, *[in_vmem(ready) for ready in (kept_near, far, picks, update, partial, known_leaf)])
    pair_parts = (xor_permute(pair_far, "rhs", 1), xor_permute(leaf_inv, "rhs", 1))
    leaf_x, sep_x = pl.pallas_call(
        functools.partial(finish_kernel, (1,)),
        out_shape=(
            jax.ShapeDtypeStruct((2, columns, leaf_rows), jnp.float32),
            jax.ShapeDtypeStruct((2, depth, width, columns), jnp.float32),
        ),
        in_specs=[whole(SMEM)] * 2 + [whole(VMEM)] * 10,
        out_specs=(whole(pl.ANY),) * 2,
        scratch_shapes=[
            pltpu.VMEM((2, columns, leaf_rows), jnp.float32),
            pltpu.VMEM((2, depth, width, columns), jnp.float32),
            pltpu.SemaphoreType.DMA((3,)),
        ],
    )(
        leaf_live,
        kept_targets,
        *[
            in_vmem(ready)
            for ready in (leaf_z, partial, parent_x, top_x, known, back, known_leaf, operator) + pair_parts
        ],
    )
    return leaf_x, sep_x.transpose(0, 3, 1, 2)


def solution(mesh):
    placed = (
        P(None, "rhs", "leaf"),
        P(None, "rhs", None, "leaf"),
        P(None, "rhs", "leaf"),
        P(None, None, "leaf"),
        P(None, None, "leaf"),
        P(None, None, "leaf"),
        P("leaf"),
        P(),
    )
    return jax.shard_map(
        body,
        mesh=mesh,
        in_specs=placed,
        out_specs=(P(None, "rhs", "leaf"), P(None, "rhs", None, "leaf")),
        check_vma=False,
    )
```

```python
import functools

import jax
import jax.numpy as jnp
from jax import lax
from jax.experimental import pallas as pl
from jax.experimental.pallas import tpu as pltpu
from jax.sharding import PartitionSpec as P

exact_mode = lax.Precision.HIGHEST
VMEM = pltpu.MemorySpace.VMEM
SMEM = pltpu.MemorySpace.SMEM


def complex_dot(operand, factor):
    row_count = operand.shape[1]
    stacked = jnp.concatenate([operand[0], operand[1]], axis=0)
    real_acc = jnp.dot(stacked, factor[0], preferred_element_type=jnp.float32)
    imag_acc = jnp.dot(stacked, factor[1], preferred_element_type=jnp.float32)
    return jnp.stack(
        [real_acc[:row_count] - imag_acc[row_count:], imag_acc[:row_count] + real_acc[row_count:]]
    )


def complex_dot_back(operand, factor):
    row_count = operand.shape[1]
    stacked = jnp.concatenate([operand[0], operand[1]], axis=0)
    contract = (((1,), (1,)), ((), ()))
    real_acc = lax.dot_general(stacked, factor[0], contract, preferred_element_type=jnp.float32)
    imag_acc = lax.dot_general(stacked, factor[1], contract, preferred_element_type=jnp.float32)
    return jnp.stack(
        [real_acc[:row_count] - imag_acc[row_count:], imag_acc[:row_count] + real_acc[row_count:]]
    )


def to_blocks(values_in, group_size):
    return (
        values_in.reshape(2, values_in.shape[1], group_size, -1)
        .transpose(2, 0, 1, 3)
        .reshape(group_size, -1)
    )


def from_blocks(blocks, columns):
    group_size = blocks.shape[0]
    return blocks.reshape(group_size, 2, columns, -1).transpose(1, 2, 0, 3).reshape(2, columns, -1)


def selector(dest_index, total_slots):
    return (dest_index[:, None] == jnp.arange(total_slots, dtype=jnp.int32)[None, :]).astype(
        jnp.float32
    )


def exchange_sum(blocks, global_dest, devices):
    routed = jnp.dot(selector(global_dest, devices).T, blocks, precision=exact_mode)
    received = lax.all_to_all(
        routed.astype(jnp.bfloat16), "leaf", split_axis=0, concat_axis=0, tiled=True
    ).astype(routed.dtype)
    return jnp.sum(received, axis=0)


def collect(blocks, local_dest, level_bits, device, devices):
    group_start = device >> level_bits << level_bits
    return exchange_sum(blocks, group_start + local_dest, devices)


def spread(own_block, level_bits, device, devices):
    group_size = 2**level_bits
    group_start = device >> level_bits << level_bits
    slot_index = jnp.arange(devices, dtype=jnp.int32)[:, None]
    inside = (slot_index >= group_start) & (slot_index < group_start + group_size)
    routed = jnp.where(inside, own_block[None, :], jnp.zeros_like(own_block)[None, :])
    received = lax.all_to_all(routed, "leaf", split_axis=0, concat_axis=0, tiled=True)
    return lax.dynamic_slice_in_dim(received, group_start, group_size, 0)


def level_by_level(leaf_rhs, sep_rhs, leaf_w, leaf_low, sep_inv, sep_low, leaf_live, targets):
    devices = lax.axis_size("leaf")
    tree_depth = devices.bit_length() - 1
    device = lax.axis_index("leaf")
    leaf_rows = leaf_low.shape[1]
    sep_width = sep_inv.shape[1]
    columns = leaf_rhs.shape[1]
    live_mask = (jnp.arange(leaf_rows) < leaf_live[0] * 128).astype(jnp.float32)
    leaf_z = (leaf_rhs * live_mask).astype(jnp.bfloat16)
    first_dest = lax.dynamic_slice_in_dim(targets[0], device, 1)
    arriving = collect(complex_dot(leaf_z, leaf_low).reshape(1, -1), first_dest, 1, device, devices)
    solved_w = []
    for level_now in range(1, tree_depth + 1):
        group_size = 2**level_now
        offset = sep_width * (group_size - 2)
        level_z = (
            sep_rhs[:, :, level_now - 1, :] - arriving.reshape(2, columns, sep_width)
        ).astype(jnp.bfloat16)
        inv_rows = sep_inv[:, :, offset : offset + sep_width * group_size]
        own_w = collect(
            to_blocks(complex_dot(level_z, inv_rows), group_size),
            jnp.arange(group_size, dtype=jnp.int32),
            level_now,
            device,
            devices,
        )
        solved_w.append(own_w.reshape(2, columns, sep_width))
        if level_now < tree_depth:
            low_rows = sep_low[:, :, offset : offset + sep_width * group_size]
            group_start = device >> level_now << level_now
            dest_index = lax.dynamic_slice_in_dim(targets[level_now], group_start, group_size)
            arriving = collect(
                to_blocks(complex_dot(level_z, low_rows), group_size),
                dest_index,
                level_now + 1,
                device,
                devices,
            )
    solved_x = [solved_w[level_now] for level_now in range(tree_depth)]
    for level_now in range(tree_depth - 1, 0, -1):
        group_size = 2**level_now
        offset = sep_width * (group_size - 2)
        low_rows = sep_low[:, :, offset : offset + sep_width * group_size]
        parent_x = spread(
            solved_x[level_now].astype(jnp.bfloat16).reshape(-1), level_now + 1, device, devices
        )
        group_start = device >> level_now << level_now
        dest_index = lax.dynamic_slice_in_dim(targets[level_now], group_start, group_size)
        picked = jnp.dot(
            selector(dest_index, 2 * group_size).astype(jnp.bfloat16),
            parent_x,
            preferred_element_type=jnp.float32,
        ).astype(jnp.bfloat16)
        solved_x[level_now - 1] = solved_w[level_now - 1] - complex_dot_back(
            from_blocks(picked, columns), low_rows
        )
    parent_x = spread(solved_x[0].astype(jnp.bfloat16).reshape(-1), 1, device, devices)
    picked = jnp.dot(
        selector(first_dest, 2).astype(jnp.bfloat16), parent_x, preferred_element_type=jnp.float32
    ).astype(jnp.bfloat16)
    leaf_x = (
        leaf_w - complex_dot_back(picked.reshape(2, columns, sep_width), leaf_low)
    ) * live_mask
    return leaf_x, jnp.stack(solved_x, axis=2)


def xor_permute(values_in, axis, offset):
    count = lax.axis_size(axis)
    return lax.ppermute(values_in, axis, [(source, source ^ offset) for source in range(count)])


def in_vmem(values_in):
    return pltpu.with_memory_space_constraint(values_in, VMEM)


def masked_rows(leaf_rhs, live_ref):
    rows = leaf_rhs.shape[2]
    live = lax.broadcasted_iota(jnp.int32, (1, rows), 1) < live_ref[0] * 128
    stacked = jnp.concatenate([leaf_rhs[0], leaf_rhs[1]], axis=0)
    return jnp.where(live, stacked, 0.0).astype(jnp.bfloat16), live


def first_kernel(out_ref):
    out_ref[...] = jnp.zeros_like(out_ref)


def pack_kernel(live_ref, _, leaf_rhs_ref, low_ref, rhs_ref, inv_ref, sep_low_ref, out_ref, tile_ref, send_ref, z_ref):
    columns = leaf_rhs_ref.shape[1]
    depth = rhs_ref.shape[1]
    leaf_z, _ = masked_rows(leaf_rhs_ref[...], live_ref)
    z_ref[...] = leaf_z
    panel = jnp.concatenate([low_ref[0], low_ref[1]], axis=0)
    product = lax.dot_general(
        panel, leaf_z, (((1,), (1,)), ((), ())), preferred_element_type=jnp.float32
    )
    width = low_ref.shape[1]
    update = [
        product[:width, :columns] - product[width:, columns:],
        product[width:, :columns] + product[:width, columns:],
    ]
    used = (1 + depth) * columns + sep_low_ref.shape[2]
    halves, turned = [], []
    for part in range(2):
        pieces = [update[part]] + [rhs_ref[part, level] for level in range(depth)]
        pieces.append(sep_low_ref[part].astype(jnp.float32))
        if used < 128:
            pieces.append(jnp.zeros((width, 128 - used), jnp.float32))
        inverse = inv_ref[part].astype(jnp.float32)
        below = width * (2**depth - 2)
        gap = jnp.zeros((width, 128 - inverse.shape[1]), jnp.float32)
        pieces += [inverse[:, below:], inverse[:, :below], gap]
        turned.append(jnp.concatenate([inverse[:, :below], gap, inverse[:, below:]], axis=1))
        halves.append(jnp.concatenate(pieces, axis=1))
    packed = jnp.concatenate(halves, axis=0).astype(jnp.bfloat16)
    out_ref[...] = packed
    tile_ref[...] = packed[:, : tile_ref.shape[1]]
    send_ref[:, : tile_ref.shape[1]] = packed[:, : tile_ref.shape[1]]
    send_ref[:, tile_ref.shape[1] :] = jnp.concatenate(turned, axis=0).astype(jnp.bfloat16)


def piece_product(step, z_ref, piece_ref):
    columns = z_ref.shape[0] // 2
    depth = piece_ref.shape[1]
    owner = lax.axis_index("rhs") ^ step
    rows = z_ref[:, pl.ds(pl.multiple_of(owner * depth, 128), depth)]
    real_acc = jnp.dot(rows, piece_ref[0], preferred_element_type=jnp.float32)
    imag_acc = jnp.dot(rows, piece_ref[1], preferred_element_type=jnp.float32)
    return real_acc[:columns] - imag_acc[columns:], imag_acc[:columns] + real_acc[columns:]


def leaf_kernel(step, z_ref, piece_ref, _, out_ref):
    product = piece_product(step, z_ref, piece_ref)
    for part in range(2):
        out_ref[part] = product[part]


def prepare_kernel(low_start, live_ref, targets_ref, low_ref, _, panel_ref, pick_ref, kept_ref):
    for level in range(targets_ref.shape[0]):
        for block in range(targets_ref.shape[1]):
            kept_ref[level, block] = targets_ref[level, block]
    depth, devices = targets_ref.shape
    width, leaf_rows = low_ref.shape[1:]
    slab = 2 * width
    live = lax.broadcasted_iota(jnp.int32, (1, leaf_rows), 1) < live_ref[0] * 128
    low = [jnp.where(live, low_ref[part].astype(jnp.float32), 0.0) for part in range(2)]
    rows = jnp.concatenate(
        [
            jnp.concatenate([low[0], low[1]], axis=1),
            jnp.concatenate([low[1], -low[0]], axis=1),
        ],
        axis=0,
    ).astype(jnp.bfloat16)
    panel_ref[...] = rows
    size = devices * slab
    row = lax.broadcasted_iota(jnp.int32, (size, size), 0)
    lane_row = lax.broadcasted_iota(jnp.int32, (1, size), 1)
    for level in range(1, depth + 1):
        offset = width * (2**level - 2) + lane_row % width
        inverse_offset = lane_row % width if level == depth else offset + width * devices
        target_lane = jnp.zeros((1, size), jnp.int32)
        for block in range(devices):
            target_lane = jnp.where(lane_row // slab == block, targets_ref[level - 1, block], target_lane)
        pick_ref[level - 1] = jnp.where(row == inverse_offset + target_lane * width, 1.0, 0.0).astype(
            jnp.bfloat16
        )
        if level == depth:
            pick_ref[2 * depth - 1] = jnp.where(
                row == size // 2 + inverse_offset + target_lane * width, 1.0, 0.0
            ).astype(jnp.bfloat16)
        if level < depth:
            own_lane = (lane_row // slab) % 2**level
            pick_ref[depth + level - 1] = jnp.where(
                row == low_start + offset + own_lane * width, 1.0, 0.0
            ).astype(jnp.bfloat16)


def join_first_kernel(own_ref, received_ref, pair_ref, out_ref, tile_ref):
    rows, lanes = own_ref.shape
    tile = pair_ref.shape[1]
    out_ref[:rows, :lanes] = own_ref[...]
    out_ref[rows:, :lanes] = received_ref[...]
    out_ref[:rows, lanes:] = pair_ref[...]
    out_ref[rows:, lanes:] = pair_ref[...]
    tile_ref[...] = received_ref[:, :tile]


def join_second_kernel(side_lanes, own_ref, first_ref, pair_ref, second_ref, _, out_ref, send_ref):
    rows, lanes = own_ref.shape
    tile = pair_ref.shape[1]
    out_ref[:rows, :] = own_ref[...]
    out_ref[rows : 2 * rows, :tile] = pair_ref[...]
    out_ref[rows : 2 * rows, tile:] = first_ref[:, tile:]
    lane = lax.broadcasted_iota(jnp.int32, (rows, tile), 1)
    merged = jnp.where(
        lane < side_lanes,
        second_ref[:rows, lanes:].astype(jnp.float32),
        second_ref[:rows, :tile].astype(jnp.float32),
    )
    out_ref[2 * rows : 3 * rows, :tile] = merged.astype(jnp.bfloat16)
    out_ref[2 * rows : 3 * rows, tile:] = second_ref[:rows, tile:lanes]
    out_ref[3 * rows :, :] = second_ref[rows:, :lanes]
    half = tile // 2
    send_ref[:rows, :] = own_ref[:, :tile]
    send_ref[rows : 2 * rows, :] = pair_ref[...]
    send_ref[2 * rows : 3 * rows, :] = merged.astype(jnp.bfloat16)
    send_ref[3 * rows : 4 * rows, :] = second_ref[rows:, :tile]
    send_ref[4 * rows : 5 * rows, :half] = own_ref[:, tile : tile + half]
    send_ref[4 * rows : 5 * rows, half:] = first_ref[:, tile + half :]
    send_ref[5 * rows :, :half] = second_ref[:rows, tile : tile + half]
    send_ref[5 * rows :, half:] = second_ref[rows:, tile + half : 2 * tile]


def far_kernel(step, z_ref, pair_z_ref, piece_ref, own_ref, out_ref, pair_out_ref):
    own_product, pair_product = [
        piece_product(step, source_ref, piece_ref) for source_ref in (z_ref, pair_z_ref)
    ]
    for part in range(2):
        out_ref[part] = own_ref[part] + own_product[part]
        pair_out_ref[part] = pair_product[part]


def owner(targets_ref, level, block):
    if level == 0:
        return jnp.int32(block)
    group = 2**level
    return block // group * group + targets_ref[level - 1, block]


def rows_of(targets_ref, level, source_ref, slab):
    device = lax.axis_index("leaf")
    return jnp.concatenate(
        [
            source_ref[
                pl.ds(pl.multiple_of((owner(targets_ref, level, block) ^ device) * slab, slab), slab), :
            ]
            for block in range(targets_ref.shape[1])
        ],
        axis=0,
    )


def side_of(raw, level, columns):
    size = raw.shape[0]
    row = lax.broadcasted_iota(jnp.int32, (columns, size), 0)
    lane = lax.broadcasted_iota(jnp.int32, (columns, size), 1)
    pick = jnp.where(lane == row + level * columns, 1.0, 0.0).astype(jnp.bfloat16)
    return times_transposed(pick, raw[:, :size])


def times_transposed(left, right):
    return lax.dot_general(left, right, (((1,), (1,)), ((), ())), preferred_element_type=jnp.float32)


def front_matrix(source, pick, level, slab):
    return front_of(jnp.dot(source, pick, preferred_element_type=jnp.float32), level, slab)


def front_of(plain, level, slab):
    size, width = plain.shape[0], slab // 2
    row = lax.broadcasted_iota(jnp.int32, (size, size), 0)
    lane = lax.broadcasted_iota(jnp.int32, (size, size), 1)
    swapped = plain.reshape(size // slab, 2, width, size)
    swapped = jnp.concatenate([swapped[:, 1:], swapped[:, :1]], axis=1).reshape(size, size)
    signed = jnp.where((row // width) % 2 == 0, plain, -plain)
    full = jnp.where((lane // width) % 2 == 0, signed, swapped)
    inside = row // (slab * 2**level) == lane // (slab * 2**level)
    return jnp.where(inside, full, 0.0).astype(jnp.bfloat16)


def conjugate(values_in, width):
    lane = lax.broadcasted_iota(jnp.int32, (1, values_in.shape[1]), 1)
    return jnp.where((lane // width) % 2 == 0, values_in, -values_in)


def near_kernel(targets_ref, near_ref, pick_ref, update_ref, partial_ref, lower_ref, kept_ref, all_ref):
    depth, devices = targets_ref.shape
    columns, size = update_ref.shape
    slab = size // devices
    half = size // 2
    for place_ref in (kept_ref, all_ref):
        place_ref[:half, :] = near_ref[...]
        for slot in range(1, devices // 2, 2):
            rows = slice(slot * slab, (slot + 1) * slab)
            turned = pltpu.roll(near_ref[rows, size:].astype(jnp.float32), half, 1)
            place_ref[rows, size:] = turned.astype(jnp.bfloat16)
    all_ref[half:, :] = jnp.zeros_like(near_ref)
    arriving = side_of(rows_of(targets_ref, 0, all_ref, slab), 0, columns)
    for level in range(1, depth):
        raw = rows_of(targets_ref, level, all_ref, slab)
        level_z = (side_of(raw, level, columns) - arriving).astype(jnp.bfloat16)
        inverse = front_matrix(raw[:, size:], pick_ref[level - 1], level, slab)
        lower = front_matrix(raw[:, :size], pick_ref[depth + level - 1], level, slab)
        lower_ref[level - 1] = lower
        partial_ref[level - 1] = jnp.dot(level_z, inverse, preferred_element_type=jnp.float32)
        arriving = jnp.dot(level_z, lower, preferred_element_type=jnp.float32)
    update_ref[...] = arriving


def operator_kernel(partial_ref, lower_ref, panel_ref, _, solved_ref, back_ref, leaf_ref, operator_ref):
    top, columns, size = partial_ref.shape
    width = size // 16
    known, operator = partial_ref[top - 1], lower_ref[top - 1]
    solved = {top: known}
    back_ref[top - 1] = operator
    for level in range(top - 1, 0, -1):
        parent = conjugate(known, width).astype(jnp.bfloat16)
        known = partial_ref[level - 1] - conjugate(times_transposed(parent, lower_ref[level - 1]), width)
        operator = -jnp.dot(lower_ref[level - 1], operator, preferred_element_type=jnp.float32)
        operator = operator.astype(jnp.bfloat16)
        solved[level] = known
        back_ref[level - 1] = operator
    stacked = [solved[level] for level in range(1, top + 1)]
    stacked.append(jnp.zeros((size - top * columns, size), jnp.float32))
    solved_ref[...] = jnp.concatenate(stacked, axis=0).T
    slab = 2 * width
    rows = pl.ds(pl.multiple_of(lax.axis_index("leaf") * slab, slab), slab)
    own = solved_ref[rows, :][:, :columns]
    own = jnp.concatenate([own[:width], -own[width:]], axis=0).astype(jnp.bfloat16)
    first = (((0,), (0,)), ((), ()))
    leaf_ref[...] = lax.dot_general(own, panel_ref[...], first, preferred_element_type=jnp.float32)
    operator_ref[...] = lax.dot_general(
        back_ref[0, rows, :], panel_ref[...], first, preferred_element_type=jnp.float32
    ).astype(jnp.bfloat16)


def top_kernel(
    targets_ref, near_ref, far_ref, pick_ref, update_ref, _, __, parent_ref, solved_ref, half_ref, all_ref
):
    depth, devices = targets_ref.shape
    columns, size = update_ref.shape
    slab = size // devices
    half = size // 2
    half_ref[:half, :] = jnp.zeros((half, size), jnp.bfloat16)
    half_ref[half:, :] = far_ref[:half]
    all_ref[:half, :] = near_ref[...]
    all_ref[half:, :size] = far_ref[:half]
    for slot in range(devices // 2):
        rows = slice(half + slot // 2 * slab, half + (slot // 2 + 1) * slab)
        all_ref[half + slot * slab : half + (slot + 1) * slab, size:] = far_ref[rows]
    raw = rows_of(targets_ref, depth, all_ref, slab)
    row_block = lax.broadcasted_iota(jnp.int32, (size, size), 0) // slab
    upper = jnp.zeros((size, size), jnp.int32)
    for block in range(devices):
        slot = owner(targets_ref, depth, block) ^ lax.axis_index("leaf")
        upper = jnp.where(row_block == block, slot, upper)
    plain = jnp.where(
        (upper >= devices // 2) & (upper % 2 == 1),
        jnp.dot(raw[:, size:], pick_ref[2 * depth - 1], preferred_element_type=jnp.float32),
        jnp.dot(raw[:, size:], pick_ref[depth - 1], preferred_element_type=jnp.float32),
    )
    inverse = front_of(plain, depth, slab)
    waiting = side_of(raw, depth, columns) - update_ref[...]
    arriving = side_of(rows_of(targets_ref, 0, half_ref, slab), 0, columns)
    for level in range(1, depth):
        raw = rows_of(targets_ref, level, half_ref, slab)
        level_z = (side_of(raw, level, columns) - arriving).astype(jnp.bfloat16)
        lower = front_matrix(raw, pick_ref[depth + level - 1], level, slab)
        arriving = jnp.dot(level_z, lower, preferred_element_type=jnp.float32)
    level_z = (waiting - arriving).astype(jnp.bfloat16)
    solved = jnp.dot(level_z, inverse, preferred_element_type=jnp.float32)
    solved_ref[...] = lax.dot_general(
        inverse, level_z, (((0,), (1,)), ((), ())), preferred_element_type=jnp.float32
    )
    parent_ref[...] = conjugate(solved, slab // 2).astype(jnp.bfloat16)


def finish_kernel(
    steps,
    live_ref,
    targets_ref,
    z_ref,
    partial_ref,
    parent_ref,
    top_ref,
    solved_ref,
    lower_ref,
    leaf_ref,
    operator_ref,
    far_ref,
    *refs,
):
    piece_refs, (leaf_out_ref, sep_out_ref) = refs[: len(steps)], refs[len(steps) : len(steps) + 2]
    leaf_place, sep_place, sems = refs[len(steps) + 2 :]
    depth, devices = targets_ref.shape
    columns, size = parent_ref.shape
    leaf_rows = leaf_place.shape[2]
    slab = size // devices
    width = slab // 2
    device = lax.axis_index("leaf")
    live = lax.broadcasted_iota(jnp.int32, (1, leaf_rows), 1) < live_ref[0] * 128
    parent = parent_ref[...]
    for level in range(1, depth + 1):
        place = jnp.int32(0)
        for block in range(devices):
            place = jnp.where(owner(targets_ref, level, block) == device, block, place)
        rows = pl.ds(pl.multiple_of(place * slab, slab), slab)
        if level < depth:
            known = solved_ref[rows, :][:, (level - 1) * columns : level * columns]
            change = times_transposed(lower_ref[level - 1, rows, :], parent)
            halves = known[:width] - change[:width], known[width:] + change[width:]
        else:
            solved = top_ref[rows, :]
            halves = solved[:width], solved[width:]
        for part in range(2):
            sep_place[part, level - 1] = halves[part]
    from_tree = leaf_ref[...] - jnp.dot(parent, operator_ref[...], preferred_element_type=jnp.float32)
    products = [piece_product(step, z_ref, piece_ref) for step, piece_ref in zip(steps, piece_refs)]
    copies = []
    for part in range(2):
        leaf_w = partial_ref[part] + far_ref[part] + sum(product[part] for product in products)
        leaf_place[part] = (
            jnp.where(live, leaf_w, 0.0) - from_tree[:, part * leaf_rows : (part + 1) * leaf_rows]
        )
        copies.append(pltpu.make_async_copy(leaf_place.at[part], leaf_out_ref.at[part], sems.at[part]))
        copies[-1].start()
    copies.append(pltpu.make_async_copy(sep_place, sep_out_ref, sems.at[2]))
    copies[-1].start()
    for copy in copies:
        copy.wait()


def whole(space):
    return pl.BlockSpec(memory_space=space)


def body(leaf_rhs, sep_rhs, leaf_inv, leaf_low, sep_inv, sep_low, leaf_live, targets):
    devices, parts = lax.axis_size("leaf"), lax.axis_size("rhs")
    columns, leaf_rows = leaf_rhs.shape[1:]
    width, depth = sep_inv.shape[1], sep_rhs.shape[2]
    slab = 2 * width
    size = devices * slab
    small_tree = (
        devices == 8 and parts % 2 == 0 and size == 128 and (1 + depth) * columns + sep_low.shape[2] <= 128 and sep_inv.shape[2] <= 128
    )
    panel = leaf_low.transpose(0, 2, 1)
    tree_rhs = sep_rhs.transpose(0, 2, 3, 1)

    if not small_tree:
        live_mask = (jnp.arange(leaf_rows) < leaf_live[0] * 128).astype(jnp.float32)
        leaf_z = (leaf_rhs * live_mask).astype(jnp.bfloat16)
        leaf_w = complex_dot(leaf_z, lax.all_gather(leaf_inv, "rhs", axis=1, tiled=True)) * live_mask
        return level_by_level(leaf_rhs, sep_rhs, leaf_w, leaf_low, sep_inv, sep_low, leaf_live, targets)

    tree_parts = (leaf_rhs, panel, tree_rhs, sep_inv, sep_low)
    first = pl.pallas_call(
        first_kernel,
        out_shape=pltpu.VMEM((8, 128), jnp.float32),
        out_specs=whole(VMEM),
        cost_estimate=pl.CostEstimate(flops=10**9, bytes_accessed=0, transcendentals=0),
    )()
    held, own_tile, sent, leaf_z = pl.pallas_call(
        pack_kernel,
        out_shape=(
            pltpu.VMEM((slab, 2 * size), jnp.bfloat16),
            pltpu.VMEM((slab, size), jnp.bfloat16),
            pltpu.VMEM((slab, 2 * size), jnp.bfloat16),
            pltpu.VMEM((2 * columns, leaf_rows), jnp.bfloat16),
        ),
        in_specs=[whole(SMEM)] + [whole(VMEM)] * 6,
        out_specs=(whole(VMEM),) * 4,
    )(leaf_live, *[in_vmem(part) for part in (first,) + tree_parts])

    def exchange(values_in, offset, flip):
        partners = [
            (source * parts + part, (source ^ offset) * parts + (part ^ flip))
            for source in range(devices)
            for part in range(parts)
        ]
        return lax.ppermute(values_in, ("leaf", "rhs"), partners)

    first_round = exchange(sent, 1, 1)
    pair_tile = xor_permute(own_tile, "rhs", 1)
    second_part, first_tile = pl.pallas_call(
        join_first_kernel,
        out_shape=(
            pltpu.VMEM((2 * slab, 3 * size), jnp.bfloat16),
            pltpu.VMEM((slab, size), jnp.bfloat16),
        ),
        in_specs=[whole(VMEM)] * 3,
        out_specs=(whole(VMEM),) * 2,
        cost_estimate=pl.CostEstimate(flops=10**11, bytes_accessed=0, transcendentals=0),
    )(*[in_vmem(ready) for ready in (held, first_round, pair_tile)])
    second_round = exchange(second_part, 2, 1)
    panel_rows, picks, kept_targets = pl.pallas_call(
        functools.partial(prepare_kernel, (1 + depth) * columns),
        out_shape=(
            pltpu.VMEM((slab, 2 * leaf_rows), jnp.bfloat16),
            pltpu.VMEM((2 * depth, size, size), jnp.bfloat16),
            pltpu.SMEM(targets.shape, jnp.int32),
        ),
        in_specs=[whole(SMEM), whole(SMEM), whole(VMEM), whole(VMEM)],
        out_specs=(whole(VMEM),) * 2 + (whole(SMEM),),
        cost_estimate=pl.CostEstimate(flops=0, bytes_accessed=0, transcendentals=0),
    )(leaf_live, targets, panel, in_vmem(first_tile))

    pair_first = xor_permute(first_tile, "rhs", 1)
    held, sent = pl.pallas_call(
        functools.partial(join_second_kernel, (1 + depth) * columns),
        out_shape=(
            pltpu.VMEM((4 * slab, 2 * size), jnp.bfloat16),
            pltpu.VMEM((6 * slab, size), jnp.bfloat16),
        ),
        in_specs=[whole(VMEM)] * 5,
        out_specs=(whole(VMEM),) * 2,
        cost_estimate=pl.CostEstimate(flops=0, bytes_accessed=0, transcendentals=0),
    )(*[in_vmem(ready) for ready in (held, first_round, pair_first, second_round, picks)])
    far = exchange(sent, 4, 0)

    kept_targets = pltpu.with_memory_space_constraint(kept_targets, SMEM)
    update, partial_x, lower, kept_near = pl.pallas_call(
        near_kernel,
        out_shape=(
            pltpu.VMEM((columns, size), jnp.float32),
            pltpu.VMEM((depth - 1, columns, size), jnp.float32),
            pltpu.VMEM((depth - 1, size, size), jnp.bfloat16),
            pltpu.VMEM((size // 2, 2 * size), jnp.bfloat16),
        ),
        in_specs=[whole(SMEM)] + [whole(VMEM)] * 2,
        out_specs=(whole(VMEM),) * 4,
        scratch_shapes=[pltpu.VMEM((size, 2 * size), jnp.bfloat16)],
        cost_estimate=pl.CostEstimate(flops=0, bytes_accessed=0, transcendentals=0),
    )(kept_targets, *[in_vmem(ready) for ready in (held, picks)])
    own_part = pl.pallas_call(
        functools.partial(leaf_kernel, 0),
        out_shape=pltpu.VMEM((2, columns, leaf_rows), jnp.float32),
        in_specs=[whole(VMEM)] * 3,
        out_specs=whole(VMEM),
        cost_estimate=pl.CostEstimate(flops=0, bytes_accessed=0, transcendentals=0),
    )(*[in_vmem(ready) for ready in (leaf_z, leaf_inv, update)])
    partial, pair_far = pl.pallas_call(
        functools.partial(far_kernel, 3),
        out_shape=(pltpu.VMEM((2, columns, leaf_rows), jnp.float32),) * 2,
        in_specs=[whole(VMEM)] * 4,
        out_specs=(whole(VMEM),) * 2,
        cost_estimate=pl.CostEstimate(flops=0, bytes_accessed=0, transcendentals=0),
    )(
        *[
            in_vmem(ready)
            for ready in (leaf_z, xor_permute(leaf_z, "rhs", 1), xor_permute(leaf_inv, "rhs", 3), own_part)
        ]
    )
    known, back, known_leaf, operator = pl.pallas_call(
        operator_kernel,
        out_shape=(
            pltpu.VMEM((size, size), jnp.float32),
            pltpu.VMEM((depth - 1, size, size), jnp.bfloat16),
            pltpu.VMEM((columns, 2 * leaf_rows), jnp.float32),
            pltpu.VMEM((size, 2 * leaf_rows), jnp.bfloat16),
        ),
        in_specs=[whole(VMEM)] * 4,
        out_specs=(whole(VMEM),) * 4,
        cost_estimate=pl.CostEstimate(flops=0, bytes_accessed=0, transcendentals=0),
    )(*[in_vmem(ready) for ready in (partial_x, lower, panel_rows, partial)])
    parent_x, top_x = pl.pallas_call(
        top_kernel,
        out_shape=(
            pltpu.VMEM((columns, size), jnp.bfloat16),
            pltpu.VMEM((size, columns), jnp.float32),
        ),
        in_specs=[whole(SMEM)] + [whole(VMEM)] * 6,
        out_specs=(whole(VMEM),) * 2,
        scratch_shapes=[
            pltpu.VMEM((size, size), jnp.bfloat16),
            pltpu.VMEM((size, 2 * size), jnp.bfloat16),
        ],
        cost_estimate=pl.CostEstimate(flops=3 * 10**9, bytes_accessed=0, transcendentals=0),
    )(kept_targets, *[in_vmem(ready) for ready in (kept_near, far, picks, update, partial, known_leaf)])
    pair_parts = (xor_permute(pair_far, "rhs", 1), xor_permute(leaf_inv, "rhs", 1))
    leaf_x, sep_x = pl.pallas_call(
        functools.partial(finish_kernel, (1,)),
        out_shape=(
            jax.ShapeDtypeStruct((2, columns, leaf_rows), jnp.float32),
            jax.ShapeDtypeStruct((2, depth, width, columns), jnp.float32),
        ),
        in_specs=[whole(SMEM)] * 2 + [whole(VMEM)] * 10,
        out_specs=(whole(pl.ANY),) * 2,
        scratch_shapes=[
            pltpu.VMEM((2, columns, leaf_rows), jnp.float32),
            pltpu.VMEM((2, depth, width, columns), jnp.float32),
            pltpu.SemaphoreType.DMA((3,)),
        ],
    )(
        leaf_live,
        kept_targets,
        *[
            in_vmem(ready)
            for ready in (leaf_z, partial, parent_x, top_x, known, back, known_leaf, operator) + pair_parts
        ],
    )
    return leaf_x, sep_x.transpose(0, 3, 1, 2)


def solution(mesh):
    placed = (
        P(None, "rhs", "leaf"),
        P(None, "rhs", None, "leaf"),
        P(None, "rhs", "leaf"),
        P(None, None, "leaf"),
        P(None, None, "leaf"),
        P(None, None, "leaf"),
        P("leaf"),
        P(),
    )
    return jax.shard_map(
        body,
        mesh=mesh,
        in_specs=placed,
        out_specs=(P(None, "rhs", "leaf"), P(None, "rhs", None, "leaf")),
        check_vma=False,
    )
```

```python
import functools

import jax
import jax.numpy as jnp
from jax import lax
from jax.experimental import pallas as pl
from jax.experimental.pallas import tpu as pltpu
from jax.sharding import PartitionSpec as P

exact_mode = lax.Precision.HIGHEST
VMEM = pltpu.MemorySpace.VMEM
SMEM = pltpu.MemorySpace.SMEM


def complex_dot(operand, factor):
    row_count = operand.shape[1]
    stacked = jnp.concatenate([operand[0], operand[1]], axis=0)
    real_acc = jnp.dot(stacked, factor[0], preferred_element_type=jnp.float32)
    imag_acc = jnp.dot(stacked, factor[1], preferred_element_type=jnp.float32)
    return jnp.stack(
        [real_acc[:row_count] - imag_acc[row_count:], imag_acc[:row_count] + real_acc[row_count:]]
    )


def complex_dot_back(operand, factor):
    row_count = operand.shape[1]
    stacked = jnp.concatenate([operand[0], operand[1]], axis=0)
    contract = (((1,), (1,)), ((), ()))
    real_acc = lax.dot_general(stacked, factor[0], contract, preferred_element_type=jnp.float32)
    imag_acc = lax.dot_general(stacked, factor[1], contract, preferred_element_type=jnp.float32)
    return jnp.stack(
        [real_acc[:row_count] - imag_acc[row_count:], imag_acc[:row_count] + real_acc[row_count:]]
    )


def to_blocks(values_in, group_size):
    return (
        values_in.reshape(2, values_in.shape[1], group_size, -1)
        .transpose(2, 0, 1, 3)
        .reshape(group_size, -1)
    )


def from_blocks(blocks, columns):
    group_size = blocks.shape[0]
    return blocks.reshape(group_size, 2, columns, -1).transpose(1, 2, 0, 3).reshape(2, columns, -1)


def selector(dest_index, total_slots):
    return (dest_index[:, None] == jnp.arange(total_slots, dtype=jnp.int32)[None, :]).astype(
        jnp.float32
    )


def exchange_sum(blocks, global_dest, devices):
    routed = jnp.dot(selector(global_dest, devices).T, blocks, precision=exact_mode)
    received = lax.all_to_all(
        routed.astype(jnp.bfloat16), "leaf", split_axis=0, concat_axis=0, tiled=True
    ).astype(routed.dtype)
    return jnp.sum(received, axis=0)


def collect(blocks, local_dest, level_bits, device, devices):
    group_start = device >> level_bits << level_bits
    return exchange_sum(blocks, group_start + local_dest, devices)


def spread(own_block, level_bits, device, devices):
    group_size = 2**level_bits
    group_start = device >> level_bits << level_bits
    slot_index = jnp.arange(devices, dtype=jnp.int32)[:, None]
    inside = (slot_index >= group_start) & (slot_index < group_start + group_size)
    routed = jnp.where(inside, own_block[None, :], jnp.zeros_like(own_block)[None, :])
    received = lax.all_to_all(routed, "leaf", split_axis=0, concat_axis=0, tiled=True)
    return lax.dynamic_slice_in_dim(received, group_start, group_size, 0)


def level_by_level(leaf_rhs, sep_rhs, leaf_w, leaf_low, sep_inv, sep_low, leaf_live, targets):
    devices = lax.axis_size("leaf")
    tree_depth = devices.bit_length() - 1
    device = lax.axis_index("leaf")
    leaf_rows = leaf_low.shape[1]
    sep_width = sep_inv.shape[1]
    columns = leaf_rhs.shape[1]
    live_mask = (jnp.arange(leaf_rows) < leaf_live[0] * 128).astype(jnp.float32)
    leaf_z = (leaf_rhs * live_mask).astype(jnp.bfloat16)
    first_dest = lax.dynamic_slice_in_dim(targets[0], device, 1)
    arriving = collect(complex_dot(leaf_z, leaf_low).reshape(1, -1), first_dest, 1, device, devices)
    solved_w = []
    for level_now in range(1, tree_depth + 1):
        group_size = 2**level_now
        offset = sep_width * (group_size - 2)
        level_z = (
            sep_rhs[:, :, level_now - 1, :] - arriving.reshape(2, columns, sep_width)
        ).astype(jnp.bfloat16)
        inv_rows = sep_inv[:, :, offset : offset + sep_width * group_size]
        own_w = collect(
            to_blocks(complex_dot(level_z, inv_rows), group_size),
            jnp.arange(group_size, dtype=jnp.int32),
            level_now,
            device,
            devices,
        )
        solved_w.append(own_w.reshape(2, columns, sep_width))
        if level_now < tree_depth:
            low_rows = sep_low[:, :, offset : offset + sep_width * group_size]
            group_start = device >> level_now << level_now
            dest_index = lax.dynamic_slice_in_dim(targets[level_now], group_start, group_size)
            arriving = collect(
                to_blocks(complex_dot(level_z, low_rows), group_size),
                dest_index,
                level_now + 1,
                device,
                devices,
            )
    solved_x = [solved_w[level_now] for level_now in range(tree_depth)]
    for level_now in range(tree_depth - 1, 0, -1):
        group_size = 2**level_now
        offset = sep_width * (group_size - 2)
        low_rows = sep_low[:, :, offset : offset + sep_width * group_size]
        parent_x = spread(
            solved_x[level_now].astype(jnp.bfloat16).reshape(-1), level_now + 1, device, devices
        )
        group_start = device >> level_now << level_now
        dest_index = lax.dynamic_slice_in_dim(targets[level_now], group_start, group_size)
        picked = jnp.dot(
            selector(dest_index, 2 * group_size).astype(jnp.bfloat16),
            parent_x,
            preferred_element_type=jnp.float32,
        ).astype(jnp.bfloat16)
        solved_x[level_now - 1] = solved_w[level_now - 1] - complex_dot_back(
            from_blocks(picked, columns), low_rows
        )
    parent_x = spread(solved_x[0].astype(jnp.bfloat16).reshape(-1), 1, device, devices)
    picked = jnp.dot(
        selector(first_dest, 2).astype(jnp.bfloat16), parent_x, preferred_element_type=jnp.float32
    ).astype(jnp.bfloat16)
    leaf_x = (
        leaf_w - complex_dot_back(picked.reshape(2, columns, sep_width), leaf_low)
    ) * live_mask
    return leaf_x, jnp.stack(solved_x, axis=2)


def xor_permute(values_in, axis, offset):
    count = lax.axis_size(axis)
    return lax.ppermute(values_in, axis, [(source, source ^ offset) for source in range(count)])


def in_vmem(values_in):
    return pltpu.with_memory_space_constraint(values_in, VMEM)


def masked_rows(leaf_rhs, live_ref):
    rows = leaf_rhs.shape[2]
    live = lax.broadcasted_iota(jnp.int32, (1, rows), 1) < live_ref[0] * 128
    stacked = jnp.concatenate([leaf_rhs[0], leaf_rhs[1]], axis=0)
    return jnp.where(live, stacked, 0.0).astype(jnp.bfloat16), live


def first_kernel(out_ref):
    out_ref[...] = jnp.zeros_like(out_ref)


def pack_kernel(live_ref, _, leaf_rhs_ref, low_ref, rhs_ref, inv_ref, sep_low_ref, out_ref, tile_ref, send_ref, z_ref):
    columns = leaf_rhs_ref.shape[1]
    depth = rhs_ref.shape[1]
    leaf_z, _ = masked_rows(leaf_rhs_ref[...], live_ref)
    z_ref[...] = leaf_z
    panel = jnp.concatenate([low_ref[0], low_ref[1]], axis=0)
    product = lax.dot_general(
        panel, leaf_z, (((1,), (1,)), ((), ())), preferred_element_type=jnp.float32
    )
    width = low_ref.shape[1]
    update = [
        product[:width, :columns] - product[width:, columns:],
        product[width:, :columns] + product[:width, columns:],
    ]
    used = (1 + depth) * columns + sep_low_ref.shape[2]
    halves, turned = [], []
    for part in range(2):
        pieces = [update[part]] + [rhs_ref[part, level] for level in range(depth)]
        pieces.append(sep_low_ref[part].astype(jnp.float32))
        if used < 128:
            pieces.append(jnp.zeros((width, 128 - used), jnp.float32))
        inverse = inv_ref[part].astype(jnp.float32)
        below = width * (2**depth - 2)
        gap = jnp.zeros((width, 128 - inverse.shape[1]), jnp.float32)
        pieces += [inverse[:, below:], inverse[:, :below], gap]
        turned.append(jnp.concatenate([inverse[:, :below], gap, inverse[:, below:]], axis=1))
        halves.append(jnp.concatenate(pieces, axis=1))
    packed = jnp.concatenate(halves, axis=0).astype(jnp.bfloat16)
    out_ref[...] = packed
    tile_ref[...] = packed[:, : tile_ref.shape[1]]
    send_ref[:, : tile_ref.shape[1]] = packed[:, : tile_ref.shape[1]]
    send_ref[:, tile_ref.shape[1] :] = jnp.concatenate(turned, axis=0).astype(jnp.bfloat16)


def piece_product(step, z_ref, piece_ref):
    columns = z_ref.shape[0] // 2
    depth = piece_ref.shape[1]
    owner = lax.axis_index("rhs") ^ step
    rows = z_ref[:, pl.ds(pl.multiple_of(owner * depth, 128), depth)]
    real_acc = jnp.dot(rows, piece_ref[0], preferred_element_type=jnp.float32)
    imag_acc = jnp.dot(rows, piece_ref[1], preferred_element_type=jnp.float32)
    return real_acc[:columns] - imag_acc[columns:], imag_acc[:columns] + real_acc[columns:]


def leaf_kernel(step, z_ref, piece_ref, _, out_ref):
    product = piece_product(step, z_ref, piece_ref)
    for part in range(2):
        out_ref[part] = product[part]


def prepare_kernel(low_start, live_ref, targets_ref, low_ref, _, panel_ref, pick_ref, kept_ref):
    for level in range(targets_ref.shape[0]):
        for block in range(targets_ref.shape[1]):
            kept_ref[level, block] = targets_ref[level, block]
    depth, devices = targets_ref.shape
    width, leaf_rows = low_ref.shape[1:]
    slab = 2 * width
    device = lax.axis_index("leaf")
    live = lax.broadcasted_iota(jnp.int32, (1, leaf_rows), 1) < live_ref[0] * 128
    low = [jnp.where(live, low_ref[part].astype(jnp.float32), 0.0) for part in range(2)]
    rows = jnp.concatenate(
        [
            jnp.concatenate([low[0], low[1]], axis=1),
            jnp.concatenate([low[1], -low[0]], axis=1),
        ],
        axis=0,
    ).astype(jnp.bfloat16)
    panel_ref[...] = jnp.zeros_like(panel_ref)
    panel_ref[pl.ds(pl.multiple_of(device * slab, slab), slab), :] = rows
    size = devices * slab
    row = lax.broadcasted_iota(jnp.int32, (size, size), 0)
    lane_row = lax.broadcasted_iota(jnp.int32, (1, size), 1)
    for level in range(1, depth + 1):
        offset = width * (2**level - 2) + lane_row % width
        inverse_offset = lane_row % width if level == depth else offset + width * devices
        target_lane = jnp.zeros((1, size), jnp.int32)
        for block in range(devices):
            target_lane = jnp.where(lane_row // slab == block, targets_ref[level - 1, block], target_lane)
        pick_ref[level - 1] = jnp.where(row == inverse_offset + target_lane * width, 1.0, 0.0).astype(
            jnp.bfloat16
        )
        if level == depth:
            pick_ref[2 * depth - 1] = jnp.where(
                row == size // 2 + inverse_offset + target_lane * width, 1.0, 0.0
            ).astype(jnp.bfloat16)
        if level < depth:
            own_lane = (lane_row // slab) % 2**level
            pick_ref[depth + level - 1] = jnp.where(
                row == low_start + offset + own_lane * width, 1.0, 0.0
            ).astype(jnp.bfloat16)


def join_first_kernel(own_ref, received_ref, pair_ref, out_ref, tile_ref):
    rows, lanes = own_ref.shape
    tile = pair_ref.shape[1]
    out_ref[:rows, :lanes] = own_ref[...]
    out_ref[rows:, :lanes] = received_ref[...]
    out_ref[:rows, lanes:] = pair_ref[...]
    out_ref[rows:, lanes:] = pair_ref[...]
    tile_ref[...] = received_ref[:, :tile]


def join_second_kernel(side_lanes, own_ref, first_ref, pair_ref, second_ref, _, out_ref, send_ref):
    rows, lanes = own_ref.shape
    tile = pair_ref.shape[1]
    out_ref[:rows, :] = own_ref[...]
    out_ref[rows : 2 * rows, :tile] = pair_ref[...]
    out_ref[rows : 2 * rows, tile:] = first_ref[:, tile:]
    lane = lax.broadcasted_iota(jnp.int32, (rows, tile), 1)
    merged = jnp.where(
        lane < side_lanes,
        second_ref[:rows, lanes:].astype(jnp.float32),
        second_ref[:rows, :tile].astype(jnp.float32),
    )
    out_ref[2 * rows : 3 * rows, :tile] = merged.astype(jnp.bfloat16)
    out_ref[2 * rows : 3 * rows, tile:] = second_ref[:rows, tile:lanes]
    out_ref[3 * rows :, :] = second_ref[rows:, :lanes]
    half = tile // 2
    send_ref[:rows, :] = own_ref[:, :tile]
    send_ref[rows : 2 * rows, :] = pair_ref[...]
    send_ref[2 * rows : 3 * rows, :] = merged.astype(jnp.bfloat16)
    send_ref[3 * rows : 4 * rows, :] = second_ref[rows:, :tile]
    send_ref[4 * rows : 5 * rows, :half] = own_ref[:, tile : tile + half]
    send_ref[4 * rows : 5 * rows, half:] = first_ref[:, tile + half :]
    send_ref[5 * rows :, :half] = second_ref[:rows, tile : tile + half]
    send_ref[5 * rows :, half:] = second_ref[rows:, tile + half : 2 * tile]


def far_kernel(step, z_ref, pair_z_ref, piece_ref, own_ref, out_ref, pair_out_ref):
    own_product, pair_product = [
        piece_product(step, source_ref, piece_ref) for source_ref in (z_ref, pair_z_ref)
    ]
    for part in range(2):
        out_ref[part] = own_ref[part] + own_product[part]
        pair_out_ref[part] = pair_product[part].astype(jnp.bfloat16)


def owner(targets_ref, level, block):
    if level == 0:
        return jnp.int32(block)
    group = 2**level
    return block // group * group + targets_ref[level - 1, block]


def rows_of(targets_ref, level, source_ref, slab):
    device = lax.axis_index("leaf")
    return jnp.concatenate(
        [
            source_ref[
                pl.ds(pl.multiple_of((owner(targets_ref, level, block) ^ device) * slab, slab), slab), :
            ]
            for block in range(targets_ref.shape[1])
        ],
        axis=0,
    )


def side_of(raw, level, columns):
    size = raw.shape[0]
    row = lax.broadcasted_iota(jnp.int32, (columns, size), 0)
    lane = lax.broadcasted_iota(jnp.int32, (columns, size), 1)
    pick = jnp.where(lane == row + level * columns, 1.0, 0.0).astype(jnp.bfloat16)
    return times_transposed(pick, raw[:, :size])


def times_transposed(left, right):
    return lax.dot_general(left, right, (((1,), (1,)), ((), ())), preferred_element_type=jnp.float32)


def front_matrix(source, pick, level, slab):
    return front_of(jnp.dot(source, pick, preferred_element_type=jnp.float32), level, slab)


def front_of(plain, level, slab):
    size, width = plain.shape[0], slab // 2
    row = lax.broadcasted_iota(jnp.int32, (size, size), 0)
    lane = lax.broadcasted_iota(jnp.int32, (size, size), 1)
    swapped = plain.reshape(size // slab, 2, width, size)
    swapped = jnp.concatenate([swapped[:, 1:], swapped[:, :1]], axis=1).reshape(size, size)
    signed = jnp.where((row // width) % 2 == 0, plain, -plain)
    full = jnp.where((lane // width) % 2 == 0, signed, swapped)
    inside = row // (slab * 2**level) == lane // (slab * 2**level)
    return jnp.where(inside, full, 0.0).astype(jnp.bfloat16)


def conjugate(values_in, width):
    lane = lax.broadcasted_iota(jnp.int32, (1, values_in.shape[1]), 1)
    return jnp.where((lane // width) % 2 == 0, values_in, -values_in)


def near_kernel(targets_ref, near_ref, pick_ref, update_ref, partial_ref, lower_ref, kept_ref, all_ref):
    depth, devices = targets_ref.shape
    columns, size = update_ref.shape
    slab = size // devices
    half = size // 2
    for place_ref in (kept_ref, all_ref):
        place_ref[:half, :] = near_ref[...]
        for slot in range(1, devices // 2, 2):
            rows = slice(slot * slab, (slot + 1) * slab)
            turned = pltpu.roll(near_ref[rows, size:].astype(jnp.float32), half, 1)
            place_ref[rows, size:] = turned.astype(jnp.bfloat16)
    all_ref[half:, :] = jnp.zeros_like(near_ref)
    arriving = side_of(rows_of(targets_ref, 0, all_ref, slab), 0, columns)
    for level in range(1, depth):
        raw = rows_of(targets_ref, level, all_ref, slab)
        level_z = (side_of(raw, level, columns) - arriving).astype(jnp.bfloat16)
        inverse = front_matrix(raw[:, size:], pick_ref[level - 1], level, slab)
        lower = front_matrix(raw[:, :size], pick_ref[depth + level - 1], level, slab)
        lower_ref[level - 1] = lower
        partial_ref[level - 1] = jnp.dot(level_z, inverse, preferred_element_type=jnp.float32)
        arriving = jnp.dot(level_z, lower, preferred_element_type=jnp.float32)
    update_ref[...] = arriving


def operator_kernel(partial_ref, lower_ref, panel_ref, _, solved_ref, back_ref, leaf_ref, operator_ref):
    top, columns, size = partial_ref.shape
    width = size // 16
    known, operator = partial_ref[top - 1], lower_ref[top - 1]
    solved = {top: known}
    back_ref[top - 1] = operator
    for level in range(top - 1, 0, -1):
        parent = conjugate(known, width).astype(jnp.bfloat16)
        known = partial_ref[level - 1] - conjugate(times_transposed(parent, lower_ref[level - 1]), width)
        operator = -jnp.dot(lower_ref[level - 1], operator, preferred_element_type=jnp.float32)
        operator = operator.astype(jnp.bfloat16)
        solved[level] = known
        back_ref[level - 1] = operator
    stacked = [solved[level] for level in range(1, top + 1)]
    stacked.append(jnp.zeros((size - top * columns, size), jnp.float32))
    solved_ref[...] = jnp.concatenate(stacked, axis=0).T
    parent = conjugate(known, width).astype(jnp.bfloat16)
    leaf_ref[...] = jnp.dot(parent, panel_ref[...], preferred_element_type=jnp.float32)
    operator_ref[...] = lax.dot_general(
        operator, panel_ref[...], (((0,), (0,)), ((), ())), preferred_element_type=jnp.float32
    ).astype(jnp.bfloat16)


def top_kernel(
    targets_ref, near_ref, far_ref, pick_ref, update_ref, _, __, parent_ref, solved_ref, half_ref, all_ref
):
    depth, devices = targets_ref.shape
    columns, size = update_ref.shape
    slab = size // devices
    half = size // 2
    half_ref[:half, :] = jnp.zeros((half, size), jnp.bfloat16)
    half_ref[half:, :] = far_ref[:half]
    all_ref[:half, :] = near_ref[...]
    all_ref[half:, :size] = far_ref[:half]
    for slot in range(devices // 2):
        rows = slice(half + slot // 2 * slab, half + (slot // 2 + 1) * slab)
        all_ref[half + slot * slab : half + (slot + 1) * slab, size:] = far_ref[rows]
    raw = rows_of(targets_ref, depth, all_ref, slab)
    row_block = lax.broadcasted_iota(jnp.int32, (size, size), 0) // slab
    upper = jnp.zeros((size, size), jnp.int32)
    for block in range(devices):
        slot = owner(targets_ref, depth, block) ^ lax.axis_index("leaf")
        upper = jnp.where(row_block == block, slot, upper)
    plain = jnp.where(
        (upper >= devices // 2) & (upper % 2 == 1),
        jnp.dot(raw[:, size:], pick_ref[2 * depth - 1], preferred_element_type=jnp.float32),
        jnp.dot(raw[:, size:], pick_ref[depth - 1], preferred_element_type=jnp.float32),
    )
    inverse = front_of(plain, depth, slab)
    waiting = side_of(raw, depth, columns) - update_ref[...]
    arriving = side_of(rows_of(targets_ref, 0, half_ref, slab), 0, columns)
    for level in range(1, depth):
        raw = rows_of(targets_ref, level, half_ref, slab)
        level_z = (side_of(raw, level, columns) - arriving).astype(jnp.bfloat16)
        lower = front_matrix(raw, pick_ref[depth + level - 1], level, slab)
        arriving = jnp.dot(level_z, lower, preferred_element_type=jnp.float32)
    level_z = (waiting - arriving).astype(jnp.bfloat16)
    solved = jnp.dot(level_z, inverse, preferred_element_type=jnp.float32)
    solved_ref[...] = lax.dot_general(
        inverse, level_z, (((0,), (1,)), ((), ())), preferred_element_type=jnp.float32
    )
    parent_ref[...] = conjugate(solved, slab // 2).astype(jnp.bfloat16)


def finish_kernel(
    steps,
    live_ref,
    targets_ref,
    z_ref,
    partial_ref,
    parent_ref,
    top_ref,
    solved_ref,
    lower_ref,
    leaf_ref,
    operator_ref,
    far_ref,
    *refs,
):
    piece_refs, (leaf_out_ref, sep_out_ref) = refs[: len(steps)], refs[len(steps) : len(steps) + 2]
    leaf_place, sep_place, sems = refs[len(steps) + 2 :]
    depth, devices = targets_ref.shape
    columns, size = parent_ref.shape
    leaf_rows = leaf_place.shape[2]
    slab = size // devices
    width = slab // 2
    device = lax.axis_index("leaf")
    live = lax.broadcasted_iota(jnp.int32, (1, leaf_rows), 1) < live_ref[0] * 128
    parent = parent_ref[...]
    for level in range(1, depth + 1):
        place = jnp.int32(0)
        for block in range(devices):
            place = jnp.where(owner(targets_ref, level, block) == device, block, place)
        rows = pl.ds(pl.multiple_of(place * slab, slab), slab)
        if level < depth:
            known = solved_ref[rows, :][:, (level - 1) * columns : level * columns]
            change = times_transposed(lower_ref[level - 1, rows, :], parent)
            halves = known[:width] - change[:width], known[width:] + change[width:]
        else:
            solved = top_ref[rows, :]
            halves = solved[:width], solved[width:]
        for part in range(2):
            sep_place[part, level - 1] = halves[part]
    from_tree = leaf_ref[...] - jnp.dot(parent, operator_ref[...], preferred_element_type=jnp.float32)
    products = [piece_product(step, z_ref, piece_ref) for step, piece_ref in zip(steps, piece_refs)]
    copies = []
    for part in range(2):
        leaf_w = partial_ref[part] + far_ref[part].astype(jnp.float32) + sum(product[part] for product in products)
        leaf_place[part] = (
            jnp.where(live, leaf_w, 0.0) - from_tree[:, part * leaf_rows : (part + 1) * leaf_rows]
        )
        copies.append(pltpu.make_async_copy(leaf_place.at[part], leaf_out_ref.at[part], sems.at[part]))
        copies[-1].start()
    copies.append(pltpu.make_async_copy(sep_place, sep_out_ref, sems.at[2]))
    copies[-1].start()
    for copy in copies:
        copy.wait()


def whole(space):
    return pl.BlockSpec(memory_space=space)


def body(leaf_rhs, sep_rhs, leaf_inv, leaf_low, sep_inv, sep_low, leaf_live, targets):
    devices, parts = lax.axis_size("leaf"), lax.axis_size("rhs")
    columns, leaf_rows = leaf_rhs.shape[1:]
    width, depth = sep_inv.shape[1], sep_rhs.shape[2]
    slab = 2 * width
    size = devices * slab
    small_tree = (
        devices == 8 and parts % 2 == 0 and size == 128 and (1 + depth) * columns + sep_low.shape[2] <= 128 and sep_inv.shape[2] <= 128
    )
    panel = leaf_low.transpose(0, 2, 1)
    tree_rhs = sep_rhs.transpose(0, 2, 3, 1)

    if not small_tree:
        live_mask = (jnp.arange(leaf_rows) < leaf_live[0] * 128).astype(jnp.float32)
        leaf_z = (leaf_rhs * live_mask).astype(jnp.bfloat16)
        leaf_w = complex_dot(leaf_z, lax.all_gather(leaf_inv, "rhs", axis=1, tiled=True)) * live_mask
        return level_by_level(leaf_rhs, sep_rhs, leaf_w, leaf_low, sep_inv, sep_low, leaf_live, targets)

    tree_parts = (leaf_rhs, panel, tree_rhs, sep_inv, sep_low)
    first = pl.pallas_call(
        first_kernel,
        out_shape=pltpu.VMEM((8, 128), jnp.float32),
        out_specs=whole(VMEM),
        cost_estimate=pl.CostEstimate(flops=10**9, bytes_accessed=0, transcendentals=0),
    )()
    held, own_tile, sent, leaf_z = pl.pallas_call(
        pack_kernel,
        out_shape=(
            pltpu.VMEM((slab, 2 * size), jnp.bfloat16),
            pltpu.VMEM((slab, size), jnp.bfloat16),
            pltpu.VMEM((slab, 2 * size), jnp.bfloat16),
            pltpu.VMEM((2 * columns, leaf_rows), jnp.bfloat16),
        ),
        in_specs=[whole(SMEM)] + [whole(VMEM)] * 6,
        out_specs=(whole(VMEM),) * 4,
    )(leaf_live, *[in_vmem(part) for part in (first,) + tree_parts])

    def exchange(values_in, offset, flip):
        partners = [
            (source * parts + part, (source ^ offset) * parts + (part ^ flip))
            for source in range(devices)
            for part in range(parts)
        ]
        return lax.ppermute(values_in, ("leaf", "rhs"), partners)

    first_round = exchange(sent, 1, 1)
    pair_tile = xor_permute(own_tile, "rhs", 1)
    second_part, first_tile = pl.pallas_call(
        join_first_kernel,
        out_shape=(
            pltpu.VMEM((2 * slab, 3 * size), jnp.bfloat16),
            pltpu.VMEM((slab, size), jnp.bfloat16),
        ),
        in_specs=[whole(VMEM)] * 3,
        out_specs=(whole(VMEM),) * 2,
        cost_estimate=pl.CostEstimate(flops=10**11, bytes_accessed=0, transcendentals=0),
    )(*[in_vmem(ready) for ready in (held, first_round, pair_tile)])
    second_round = exchange(second_part, 2, 1)
    panel_rows, picks, kept_targets = pl.pallas_call(
        functools.partial(prepare_kernel, (1 + depth) * columns),
        out_shape=(
            pltpu.VMEM((size, 2 * leaf_rows), jnp.bfloat16),
            pltpu.VMEM((2 * depth, size, size), jnp.bfloat16),
            pltpu.SMEM(targets.shape, jnp.int32),
        ),
        in_specs=[whole(SMEM), whole(SMEM), whole(VMEM), whole(VMEM)],
        out_specs=(whole(VMEM),) * 2 + (whole(SMEM),),
        cost_estimate=pl.CostEstimate(flops=0, bytes_accessed=0, transcendentals=0),
    )(leaf_live, targets, panel, in_vmem(first_tile))

    pair_first = xor_permute(first_tile, "rhs", 1)
    held, sent = pl.pallas_call(
        functools.partial(join_second_kernel, (1 + depth) * columns),
        out_shape=(
            pltpu.VMEM((4 * slab, 2 * size), jnp.bfloat16),
            pltpu.VMEM((6 * slab, size), jnp.bfloat16),
        ),
        in_specs=[whole(VMEM)] * 5,
        out_specs=(whole(VMEM),) * 2,
        cost_estimate=pl.CostEstimate(flops=0, bytes_accessed=0, transcendentals=0),
    )(*[in_vmem(ready) for ready in (held, first_round, pair_first, second_round, picks)])
    far = exchange(sent, 4, 0)

    kept_targets = pltpu.with_memory_space_constraint(kept_targets, SMEM)
    update, partial_x, lower, kept_near = pl.pallas_call(
        near_kernel,
        out_shape=(
            pltpu.VMEM((columns, size), jnp.float32),
            pltpu.VMEM((depth - 1, columns, size), jnp.float32),
            pltpu.VMEM((depth - 1, size, size), jnp.bfloat16),
            pltpu.VMEM((size // 2, 2 * size), jnp.bfloat16),
        ),
        in_specs=[whole(SMEM)] + [whole(VMEM)] * 2,
        out_specs=(whole(VMEM),) * 4,
        scratch_shapes=[pltpu.VMEM((size, 2 * size), jnp.bfloat16)],
        cost_estimate=pl.CostEstimate(flops=0, bytes_accessed=0, transcendentals=0),
    )(kept_targets, *[in_vmem(ready) for ready in (held, picks)])
    own_part = pl.pallas_call(
        functools.partial(leaf_kernel, 0),
        out_shape=pltpu.VMEM((2, columns, leaf_rows), jnp.float32),
        in_specs=[whole(VMEM)] * 3,
        out_specs=whole(VMEM),
        cost_estimate=pl.CostEstimate(flops=0, bytes_accessed=0, transcendentals=0),
    )(*[in_vmem(ready) for ready in (leaf_z, leaf_inv, update)])
    partial, pair_far = pl.pallas_call(
        functools.partial(far_kernel, 3),
        out_shape=(
            pltpu.VMEM((2, columns, leaf_rows), jnp.float32),
            pltpu.VMEM((2, columns, leaf_rows), jnp.bfloat16),
        ),
        in_specs=[whole(VMEM)] * 4,
        out_specs=(whole(VMEM),) * 2,
        cost_estimate=pl.CostEstimate(flops=0, bytes_accessed=0, transcendentals=0),
    )(
        *[
            in_vmem(ready)
            for ready in (leaf_z, xor_permute(leaf_z, "rhs", 1), xor_permute(leaf_inv, "rhs", 3), own_part)
        ]
    )
    known, back, known_leaf, operator = pl.pallas_call(
        operator_kernel,
        out_shape=(
            pltpu.VMEM((size, size), jnp.float32),
            pltpu.VMEM((depth - 1, size, size), jnp.bfloat16),
            pltpu.VMEM((columns, 2 * leaf_rows), jnp.float32),
            pltpu.VMEM((size, 2 * leaf_rows), jnp.bfloat16),
        ),
        in_specs=[whole(VMEM)] * 4,
        out_specs=(whole(VMEM),) * 4,
        cost_estimate=pl.CostEstimate(flops=0, bytes_accessed=0, transcendentals=0),
    )(*[in_vmem(ready) for ready in (partial_x, lower, panel_rows, partial)])
    parent_x, top_x = pl.pallas_call(
        top_kernel,
        out_shape=(
            pltpu.VMEM((columns, size), jnp.bfloat16),
            pltpu.VMEM((size, columns), jnp.float32),
        ),
        in_specs=[whole(SMEM)] + [whole(VMEM)] * 6,
        out_specs=(whole(VMEM),) * 2,
        scratch_shapes=[
            pltpu.VMEM((size, size), jnp.bfloat16),
            pltpu.VMEM((size, 2 * size), jnp.bfloat16),
        ],
        cost_estimate=pl.CostEstimate(flops=3 * 10**9, bytes_accessed=0, transcendentals=0),
    )(kept_targets, *[in_vmem(ready) for ready in (kept_near, far, picks, update, partial, known_leaf)])
    pair_parts = (xor_permute(pair_far, "rhs", 1), xor_permute(leaf_inv, "rhs", 1))
    leaf_x, sep_x = pl.pallas_call(
        functools.partial(finish_kernel, (1,)),
        out_shape=(
            jax.ShapeDtypeStruct((2, columns, leaf_rows), jnp.float32),
            jax.ShapeDtypeStruct((2, depth, width, columns), jnp.float32),
        ),
        in_specs=[whole(SMEM)] * 2 + [whole(VMEM)] * 10,
        out_specs=(whole(pl.ANY),) * 2,
        scratch_shapes=[
            pltpu.VMEM((2, columns, leaf_rows), jnp.float32),
            pltpu.VMEM((2, depth, width, columns), jnp.float32),
            pltpu.SemaphoreType.DMA((3,)),
        ],
    )(
        leaf_live,
        kept_targets,
        *[
            in_vmem(ready)
            for ready in (leaf_z, partial, parent_x, top_x, known, back, known_leaf, operator) + pair_parts
        ],
    )
    return leaf_x, sep_x.transpose(0, 3, 1, 2)


def solution(mesh):
    placed = (
        P(None, "rhs", "leaf"),
        P(None, "rhs", None, "leaf"),
        P(None, "rhs", "leaf"),
        P(None, None, "leaf"),
        P(None, None, "leaf"),
        P(None, None, "leaf"),
        P("leaf"),
        P(),
    )
    return jax.shard_map(
        body,
        mesh=mesh,
        in_specs=placed,
        out_specs=(P(None, "rhs", "leaf"), P(None, "rhs", None, "leaf")),
        check_vma=False,
    )
```
